256 devices in a mesh: prod: 64 (over z, x, core), tile: 4 (over y).
Axes of the slice: x: 4, y: 4, z: 8, core: 2. Of those that a mesh axis runs over, the one named last changes fastest.
Arguments:
- embeddings: bfloat16 [65536, 4096], P('prod')
- cluster_ids: int32 [65536], P('prod'), may hold values from 0 to 511, as said below
Outputs:
- best_cosine: float32 [65536], P('prod')
The draws below stay inside these ranges and needn't reach their ends.
Inputs may be any that keep to these rules, and one draw needn't show every extreme that they name: `cluster_ids`: cluster c belongs to owner c // 8. On each index of prod at most 32 items belong to one owner, exactly 32 to one owner that is the same for all indices, and at least one to every owner.
All inputs are finite; a program needn't handle non-finite values.
Results may differ from the reference program's by a relative error of at most 0.00043.
Values may be sent and summed in bfloat16 or wider, within the bound.
A program may use at most 128 MiB of HBM per device.

```python
import math
import jax
import jax.numpy as jnp
from jax import lax

D = 4096
ITEM_DEV = 1024
CLU_OWN = 8
SEND = 32
ITEMS = 65536
CLUSTERS = 512
N_PROD = 64


sub_centres = 4


pair_groups = 8


def cluster_layout(key):
    key_owner, key_rank, key_shift, key_lone = jax.random.split(key, 4)
    key_lone_cluster, key_lone_device = jax.random.split(key_lone)
    busiest = jax.random.randint(key_owner, (), 0, N_PROD)
    shifts = jax.random.randint(key_shift, (N_PROD,), 0, CLU_OWN - 1)
    lone_cluster = jax.random.randint(key_lone_cluster, (N_PROD,), 0, CLU_OWN)
    lone_device = jax.random.randint(key_lone_device, (N_PROD,), 0, N_PROD)
    grid = N_PROD * SEND
    positions = jnp.arange(grid, dtype=jnp.int32)
    block_owner = positions // SEND
    leading = positions % SEND == 0

    def one_device(device_key, device):
        key_order, key_pick, key_shuffle = jax.random.split(device_key, 3)
        order = jax.random.permutation(key_order, grid).astype(jnp.int32)
        priority = order - jnp.where(block_owner == busiest, 3 * grid, 0) - jnp.where(leading, grid, 0)
        chosen = jnp.argsort(priority, stable=True)[:ITEM_DEV].astype(jnp.int32)
        chosen_owner = chosen // SEND
        owner_lone = lone_cluster[chosen_owner]
        owner_lone_device = lone_device[chosen_owner]
        drawn = jax.random.randint(key_pick, (ITEM_DEV,), 0, CLU_OWN - 1).astype(jnp.int32)
        random_local = drawn + (drawn >= owner_lone).astype(jnp.int32)
        rank = device - (device > owner_lone_device).astype(jnp.int32)
        other = (rank + shifts[chosen_owner]) % (CLU_OWN - 1)
        other_local = other + (other >= owner_lone).astype(jnp.int32)
        forced_local = jnp.where(owner_lone_device == device, owner_lone, other_local)
        local = jnp.where(chosen % SEND == 0, forced_local, random_local)
        member_ids = (chosen_owner * CLU_OWN + local).astype(jnp.int32)
        return member_ids[jax.random.permutation(key_shuffle, ITEM_DEV)]
    device_keys = jax.random.split(key_rank, N_PROD)
    devices = jnp.arange(N_PROD, dtype=jnp.int32)
    return jax.vmap(one_device)(device_keys, devices).reshape(ITEMS).astype(jnp.int32)


def draw_cluster_ids(key, part):
    return cluster_layout(key)


def draw_embeddings(key, part):
    member_ids = cluster_layout(key)
    key = jax.random.fold_in(key, 7)
    key_center = jax.random.fold_in(key, 0)
    key_noise = jax.random.fold_in(key, 1)
    key_mix = jax.random.fold_in(key, 2)
    key_scale = jax.random.fold_in(key, 3)
    key_extra = jax.random.fold_in(key, 5)
    key_kind = jax.random.fold_in(key, 6)
    key_sub, key_copy, key_seed, key_tight, key_weight = jax.random.split(key_kind, 5)
    centers = jax.random.normal(key_center, (CLUSTERS, D), jnp.float32)
    mixing = jax.random.uniform(key_mix, (ITEMS, 1), jnp.float32, 0.3, 2.0)
    sub_weight = jax.random.uniform(key_weight, (ITEMS, 1), jnp.float32, 0.5, 1.5)
    tightness = jnp.exp(jax.random.uniform(key_tight, (ITEMS, 1), jnp.float32, math.log(0.03), math.log(0.3)))
    sub_pick = jax.random.randint(key_sub, (ITEMS,), 0, sub_centres).astype(jnp.int32)
    seed_pick = jax.random.randint(key_seed, (ITEMS,), 0, pair_groups).astype(jnp.int32)
    copied = jax.random.randint(key_copy, (ITEMS,), 0, 10) < 3
    tags = jnp.where(copied, CLUSTERS * sub_centres + member_ids * pair_groups + seed_pick, member_ids * sub_centres + sub_pick).astype(jnp.int32)
    extra = jax.vmap(lambda tag: jax.random.normal(jax.random.fold_in(key_extra, tag), (D,), jnp.float32))(tags)
    noise = jax.random.normal(key_noise, (ITEMS, D), jnp.float32)
    scales = jnp.exp(jax.random.uniform(key_scale, (ITEMS, 1), jnp.float32, 0.0, 2.3))
    entries = mixing * centers[member_ids] + sub_weight * extra + noise
    planted = extra + tightness * noise
    values = scales * jnp.where(copied[:, None], planted, entries)
    return values.astype(jnp.bfloat16)


def setup_inputs(seed: int = 0) -> dict:
    keys = jax.random.split(jax.random.key(seed), 3)
    embeddings = draw_embeddings(jax.random.fold_in(keys[2], 71), 0)
    cluster_ids = draw_cluster_ids(jax.random.fold_in(keys[2], 71), 0)
    return dict(embeddings=embeddings, cluster_ids=cluster_ids)


def reference(embeddings, cluster_ids):
    widened = embeddings.astype(jnp.float32)
    normed = (widened * lax.rsqrt(lax.optimization_barrier(jnp.sum(widened * widened, axis=1, keepdims=True)) + 1e-06)).astype(jnp.bfloat16)
    owners = (cluster_ids // CLU_OWN).astype(jnp.int32)
    owner_hot = (owners.reshape(N_PROD, ITEM_DEV)[:, :, None] == jnp.arange(N_PROD, dtype=jnp.int32)[None, None, :]).astype(jnp.int32)
    running = jnp.cumsum(owner_hot, axis=1).astype(jnp.int32)
    slot_index = (lax.optimization_barrier(jnp.sum(running * owner_hot, axis=2)) - 1).reshape(ITEMS).astype(jnp.int32)
    source = (jnp.arange(ITEMS, dtype=jnp.int32) // ITEM_DEV).astype(jnp.int32)
    group_rows = N_PROD * SEND
    position = (owners * group_rows + source * SEND + slot_index).astype(jnp.int32)
    inverse = jnp.full((N_PROD * group_rows,), ITEMS, jnp.int32).at[position].set(jnp.arange(ITEMS, dtype=jnp.int32))
    padded = jnp.concatenate([normed, jnp.zeros((1, D), normed.dtype)], axis=0)
    labels = jnp.concatenate([cluster_ids, jnp.full((1,), -1, jnp.int32)], axis=0)
    identity = jnp.arange(group_rows, dtype=jnp.int32)

    def one_owner(members):
        block = padded[members]
        member_tags = labels[members]
        scores = jnp.dot(block, block.T, preferred_element_type=jnp.float32)
        in_cluster = (member_tags[:, None] == member_tags[None, :]) & (member_tags[:, None] >= 0) & (identity[:, None] != identity[None, :])
        return lax.optimization_barrier(jnp.max(jnp.where(in_cluster, scores, -1.0), axis=1))
    best = lax.map(one_owner, inverse.reshape(N_PROD, group_rows))
    return best.reshape(N_PROD * group_rows)[position]
```

```python
import functools

import jax
import jax.numpy as jnp
from jax import lax
from jax.experimental import pallas as pl
from jax.experimental.pallas import tpu as pltpu
from jax.sharding import PartitionSpec as P

CLU_OWN = 8
SLOTS = 32
Z_SLOTS = 176
BLOCK = 128
CAP = 3 * BLOCK
F32 = jnp.float32
BF16 = jnp.bfloat16
MESH = pl.DeviceIdType.MESH
NN = (((1,), (0,)), ((), ()))
NT = (((1,), (1,)), ((), ()))


def dot(a, b, dims=NN, precision=None):
    return lax.dot_general(a, b, dims, preferred_element_type=F32, precision=precision)


def iota(shape, dim):
    return lax.broadcasted_iota(jnp.int32, shape, dim)


def hot(cond):
    return jnp.where(cond, 1.0, 0.0).astype(BF16)


def pack_kernel(
    planes, owners_in, ids_ref, x_ref, packed_ref, lids_ref, index_ref, hist_ref, unit, counts
):
    step = pl.program_id(0)
    rows, width = x_ref.shape
    items = ids_ref.shape[1]
    part = unit.shape[1]
    tile = lax.axis_index("tile")

    total = jnp.zeros((rows, BLOCK), F32)
    for c in range(width // BLOCK):
        x = x_ref[:, c * BLOCK : (c + 1) * BLOCK].astype(F32)
        total += x * x
    scale = lax.rsqrt(jnp.sum(total, axis=1, keepdims=True) + 1e-06)
    mine = x_ref[:, pl.ds(pl.multiple_of(tile * part, part), part)].astype(F32)
    unit[pl.ds(pl.multiple_of(step * rows, rows), rows), :] = (mine * scale).astype(BF16)

    ids = ids_ref[...]
    owner = ids // CLU_OWN
    plane = owner // owners_in
    key = (owner * items + iota((1, items), 1)).astype(F32)
    plane_key = (plane * (owners_in * items)).astype(F32)
    owner_key = (owner * items).astype(F32)
    here = ids_ref[:, pl.ds(pl.multiple_of(step * rows, rows), rows)]
    here_key = ((here // CLU_OWN) * items + iota((1, rows), 1) + step * rows).astype(F32)
    column = jnp.broadcast_to(here_key, (BLOCK, rows)).T

    @pl.when(step == 0)
    def _():
        counts[...] = jnp.zeros_like(counts)

    for g in range(items // BLOCK):
        lanes = slice(g * BLOCK, (g + 1) * BLOCK)
        for n, bound in enumerate((key, plane_key, owner_key)):
            less = jnp.where(column < bound[:, lanes], 1.0, 0.0)
            counts[n : n + 1, lanes] += jnp.sum(less, axis=0, keepdims=True)

    @pl.when(step == pl.num_programs(0) - 1)
    def _():
        before = counts[0:1, :]
        position = (before - counts[1:2, :]).astype(jnp.int32)
        slot = (before - counts[2:3, :]).astype(jnp.int32)
        place = (owner % owners_in) * SLOTS + slot
        lid = ids % CLU_OWN
        for z in range(planes):
            pick = hot((iota((Z_SLOTS, items), 0) == position) & (plane == z))
            packed_ref[z] = dot(pick, unit[...]).astype(BF16)
        by_plane = jnp.where(iota((8, items), 0) == plane, lid + 1, 0).astype(F32).astype(BF16)
        by_place = hot(iota((owners_in * SLOTS, items), 0) == place)
        lids = dot(by_plane, by_place, NT)
        for z in range(planes):
            lids_ref[z] = jnp.broadcast_to(lids[z : z + 1], lids_ref.shape[1:])
        row = iota((8, items), 0)
        index_ref[...] = jnp.where(row == 0, plane, place)
        by_owner = hot(iota((planes * owners_in, items), 0) == owner)
        kind = iota((16, items), 0)
        by_lid = jnp.where(kind == lid, 1.0, 0.0) + jnp.where(
            (kind == CLU_OWN) & (position >= Z_SLOTS), 1024.0, 0.0
        )
        hist_ref[...] = dot(by_owner, by_lid.astype(BF16), NT)


def pack(planes, owners_in, embeddings, cluster_ids, part):
    items, width = embeddings.shape
    lanes = owners_in * SLOTS
    whole = lambda shape: pl.BlockSpec(shape, lambda i: (0,) * len(shape))
    shapes = (
        jax.ShapeDtypeStruct((planes, Z_SLOTS, part), BF16),
        jax.ShapeDtypeStruct((planes, 8, lanes), F32),
        jax.ShapeDtypeStruct((8, items), jnp.int32),
        jax.ShapeDtypeStruct((planes * owners_in, 16), F32),
    )
    return pl.pallas_call(
        functools.partial(pack_kernel, planes, owners_in),
        grid=(items // BLOCK,),
        in_specs=[whole((1, items)), pl.BlockSpec((BLOCK, width), lambda i: (i, 0))],
        out_specs=[whole(s.shape) for s in shapes],
        out_shape=shapes,
        scratch_shapes=[pltpu.VMEM((items, part), BF16), pltpu.VMEM((8, items), F32)],
        compiler_params=pltpu.CompilerParams(vmem_limit_bytes=40 * 1024 * 1024),
    )(cluster_ids.reshape(1, items), embeddings)


def nearest_first(n):
    order = [0]
    for d in range(1, n // 2 + 1):
        order += [d] if 2 * d == n else [d, n - d]
    return order


def route_kernel(
    planes,
    owners_in,
    packed_ref,
    lids_ref,
    index_ref,
    out_ref,
    z_rows,
    z_lids,
    lids_out,
    x_lids,
    staged,
    rows,
    sorted_rows,
    partial,
    relay,
    near,
    far,
    forward,
    found,
    values_out,
    x_back,
    values_home,
    z_back,
    own_sem,
    z_send,
    z_recv,
    zl_send,
    zl_recv,
    xl_send,
    xl_recv,
    x_send,
    x_recv,
    y_send,
    y_recv,
    f_send,
    f_recv,
    xb_send,
    xb_recv,
    zb_send,
    zb_recv,
):
    lanes = owners_in * SLOTS
    half = partial.shape[1] // 2
    me = lax.axis_index("prod")
    tile = lax.axis_index("tile")
    my_plane = me // owners_in
    my_col = lax.rem(me, owners_in)
    at_plane = lambda d: lax.rem(my_plane + d, planes)
    at_col = lambda k: lax.rem(my_col + k, owners_in)
    at_tile = lambda k: lax.rem(tile + k, 4)
    to_plane = lambda d: {"prod": at_plane(d) * owners_in + my_col}
    to_col = lambda k: {"prod": my_plane * owners_in + at_col(k)}
    to_tile = lambda k: {"tile": at_tile(k)}

    def send(src, dst, send_sem, recv_sem, device):
        return pltpu.make_async_remote_copy(
            src_ref=src,
            dst_ref=dst,
            send_sem=send_sem,
            recv_sem=recv_sem,
            device_id=device,
            device_id_type=MESH,
        )

    barrier = pltpu.get_barrier_semaphore()
    for d in range(1, planes):
        pl.semaphore_signal(barrier, inc=1, device_id=to_plane(d), device_id_type=MESH)
    for k in range(1, owners_in):
        pl.semaphore_signal(barrier, inc=1, device_id=to_col(k), device_id_type=MESH)
    for k in range(1, 4):
        pl.semaphore_signal(barrier, inc=1, device_id=to_tile(k), device_id_type=MESH)
    pl.semaphore_wait(barrier, planes + owners_in + 1)

    order = nearest_first(planes)
    lid_sends = [
        send(lids_ref.at[at_plane(d)], z_lids.at[d], zl_send.at[d], zl_recv.at[d], to_plane(d))
        for d in order[1:]
    ]
    for copy in lid_sends:
        copy.start()
    own = pltpu.make_async_copy(packed_ref.at[my_plane], z_rows.at[0], own_sem)
    own.start()
    row_sends = {
        d: send(packed_ref.at[at_plane(d)], z_rows.at[d], z_send.at[d], z_recv.at[d], to_plane(d))
        for d in order[1:]
    }
    for d in order[1:]:
        row_sends[d].start()

    for copy in lid_sends:
        copy.wait_recv()
    lids = jnp.concatenate(
        [lids_ref[my_plane][0:1]] + [z_lids[d][0:1] for d in range(1, planes)], axis=0
    )
    lids_out[...] = pltpu.roll(lids, lax.rem(owners_in - my_col, owners_in) * SLOTS, 1)
    col_lid_sends = [
        send(lids_out, x_lids.at[k], xl_send.at[k], xl_recv.at[k], to_col(k))
        for k in range(1, owners_in)
    ]
    for copy in col_lid_sends:
        copy.start()
    before = hot(iota((lanes, lanes), 0) < iota((lanes, lanes), 1))
    rank = dot(hot(lids > 0.0), before)
    source = jnp.where(lids > 0.0, rank, -1.0)
    source = jnp.concatenate([source, jnp.zeros((BLOCK - planes, lanes), F32)], axis=0).T

    for copy in col_lid_sends:
        copy.wait_recv()
    got = jnp.zeros((planes, lanes), F32)
    group = iota((planes, lanes), 1) // SLOTS
    for k in range(owners_in):
        got += jnp.where(group == k, lids_out[...] if k == 0 else x_lids[k], 0.0)
    member = jnp.concatenate([hot(got == c + 1.0) for c in range(CLU_OWN)], axis=0)
    in_row = dot(member, before)
    in_rows = dot(member, jnp.ones((lanes, lanes), BF16))
    a, b = (iota((CLU_OWN * planes, CLU_OWN * planes), n) for n in (0, 1))
    earlier = dot(hot((a // planes == b // planes) & (b < a)), in_rows.astype(BF16))
    rank_all = in_row + earlier
    a, b = (iota((CLU_OWN, CLU_OWN * planes), n) for n in (0, 1))
    sizes = dot(hot(a == b // planes), in_rows.astype(BF16))
    ranked = jnp.zeros((planes, lanes), F32)
    for c in range(CLU_OWN):
        this = slice(c * planes, (c + 1) * planes)
        ranked += jnp.where(got == c + 1.0, rank_all[this], 0.0)
    target = jnp.where(got > 0.0, (got - 1.0) * CAP + ranked, -1.0).astype(jnp.int32)

    def forward_rows(d):
        if d == 0:
            own.wait()
        else:
            row_sends[d].wait_recv()
        take = source[:, d : d + 1].astype(jnp.int32) == iota((lanes, Z_SLOTS), 1)
        staged[d] = dot(hot(take), z_rows[d]).astype(BF16)
        copies = []
        for k in range(owners_in):
            start = pl.multiple_of(at_col(k) * SLOTS, SLOTS)
            src = staged.at[d, pl.ds(start, SLOTS)]
            dst = rows.at[d, pl.ds(k * SLOTS, SLOTS)]
            if k == 0:
                copy = pltpu.make_async_copy(src, dst, x_recv.at[d, 0])
            else:
                copy = send(src, dst, x_send.at[d, k], x_recv.at[d, k], to_col(k))
            copy.start()
            copies.append(copy)
        return copies

    def place_rows(d, copies, first):
        copies[0].wait()
        for copy in copies[1:]:
            copy.wait_recv()
        goal = target[d : d + 1]

        def body(c, carry):
            start = pl.multiple_of(c * CAP, CAP)
            chosen = hot(iota((CAP, lanes), 0) + start == goal)
            moved = dot(chosen, rows[d]).astype(BF16)
            span = pl.ds(start, CAP)
            if first:
                sorted_rows[span, :] = moved
            else:
                sorted_rows[span, :] = sorted_rows[span, :] + moved
            return carry

        lax.fori_loop(0, CLU_OWN, body, 0)

    x_copies = {}
    lag = 2
    for n, d in enumerate(order):
        x_copies[d] = forward_rows(d)
        if n >= lag:
            place_rows(order[n - lag], x_copies[order[n - lag]], n == lag)
    for n in range(max(0, len(order) - lag), len(order)):
        place_rows(order[n], x_copies[order[n]], n == 0)

    r, c = (iota((BLOCK, BLOCK), n) for n in (0, 1))

    def scores(t):
        thirds = []
        for j in range(2):
            start = pl.multiple_of((2 * t + j) * CAP, CAP)
            block = sorted_rows[pl.ds(start, CAP), :]
            one = dot(block[:BLOCK], block, NT)
            two = dot(block[BLOCK : 2 * BLOCK], block[BLOCK:], NT)
            three = dot(block[2 * BLOCK :], block[2 * BLOCK :], NT)
            base = 4 * j * BLOCK
            partial[t, base : base + BLOCK] = one[:, BLOCK : 2 * BLOCK]
            partial[t, base + BLOCK : base + 2 * BLOCK] = one[:, 2 * BLOCK :]
            partial[t, base + 2 * BLOCK : base + 3 * BLOCK] = two[:, BLOCK:]
            partial[t, base + 3 * BLOCK : base + 4 * BLOCK] = jnp.where(
                c > r, one[:, :BLOCK], two[:, :BLOCK]
            )
            thirds.append(three)
        partial[t, 8 * BLOCK : 9 * BLOCK] = jnp.where(c > r, thirds[0], thirds[1])

    right, left, across = at_tile(1), at_tile(3), at_tile(2)
    head, tail = pl.ds(0, half), pl.ds(half, half)
    scores(across)
    first = [
        send(partial.at[across, head], relay.at[0], y_send.at[0], y_recv.at[0], to_tile(1)),
        send(partial.at[across, tail], relay.at[1], y_send.at[1], y_recv.at[1], to_tile(3)),
    ]
    for copy in first:
        copy.start()
    scores(right)
    second = [send(partial.at[right, tail], near.at[1], y_send.at[2], y_recv.at[2], to_tile(1))]
    second[0].start()
    scores(left)
    second += [send(partial.at[left, head], near.at[0], y_send.at[3], y_recv.at[3], to_tile(3))]
    second[1].start()
    scores(tile)
    first[0].wait_recv()
    forward[0] = relay[0] + partial[right, 0:half]
    third_sends = [send(forward.at[0], far.at[0], y_send.at[4], y_recv.at[4], to_tile(1))]
    third_sends[0].start()
    first[1].wait_recv()
    forward[1] = relay[1] + partial[left, half : 2 * half]
    third_sends += [send(forward.at[1], far.at[1], y_send.at[5], y_recv.at[5], to_tile(3))]
    third_sends[1].start()
    for copy in second + third_sends:
        copy.wait_recv()
    summed = jnp.concatenate(
        [
            partial[tile, 0:half] + near[0] + far[0],
            partial[tile, half : 2 * half] + near[1] + far[1],
        ],
        axis=0,
    )

    size_rows = iota(sizes.shape, 0)
    best = []

    def highest(score, limit):
        return jnp.max(jnp.where(limit, score, -1.0), axis=0, keepdims=True)

    corner = summed[8 * BLOCK : 9 * BLOCK]
    for j in range(2):
        size = jnp.sum(
            jnp.where(size_rows == 2 * tile + j, sizes, 0.0), axis=0, keepdims=True
        )[:, :BLOCK].astype(jnp.int32)
        ok = [r + n * BLOCK < size for n in range(3)]
        ab, ac, bc, diagonal = (
            summed[(4 * j + n) * BLOCK : (4 * j + n + 1) * BLOCK] for n in range(4)
        )
        above, below = (c > r), (c < r)
        mine, theirs = (above, below) if j == 0 else (below, above)
        turned = diagonal.T
        corner_turned = corner.T
        zero = [
            highest(diagonal, ok[0] & above),
            highest(turned, ok[0] & below),
            highest(ab.T, ok[1]),
            highest(ac.T, ok[2]),
        ]
        one = [
            highest(diagonal, ok[1] & below),
            highest(turned, ok[1] & above),
            highest(ab, ok[0]),
            highest(bc.T, ok[2]),
        ]
        two = [
            highest(corner, ok[2] & mine),
            highest(corner_turned, ok[2] & theirs),
            highest(ac, ok[0]),
            highest(bc, ok[1]),
        ]
        best += [functools.reduce(jnp.maximum, parts) for parts in (zero, one, two)]
    found[tile] = jnp.concatenate(best + [jnp.zeros((2, BLOCK), F32)], axis=0)
    spread = [
        send(found.at[tile], found.at[tile], f_send.at[k], f_recv.at[k], to_tile(k))
        for k in range(1, 4)
    ]
    for copy in spread:
        copy.start()
    for k in range(1, 4):
        send(
            found.at[at_tile(4 - k)], found.at[at_tile(4 - k)], f_send.at[k], f_recv.at[k], to_tile(k)
        ).wait_recv()

    table = jnp.concatenate([found[t] for t in range(4)] + [jnp.zeros((BLOCK - 32, BLOCK), F32)], 0).T
    lid = got.astype(jnp.int32) - 1
    ranked = ranked.astype(jnp.int32)
    third = ranked // BLOCK
    table_row = (lid // 2) * 8 + (lid % 2) * 3 + third
    lane = ranked - third * BLOCK
    picked = []
    for d in range(planes):
        chosen = jnp.where(iota((BLOCK, lanes), 0) == table_row[d : d + 1], 1.0, 0.0)
        values = dot(table, chosen, precision=lax.Precision.HIGHEST)
        mask = iota((BLOCK, lanes), 0) == lane[d : d + 1]
        picked.append(jnp.sum(jnp.where(mask, values, 0.0), axis=0, keepdims=True))
    values_out[...] = jnp.concatenate(picked, axis=0)
    col_back = [
        send(
            values_out,
            x_back.at[k],
            xb_send.at[k],
            xb_recv.at[k],
            to_col(owners_in - k),
        )
        for k in range(1, owners_in)
    ]
    for copy in col_back:
        copy.start()
    home = jnp.where(group == 0, values_out[...], 0.0)
    for k in range(1, owners_in):
        col_back[k - 1].wait_recv()
        home += jnp.where(group == k, x_back[k], 0.0)
    values_home[...] = pltpu.roll(home, my_col * SLOTS, 1)
    plane_back = [
        send(
            values_home,
            z_back.at[d],
            zb_send.at[d],
            zb_recv.at[d],
            to_plane(planes - d),
        )
        for d in range(1, planes)
    ]
    for copy in plane_back:
        copy.start()
    for copy in plane_back:
        copy.wait_recv()
    mine = jnp.concatenate(
        [values_home[0:1]] + [z_back[d][d : d + 1] for d in range(1, planes)], axis=0
    )
    mine = jnp.concatenate([mine, jnp.zeros((BLOCK - planes, lanes), F32)], axis=0).T
    items = out_ref.shape[1]
    ahead = lax.rem(index_ref[0:1, :] - my_plane + planes, planes)
    chosen = jnp.where(iota((BLOCK, items), 0) == ahead, 1.0, 0.0)
    values = dot(mine, chosen, precision=lax.Precision.HIGHEST)
    mask = iota((lanes, items), 0) == index_ref[1:2, :]
    out_ref[...] = jnp.sum(jnp.where(mask, values, 0.0), axis=0, keepdims=True)

    for copy in lid_sends + col_lid_sends + first + second + third_sends + spread:
        copy.wait_send()
    for d in order[1:]:
        row_sends[d].wait_send()
    for d in order:
        for copy in x_copies[d][1:]:
            copy.wait_send()
    for copy in col_back + plane_back:
        copy.wait_send()


def route(planes, owners_in, packed, lids, index):
    part = packed.shape[2]
    items = index.shape[1]
    lanes = owners_in * SLOTS
    tiles = 9 * BLOCK
    vmem = pl.BlockSpec(memory_space=pltpu.VMEM)
    dma = lambda *shape: pltpu.SemaphoreType.DMA(shape)
    buffer = pltpu.VMEM
    return pl.pallas_call(
        functools.partial(route_kernel, planes, owners_in),
        out_shape=jax.ShapeDtypeStruct((1, items), F32),
        in_specs=[pl.BlockSpec(memory_space=pl.ANY), vmem, vmem],
        out_specs=vmem,
        scratch_shapes=[
            buffer((planes, Z_SLOTS, part), BF16),
            buffer((planes, 8, lanes), F32),
            buffer((planes, lanes), F32),
            buffer((owners_in, planes, lanes), F32),
            buffer((planes, lanes, part), BF16),
            buffer((planes, lanes, part), BF16),
            buffer((CLU_OWN * CAP, part), BF16),
            buffer((4, tiles, BLOCK), F32),
            buffer((2, tiles // 2, BLOCK), F32),
            buffer((2, tiles // 2, BLOCK), F32),
            buffer((2, tiles // 2, BLOCK), F32),
            buffer((2, tiles // 2, BLOCK), F32),
            buffer((4, 8, BLOCK), F32),
            buffer((planes, lanes), F32),
            buffer((owners_in, planes, lanes), F32),
            buffer((planes, lanes), F32),
            buffer((planes, planes, lanes), F32),
            pltpu.SemaphoreType.DMA,
            dma(planes),
            dma(planes),
            dma(planes),
            dma(planes),
            dma(owners_in),
            dma(owners_in),
            dma(planes, owners_in),
            dma(planes, owners_in),
            dma(6),
            dma(6),
            dma(4),
            dma(4),
            dma(owners_in),
            dma(owners_in),
            dma(planes),
            dma(planes),
        ],
        compiler_params=pltpu.CompilerParams(
            collective_id=0, has_side_effects=True, vmem_limit_bytes=52 * 1024 * 1024
        ),
    )(packed, lids, index)


def pair_best(row_block, row_labels, columns, column_labels, column_start):
    scores = lax.dot_general(
        row_block, columns, (((1,), (1,)), ((), ())), preferred_element_type=jnp.float32
    )
    row_ident = jnp.arange(row_block.shape[0], dtype=jnp.int32)
    column_ident = column_start + jnp.arange(columns.shape[0], dtype=jnp.int32)
    in_cluster = (
        (row_labels[:, None] == column_labels[None, :])
        & (row_labels[:, None] >= 0)
        & (row_ident[:, None] != column_ident[None, :])
    )
    return jnp.max(jnp.where(in_cluster, scores, -1.0), axis=1)


def any_layout(embeddings, cluster_ids):
    prod_count = lax.axis_size("prod")
    tile_count = lax.axis_size("tile")
    item_dev = embeddings.shape[0]
    width = embeddings.shape[1]
    group_rows = prod_count * SLOTS
    widened = embeddings.astype(jnp.float32)
    normed = (
        widened * lax.rsqrt(jnp.sum(widened * widened, axis=1, keepdims=True) + 1e-06)
    ).astype(jnp.bfloat16)
    owners = cluster_ids // CLU_OWN
    owner_hot = (owners[:, None] == jnp.arange(prod_count, dtype=jnp.int32)[None, :]).astype(
        jnp.int32
    )
    running = jnp.cumsum(owner_hot, axis=0)
    slot_index = jnp.sum(running * owner_hot, axis=1) - 1
    position = owners * SLOTS + slot_index
    inverse = (
        jnp.full((group_rows,), item_dev, jnp.int32)
        .at[position]
        .set(jnp.arange(item_dev, dtype=jnp.int32))
    )
    padded = jnp.concatenate([normed, jnp.zeros((1, width), jnp.bfloat16)], axis=0)
    labels = jnp.concatenate([cluster_ids, jnp.full((1,), -1, jnp.int32)], axis=0)
    outgoing = padded[inverse].reshape(prod_count, SLOTS, width)
    out_labels = labels[inverse].reshape(prod_count, SLOTS)
    tile_pos = lax.axis_index("tile")
    row_block, row_labels = (
        lax.all_to_all(outgoing, "prod", split_axis=0, concat_axis=0, tiled=True),
        lax.all_to_all(out_labels, "prod", split_axis=0, concat_axis=0, tiled=True),
    )
    row_block = row_block.reshape(group_rows, width)
    row_labels = row_labels.reshape(group_rows)
    piece_rows = group_rows // tile_count
    row_start = tile_pos * piece_rows
    columns = lax.dynamic_slice_in_dim(row_block, row_start, piece_rows, 0)
    column_labels = lax.dynamic_slice_in_dim(row_labels, row_start, piece_rows, 0)
    partial_best = pair_best(row_block, row_labels, columns, column_labels, row_start)
    maxima = lax.pmax(partial_best, "tile")
    returned = lax.all_to_all(
        maxima.reshape(prod_count, -1), "prod", split_axis=0, concat_axis=0, tiled=True
    )
    return returned.reshape(group_rows)[position]


def shards(embeddings, cluster_ids):
    prod_count = lax.axis_size("prod")
    owners_in = 8 if prod_count >= 64 else 4
    planes = prod_count // owners_in
    part = embeddings.shape[1] // lax.axis_size("tile")
    packed, lids, index, hist = pack(planes, owners_in, embeddings, cluster_ids, part)
    fits = jnp.max(lax.psum(hist, "prod")) <= CAP
    best = route(planes, owners_in, packed, lids, index).reshape(-1)
    return lax.cond(
        fits, lambda e, i, b: b, lambda e, i, b: any_layout(e, i), embeddings, cluster_ids, best
    )


def solution(mesh):
    placed = (P("prod", None), P("prod"))
    return jax.shard_map(shards, mesh=mesh, in_specs=placed, out_specs=P("prod"), check_vma=False)
```

```python
import functools

import jax
import jax.numpy as jnp
from jax import lax
from jax.experimental import pallas as pl
from jax.experimental.pallas import tpu as pltpu
from jax.sharding import PartitionSpec as P

CLU_OWN = 8
SLOTS = 32
Z_SLOTS = 176
BLOCK = 128
CAP = 3 * BLOCK
TOO_MANY = 4.0 * CLU_OWN
F32 = jnp.float32
BF16 = jnp.bfloat16
MESH = pl.DeviceIdType.MESH
NN = (((1,), (0,)), ((), ()))
NT = (((1,), (1,)), ((), ()))


def dot(a, b, dims=NN, precision=None):
    return lax.dot_general(a, b, dims, preferred_element_type=F32, precision=precision)


def iota(shape, dim):
    return lax.broadcasted_iota(jnp.int32, shape, dim)


def hot(cond):
    return jnp.where(cond, 1.0, 0.0).astype(BF16)


def pack_kernel(
    planes, owners_in, ids_ref, x_ref, packed_ref, lids_ref, index_ref, unit, counts
):
    step = pl.program_id(0)
    rows, width = x_ref.shape
    items = ids_ref.shape[1]
    part = unit.shape[1]
    tile = lax.axis_index("tile")

    total = jnp.zeros((rows, BLOCK), F32)
    for c in range(width // BLOCK):
        x = x_ref[:, c * BLOCK : (c + 1) * BLOCK].astype(F32)
        total += x * x
    scale = lax.rsqrt(jnp.sum(total, axis=1, keepdims=True) + 1e-06)
    mine = x_ref[:, pl.ds(pl.multiple_of(tile * part, part), part)].astype(F32)
    unit[pl.ds(pl.multiple_of(step * rows, rows), rows), :] = (mine * scale).astype(BF16)

    ids = ids_ref[...]
    owner = ids // CLU_OWN
    plane = owner // owners_in
    key = (owner * items + iota((1, items), 1)).astype(F32)
    plane_key = (plane * (owners_in * items)).astype(F32)
    owner_key = (owner * items).astype(F32)
    here = ids_ref[:, pl.ds(pl.multiple_of(step * rows, rows), rows)]
    here_key = ((here // CLU_OWN) * items + iota((1, rows), 1) + step * rows).astype(F32)
    column = jnp.broadcast_to(here_key, (BLOCK, rows)).T

    @pl.when(step == 0)
    def _():
        counts[...] = jnp.zeros_like(counts)

    for g in range(items // BLOCK):
        lanes = slice(g * BLOCK, (g + 1) * BLOCK)
        for n, bound in enumerate((key, plane_key, owner_key)):
            less = jnp.where(column < bound[:, lanes], 1.0, 0.0)
            counts[n : n + 1, lanes] += jnp.sum(less, axis=0, keepdims=True)

    @pl.when(step == pl.num_programs(0) - 1)
    def _():
        before = counts[0:1, :]
        position = (before - counts[1:2, :]).astype(jnp.int32)
        slot = (before - counts[2:3, :]).astype(jnp.int32)
        place = (owner % owners_in) * SLOTS + slot
        lid = ids % CLU_OWN
        for z in range(planes):
            pick = hot((iota((Z_SLOTS, items), 0) == position) & (plane == z))
            packed_ref[z] = dot(pick, unit[...]).astype(BF16)
        by_plane = jnp.where(iota((8, items), 0) == plane, lid + 1, 0).astype(F32).astype(BF16)
        by_place = hot(iota((owners_in * SLOTS, items), 0) == place)
        lids = dot(by_plane, by_place, NT)
        lids += jnp.where(jnp.max(position, axis=1, keepdims=True) >= Z_SLOTS, TOO_MANY, 0.0)
        for z in range(planes):
            lids_ref[z] = jnp.broadcast_to(lids[z : z + 1], lids_ref.shape[1:])
        row = iota((8, items), 0)
        index_ref[...] = jnp.where(row == 0, plane, place)


def pack(planes, owners_in, embeddings, cluster_ids, part):
    items, width = embeddings.shape
    lanes = owners_in * SLOTS
    whole = lambda shape: pl.BlockSpec(shape, lambda i: (0,) * len(shape))
    shapes = (
        jax.ShapeDtypeStruct((planes, Z_SLOTS, part), BF16),
        jax.ShapeDtypeStruct((planes, 8, lanes), F32),
        jax.ShapeDtypeStruct((8, items), jnp.int32),
    )
    return pl.pallas_call(
        functools.partial(pack_kernel, planes, owners_in),
        grid=(items // BLOCK,),
        in_specs=[whole((1, items)), pl.BlockSpec((BLOCK, width), lambda i: (i, 0))],
        out_specs=[whole(s.shape) for s in shapes],
        out_shape=shapes,
        scratch_shapes=[pltpu.VMEM((items, part), BF16), pltpu.VMEM((8, items), F32)],
        compiler_params=pltpu.CompilerParams(vmem_limit_bytes=40 * 1024 * 1024),
    )(cluster_ids.reshape(1, items), embeddings)


def nearest_first(n):
    order = [0]
    for d in range(1, n // 2 + 1):
        order += [d] if 2 * d == n else [d, n - d]
    return order


def route_kernel(
    planes,
    owners_in,
    packed_ref,
    lids_ref,
    index_ref,
    out_ref,
    z_rows,
    z_lids,
    lids_out,
    x_lids,
    staged,
    rows,
    sorted_rows,
    partial,
    relay,
    near,
    far,
    forward,
    found,
    values_out,
    x_back,
    values_home,
    z_back,
    own_sem,
    z_send,
    z_recv,
    zl_send,
    zl_recv,
    xl_send,
    xl_recv,
    x_send,
    x_recv,
    y_send,
    y_recv,
    f_send,
    f_recv,
    xb_send,
    xb_recv,
    zb_send,
    zb_recv,
):
    lanes = owners_in * SLOTS
    half = partial.shape[1] // 2
    me = lax.axis_index("prod")
    tile = lax.axis_index("tile")
    my_plane = me // owners_in
    my_col = lax.rem(me, owners_in)
    at_plane = lambda d: lax.rem(my_plane + d, planes)
    at_col = lambda k: lax.rem(my_col + k, owners_in)
    at_tile = lambda k: lax.rem(tile + k, 4)
    to_plane = lambda d: {"prod": at_plane(d) * owners_in + my_col}
    to_col = lambda k: {"prod": my_plane * owners_in + at_col(k)}
    to_tile = lambda k: {"tile": at_tile(k)}

    def send(src, dst, send_sem, recv_sem, device):
        return pltpu.make_async_remote_copy(
            src_ref=src,
            dst_ref=dst,
            send_sem=send_sem,
            recv_sem=recv_sem,
            device_id=device,
            device_id_type=MESH,
        )

    barrier = pltpu.get_barrier_semaphore()
    for d in range(1, planes):
        pl.semaphore_signal(barrier, inc=1, device_id=to_plane(d), device_id_type=MESH)
    for k in range(1, owners_in):
        pl.semaphore_signal(barrier, inc=1, device_id=to_col(k), device_id_type=MESH)
    for k in range(1, 4):
        pl.semaphore_signal(barrier, inc=1, device_id=to_tile(k), device_id_type=MESH)
    pl.semaphore_wait(barrier, planes + owners_in + 1)

    order = nearest_first(planes)
    lid_sends = [
        send(lids_ref.at[at_plane(d)], z_lids.at[d], zl_send.at[d], zl_recv.at[d], to_plane(d))
        for d in order[1:]
    ]
    for copy in lid_sends:
        copy.start()
    own = pltpu.make_async_copy(packed_ref.at[my_plane], z_rows.at[0], own_sem)
    own.start()
    row_sends = {
        d: send(packed_ref.at[at_plane(d)], z_rows.at[d], z_send.at[d], z_recv.at[d], to_plane(d))
        for d in order[1:]
    }
    for d in order[1:]:
        row_sends[d].start()

    for copy in lid_sends:
        copy.wait_recv()
    lids = jnp.concatenate(
        [lids_ref[my_plane][0:1]] + [z_lids[d][0:1] for d in range(1, planes)], axis=0
    )
    lids_out[...] = pltpu.roll(lids, lax.rem(owners_in - my_col, owners_in) * SLOTS, 1)
    col_lid_sends = [
        send(lids_out, x_lids.at[k], xl_send.at[k], xl_recv.at[k], to_col(k))
        for k in range(1, owners_in)
    ]
    for copy in col_lid_sends:
        copy.start()
    before = hot(iota((lanes, lanes), 0) < iota((lanes, lanes), 1))
    rank = dot(hot(lids > 0.0), before)
    source = jnp.where(lids > 0.0, rank, -1.0)
    source = jnp.concatenate([source, jnp.zeros((BLOCK - planes, lanes), F32)], axis=0).T

    for copy in col_lid_sends:
        copy.wait_recv()
    got = jnp.zeros((planes, lanes), F32)
    marks = lids_out[...]
    group = iota((planes, lanes), 1) // SLOTS
    for k in range(owners_in):
        theirs = lids_out[...] if k == 0 else x_lids[k]
        got += jnp.where(group == k, theirs, 0.0)
        marks = jnp.maximum(marks, theirs)
    member = jnp.concatenate([hot(got == c + 1.0) for c in range(CLU_OWN)], axis=0)
    in_row = dot(member, before)
    in_rows = dot(member, jnp.ones((lanes, lanes), BF16))
    a, b = (iota((CLU_OWN * planes, CLU_OWN * planes), n) for n in (0, 1))
    earlier = dot(hot((a // planes == b // planes) & (b < a)), in_rows.astype(BF16))
    rank_all = in_row + earlier
    a, b = (iota((CLU_OWN, CLU_OWN * planes), n) for n in (0, 1))
    sizes = dot(hot(a == b // planes), in_rows.astype(BF16))
    most = lambda a: jnp.max(jnp.max(a, axis=1, keepdims=True), axis=0, keepdims=True)
    unfit = (most(marks) >= TOO_MANY) | (most(sizes) > CAP)
    ranked = jnp.zeros((planes, lanes), F32)
    for c in range(CLU_OWN):
        this = slice(c * planes, (c + 1) * planes)
        ranked += jnp.where(got == c + 1.0, rank_all[this], 0.0)
    target = jnp.where(got > 0.0, (got - 1.0) * CAP + ranked, -1.0).astype(jnp.int32)

    def forward_rows(d):
        if d == 0:
            own.wait()
        else:
            row_sends[d].wait_recv()
        take = source[:, d : d + 1].astype(jnp.int32) == iota((lanes, Z_SLOTS), 1)
        staged[d] = dot(hot(take), z_rows[d]).astype(BF16)
        copies = []
        for k in range(owners_in):
            start = pl.multiple_of(at_col(k) * SLOTS, SLOTS)
            src = staged.at[d, pl.ds(start, SLOTS)]
            dst = rows.at[d, pl.ds(k * SLOTS, SLOTS)]
            if k == 0:
                copy = pltpu.make_async_copy(src, dst, x_recv.at[d, 0])
            else:
                copy = send(src, dst, x_send.at[d, k], x_recv.at[d, k], to_col(k))
            copy.start()
            copies.append(copy)
        return copies

    def place_rows(d, copies, first):
        copies[0].wait()
        for copy in copies[1:]:
            copy.wait_recv()
        goal = target[d : d + 1]

        def body(c, carry):
            start = pl.multiple_of(c * CAP, CAP)
            chosen = hot(iota((CAP, lanes), 0) + start == goal)
            moved = dot(chosen, rows[d]).astype(BF16)
            span = pl.ds(start, CAP)
            if first:
                sorted_rows[span, :] = moved
            else:
                sorted_rows[span, :] = sorted_rows[span, :] + moved
            return carry

        lax.fori_loop(0, CLU_OWN, body, 0)

    x_copies = {}
    lag = 2
    for n, d in enumerate(order):
        x_copies[d] = forward_rows(d)
        if n >= lag:
            place_rows(order[n - lag], x_copies[order[n - lag]], n == lag)
    for n in range(max(0, len(order) - lag), len(order)):
        place_rows(order[n], x_copies[order[n]], n == 0)

    r, c = (iota((BLOCK, BLOCK), n) for n in (0, 1))

    def scores(t):
        thirds = []
        for j in range(2):
            start = pl.multiple_of((2 * t + j) * CAP, CAP)
            block = sorted_rows[pl.ds(start, CAP), :]
            one = dot(block[:BLOCK], block, NT)
            two = dot(block[BLOCK : 2 * BLOCK], block[BLOCK:], NT)
            three = dot(block[2 * BLOCK :], block[2 * BLOCK :], NT)
            base = 4 * j * BLOCK
            partial[t, base : base + BLOCK] = one[:, BLOCK : 2 * BLOCK]
            partial[t, base + BLOCK : base + 2 * BLOCK] = one[:, 2 * BLOCK :]
            partial[t, base + 2 * BLOCK : base + 3 * BLOCK] = two[:, BLOCK:]
            partial[t, base + 3 * BLOCK : base + 4 * BLOCK] = jnp.where(
                c > r, one[:, :BLOCK], two[:, :BLOCK]
            )
            thirds.append(three)
        partial[t, 8 * BLOCK : 9 * BLOCK] = jnp.where(c > r, thirds[0], thirds[1])

    right, left, across = at_tile(1), at_tile(3), at_tile(2)
    head, tail = pl.ds(0, half), pl.ds(half, half)
    scores(across)
    first = [
        send(partial.at[across, head], relay.at[0], y_send.at[0], y_recv.at[0], to_tile(1)),
        send(partial.at[across, tail], relay.at[1], y_send.at[1], y_recv.at[1], to_tile(3)),
    ]
    for copy in first:
        copy.start()
    scores(right)
    second = [send(partial.at[right, tail], near.at[1], y_send.at[2], y_recv.at[2], to_tile(1))]
    second[0].start()
    scores(left)
    second += [send(partial.at[left, head], near.at[0], y_send.at[3], y_recv.at[3], to_tile(3))]
    second[1].start()
    scores(tile)
    first[0].wait_recv()
    forward[0] = relay[0] + partial[right, 0:half]
    third_sends = [send(forward.at[0], far.at[0], y_send.at[4], y_recv.at[4], to_tile(1))]
    third_sends[0].start()
    first[1].wait_recv()
    forward[1] = relay[1] + partial[left, half : 2 * half]
    third_sends += [send(forward.at[1], far.at[1], y_send.at[5], y_recv.at[5], to_tile(3))]
    third_sends[1].start()
    for copy in second + third_sends:
        copy.wait_recv()
    summed = jnp.concatenate(
        [
            partial[tile, 0:half] + near[0] + far[0],
            partial[tile, half : 2 * half] + near[1] + far[1],
        ],
        axis=0,
    )

    size_rows = iota(sizes.shape, 0)
    best = []

    def highest(score, limit):
        return jnp.max(jnp.where(limit, score, -1.0), axis=0, keepdims=True)

    corner = summed[8 * BLOCK : 9 * BLOCK]
    for j in range(2):
        size = jnp.sum(
            jnp.where(size_rows == 2 * tile + j, sizes, 0.0), axis=0, keepdims=True
        )[:, :BLOCK].astype(jnp.int32)
        ok = [r + n * BLOCK < size for n in range(3)]
        ab, ac, bc, diagonal = (
            summed[(4 * j + n) * BLOCK : (4 * j + n + 1) * BLOCK] for n in range(4)
        )
        above, below = (c > r), (c < r)
        mine, theirs = (above, below) if j == 0 else (below, above)
        turned = diagonal.T
        corner_turned = corner.T
        zero = [
            highest(diagonal, ok[0] & above),
            highest(turned, ok[0] & below),
            highest(ab.T, ok[1]),
            highest(ac.T, ok[2]),
        ]
        one = [
            highest(diagonal, ok[1] & below),
            highest(turned, ok[1] & above),
            highest(ab, ok[0]),
            highest(bc.T, ok[2]),
        ]
        two = [
            highest(corner, ok[2] & mine),
            highest(corner_turned, ok[2] & theirs),
            highest(ac, ok[0]),
            highest(bc, ok[1]),
        ]
        best += [functools.reduce(jnp.maximum, parts) for parts in (zero, one, two)]
    found[tile] = jnp.concatenate(best + [jnp.zeros((2, BLOCK), F32)], axis=0)
    spread = [
        send(found.at[tile], found.at[tile], f_send.at[k], f_recv.at[k], to_tile(k))
        for k in range(1, 4)
    ]
    for copy in spread:
        copy.start()
    for k in range(1, 4):
        send(
            found.at[at_tile(4 - k)], found.at[at_tile(4 - k)], f_send.at[k], f_recv.at[k], to_tile(k)
        ).wait_recv()

    table = jnp.concatenate([found[t] for t in range(4)] + [jnp.zeros((BLOCK - 32, BLOCK), F32)], 0).T
    lid = got.astype(jnp.int32) - 1
    ranked = ranked.astype(jnp.int32)
    third = ranked // BLOCK
    table_row = (lid // 2) * 8 + (lid % 2) * 3 + third
    lane = ranked - third * BLOCK
    picked = []
    for d in range(planes):
        chosen = jnp.where(iota((BLOCK, lanes), 0) == table_row[d : d + 1], 1.0, 0.0)
        values = dot(table, chosen, precision=lax.Precision.HIGHEST)
        mask = iota((BLOCK, lanes), 0) == lane[d : d + 1]
        picked.append(jnp.sum(jnp.where(mask, values, 0.0), axis=0, keepdims=True))
    values_out[...] = jnp.where(unfit, TOO_MANY, jnp.concatenate(picked, axis=0))
    col_back = [
        send(
            values_out,
            x_back.at[k],
            xb_send.at[k],
            xb_recv.at[k],
            to_col(owners_in - k),
        )
        for k in range(1, owners_in)
    ]
    for copy in col_back:
        copy.start()
    home = jnp.where(group == 0, values_out[...], 0.0)
    for k in range(1, owners_in):
        col_back[k - 1].wait_recv()
        home += jnp.where(group == k, x_back[k], 0.0)
    values_home[...] = pltpu.roll(home, my_col * SLOTS, 1)
    plane_back = [
        send(
            values_home,
            z_back.at[d],
            zb_send.at[d],
            zb_recv.at[d],
            to_plane(planes - d),
        )
        for d in range(1, planes)
    ]
    for copy in plane_back:
        copy.start()
    for copy in plane_back:
        copy.wait_recv()
    marks = values_home[...]
    for d in range(1, planes):
        marks = jnp.maximum(marks, z_back[d])
    unfit = most(marks) >= TOO_MANY
    mine = jnp.concatenate(
        [values_home[0:1]] + [z_back[d][d : d + 1] for d in range(1, planes)], axis=0
    )
    mine = jnp.concatenate([mine, jnp.zeros((BLOCK - planes, lanes), F32)], axis=0).T
    items = out_ref.shape[1]
    ahead = lax.rem(index_ref[0:1, :] - my_plane + planes, planes)
    chosen = jnp.where(iota((BLOCK, items), 0) == ahead, 1.0, 0.0)
    values = dot(mine, chosen, precision=lax.Precision.HIGHEST)
    mask = iota((lanes, items), 0) == index_ref[1:2, :]
    best = jnp.sum(jnp.where(mask, values, 0.0), axis=0, keepdims=True)
    out_ref[...] = jnp.where(unfit, TOO_MANY, best)

    for copy in lid_sends + col_lid_sends + first + second + third_sends + spread:
        copy.wait_send()
    for d in order[1:]:
        row_sends[d].wait_send()
    for d in order:
        for copy in x_copies[d][1:]:
            copy.wait_send()
    for copy in col_back + plane_back:
        copy.wait_send()


def route(planes, owners_in, packed, lids, index):
    part = packed.shape[2]
    items = index.shape[1]
    lanes = owners_in * SLOTS
    tiles = 9 * BLOCK
    vmem = pl.BlockSpec(memory_space=pltpu.VMEM)
    dma = lambda *shape: pltpu.SemaphoreType.DMA(shape)
    buffer = pltpu.VMEM
    return pl.pallas_call(
        functools.partial(route_kernel, planes, owners_in),
        out_shape=jax.ShapeDtypeStruct((1, items), F32),
        in_specs=[pl.BlockSpec(memory_space=pl.ANY), vmem, vmem],
        out_specs=vmem,
        scratch_shapes=[
            buffer((planes, Z_SLOTS, part), BF16),
            buffer((planes, 8, lanes), F32),
            buffer((planes, lanes), F32),
            buffer((owners_in, planes, lanes), F32),
            buffer((planes, lanes, part), BF16),
            buffer((planes, lanes, part), BF16),
            buffer((CLU_OWN * CAP, part), BF16),
            buffer((4, tiles, BLOCK), F32),
            buffer((2, tiles // 2, BLOCK), F32),
            buffer((2, tiles // 2, BLOCK), F32),
            buffer((2, tiles // 2, BLOCK), F32),
            buffer((2, tiles // 2, BLOCK), F32),
            buffer((4, 8, BLOCK), F32),
            buffer((planes, lanes), F32),
            buffer((owners_in, planes, lanes), F32),
            buffer((planes, lanes), F32),
            buffer((planes, planes, lanes), F32),
            pltpu.SemaphoreType.DMA,
            dma(planes),
            dma(planes),
            dma(planes),
            dma(planes),
            dma(owners_in),
            dma(owners_in),
            dma(planes, owners_in),
            dma(planes, owners_in),
            dma(6),
            dma(6),
            dma(4),
            dma(4),
            dma(owners_in),
            dma(owners_in),
            dma(planes),
            dma(planes),
        ],
        compiler_params=pltpu.CompilerParams(
            collective_id=0, has_side_effects=True, vmem_limit_bytes=52 * 1024 * 1024
        ),
    )(packed, lids, index)


def pair_best(row_block, row_labels, columns, column_labels, column_start):
    scores = lax.dot_general(
        row_block, columns, (((1,), (1,)), ((), ())), preferred_element_type=jnp.float32
    )
    row_ident = jnp.arange(row_block.shape[0], dtype=jnp.int32)
    column_ident = column_start + jnp.arange(columns.shape[0], dtype=jnp.int32)
    in_cluster = (
        (row_labels[:, None] == column_labels[None, :])
        & (row_labels[:, None] >= 0)
        & (row_ident[:, None] != column_ident[None, :])
    )
    return jnp.max(jnp.where(in_cluster, scores, -1.0), axis=1)


def any_layout(embeddings, cluster_ids):
    prod_count = lax.axis_size("prod")
    tile_count = lax.axis_size("tile")
    item_dev = embeddings.shape[0]
    width = embeddings.shape[1]
    group_rows = prod_count * SLOTS
    widened = embeddings.astype(jnp.float32)
    normed = (
        widened * lax.rsqrt(jnp.sum(widened * widened, axis=1, keepdims=True) + 1e-06)
    ).astype(jnp.bfloat16)
    owners = cluster_ids // CLU_OWN
    owner_hot = (owners[:, None] == jnp.arange(prod_count, dtype=jnp.int32)[None, :]).astype(
        jnp.int32
    )
    running = jnp.cumsum(owner_hot, axis=0)
    slot_index = jnp.sum(running * owner_hot, axis=1) - 1
    position = owners * SLOTS + slot_index
    inverse = (
        jnp.full((group_rows,), item_dev, jnp.int32)
        .at[position]
        .set(jnp.arange(item_dev, dtype=jnp.int32))
    )
    padded = jnp.concatenate([normed, jnp.zeros((1, width), jnp.bfloat16)], axis=0)
    labels = jnp.concatenate([cluster_ids, jnp.full((1,), -1, jnp.int32)], axis=0)
    outgoing = padded[inverse].reshape(prod_count, SLOTS, width)
    out_labels = labels[inverse].reshape(prod_count, SLOTS)
    tile_pos = lax.axis_index("tile")
    row_block, row_labels = (
        lax.all_to_all(outgoing, "prod", split_axis=0, concat_axis=0, tiled=True),
        lax.all_to_all(out_labels, "prod", split_axis=0, concat_axis=0, tiled=True),
    )
    row_block = row_block.reshape(group_rows, width)
    row_labels = row_labels.reshape(group_rows)
    piece_rows = group_rows // tile_count
    row_start = tile_pos * piece_rows
    columns = lax.dynamic_slice_in_dim(row_block, row_start, piece_rows, 0)
    column_labels = lax.dynamic_slice_in_dim(row_labels, row_start, piece_rows, 0)
    partial_best = pair_best(row_block, row_labels, columns, column_labels, row_start)
    maxima = lax.pmax(partial_best, "tile")
    returned = lax.all_to_all(
        maxima.reshape(prod_count, -1), "prod", split_axis=0, concat_axis=0, tiled=True
    )
    return returned.reshape(group_rows)[position]


def shards(embeddings, cluster_ids):
    prod_count = lax.axis_size("prod")
    owners_in = 8 if prod_count >= 64 else 4
    planes = prod_count // owners_in
    part = embeddings.shape[1] // lax.axis_size("tile")
    packed, lids, index = pack(planes, owners_in, embeddings, cluster_ids, part)
    best = route(planes, owners_in, packed, lids, index).reshape(-1)
    fits = jnp.max(best) < TOO_MANY
    return lax.cond(
        fits, lambda e, i, b: b, lambda e, i, b: any_layout(e, i), embeddings, cluster_ids, best
    )


def solution(mesh):
    placed = (P("prod", None), P("prod"))
    return jax.shard_map(shards, mesh=mesh, in_specs=placed, out_specs=P("prod"), check_vma=False)
```

```python
import functools

import jax
import jax.numpy as jnp
from jax import lax
from jax.experimental import pallas as pl
from jax.experimental.pallas import tpu as pltpu
from jax.sharding import PartitionSpec as P

CLU_OWN = 8
SLOTS = 32
Z_SLOTS = 176
BLOCK = 128
LATE = 3
FEW = 64
MANY = 2 * BLOCK
CAP = MANY + LATE * FEW
STARTS = (0, MANY, MANY + FEW, MANY + 2 * FEW)
SCORE_ROWS = (4 * BLOCK, 2 * BLOCK + FEW, 3 * BLOCK, 3 * BLOCK + FEW)
TOO_MANY = 4.0 * CLU_OWN
F32 = jnp.float32
BF16 = jnp.bfloat16
MESH = pl.DeviceIdType.MESH
NN = (((1,), (0,)), ((), ()))
NT = (((1,), (1,)), ((), ()))


def dot(a, b, dims=NN, precision=None):
    return lax.dot_general(a, b, dims, preferred_element_type=F32, precision=precision)


def iota(shape, dim):
    return lax.broadcasted_iota(jnp.int32, shape, dim)


def hot(cond):
    return jnp.where(cond, 1.0, 0.0).astype(BF16)


def nearest_first(n):
    order = [0]
    for d in range(1, n // 2 + 1):
        order += [d] if 2 * d == n else [d, n - d]
    return order


def highest(score, limit):
    return jnp.max(jnp.where(limit, score, -1.0), axis=0, keepdims=True)


def most(a):
    return jnp.max(jnp.max(a, axis=1, keepdims=True), axis=0, keepdims=True)


def kernel(
    planes,
    owners_in,
    ids_ref,
    x_ref,
    out_ref,
    flag_ref,
    x_rows,
    unit,
    index,
    packed,
    z_rows,
    lids_own,
    z_lids,
    lids_out,
    x_lids,
    staged,
    rows,
    sorted_rows,
    partial,
    relay,
    near,
    far,
    forward,
    values_out,
    x_back,
    values_home,
    z_back,
    load_sem,
    z_send,
    z_recv,
    zl_send,
    zl_recv,
    xl_send,
    xl_recv,
    x_send,
    x_recv,
    y_send,
    y_recv,
    xb_send,
    xb_recv,
    zb_send,
    zb_recv,
):
    lanes = owners_in * SLOTS
    owners = planes * owners_in
    items = ids_ref.shape[1]
    blocks, _, width = x_rows.shape
    part = unit.shape[1]
    me = lax.axis_index("prod")
    tile = lax.axis_index("tile")
    my_plane = me // owners_in
    my_col = lax.rem(me, owners_in)
    at_plane = lambda d: lax.rem(my_plane + d, planes)
    at_col = lambda k: lax.rem(my_col + k, owners_in)
    at_tile = lambda k: lax.rem(tile + k, 4)
    to_plane = lambda d: {"prod": at_plane(d) * owners_in + my_col}
    to_col = lambda k: {"prod": my_plane * owners_in + at_col(k)}
    to_tile = lambda k: {"tile": at_tile(k)}
    to_both = lambda k, j: {"prod": my_plane * owners_in + at_col(k), "tile": at_tile(j)}
    order = nearest_first(planes)
    first_late = planes - LATE
    started = []

    def send(src, dst, send_sem, recv_sem, device):
        copy = pltpu.make_async_remote_copy(
            src_ref=src,
            dst_ref=dst,
            send_sem=send_sem,
            recv_sem=recv_sem,
            device_id=device,
            device_id_type=MESH,
        )
        copy.start()
        started.append(copy)
        return copy

    loads = [
        pltpu.make_async_copy(
            x_ref.at[pl.ds(n * BLOCK, BLOCK)], x_rows.at[n], load_sem.at[n]
        )
        for n in range(blocks)
    ]
    for load in loads:
        load.start()

    barrier = pltpu.get_barrier_semaphore()
    for d in range(1, planes):
        pl.semaphore_signal(barrier, inc=1, device_id=to_plane(d), device_id_type=MESH)
    for k in range(owners_in):
        for j in range(4):
            if k or j:
                pl.semaphore_signal(
                    barrier, inc=1, device_id=to_both(k, j), device_id_type=MESH
                )

    ids = ids_ref[...]
    owner = ids // CLU_OWN
    plane = owner // owners_in
    lid = lax.rem(ids, CLU_OWN)
    owned = jnp.where(iota((owners, items), 0) == owner, 1.0, 0.0)
    before_block = hot(iota((BLOCK, BLOCK), 0) < iota((BLOCK, BLOCK), 1))
    count = jnp.zeros((owners, 1), F32)
    ahead = []
    for n in range(items // BLOCK):
        block = owned[:, n * BLOCK : (n + 1) * BLOCK]
        ahead.append(dot(block.astype(BF16), before_block) + count)
        count += jnp.sum(block, axis=1, keepdims=True)
    ahead = jnp.concatenate(ahead, axis=1)
    a, b = (iota((owners, owners), n) for n in (0, 1))
    lower = hot((a // owners_in == b // owners_in) & (b < a))
    offset = dot(lower, jnp.broadcast_to(count, (owners, BLOCK)).astype(BF16))[:, :1]
    slot = jnp.sum(owned * ahead, axis=0, keepdims=True).astype(jnp.int32)
    position = jnp.sum(owned * (ahead + offset), axis=0, keepdims=True).astype(jnp.int32)
    place = lax.rem(owner, owners_in) * SLOTS + slot
    row = iota((8, items), 0)
    index[...] = jnp.where(
        row == 0, lax.rem(plane - my_plane + planes, planes), jnp.where(row == 1, place, position)
    )
    by_plane = jnp.where(iota((planes, items), 0) == plane, lid + 1, 0).astype(F32).astype(BF16)
    by_place = hot(iota((lanes, items), 0) == place)
    lids = dot(by_plane, by_place, NT)
    lids += jnp.where(jnp.max(position, axis=1, keepdims=True) >= Z_SLOTS, TOO_MANY, 0.0)
    for z in range(planes):
        lids_own[z] = jnp.broadcast_to(lids[z : z + 1], lids_own.shape[1:])

    def unit_rows(n, carry):
        pltpu.make_async_copy(
            x_ref.at[pl.ds(pl.multiple_of(n * BLOCK, BLOCK), BLOCK)], x_rows.at[n], load_sem.at[n]
        ).wait()
        total = jnp.zeros((BLOCK, BLOCK), F32)
        for c in range(width // BLOCK):
            x = x_rows[n, :, c * BLOCK : (c + 1) * BLOCK].astype(F32)
            total += x * x
        scale = lax.rsqrt(jnp.sum(total, axis=1, keepdims=True) + 1e-06)
        mine = x_rows[n, :, pl.ds(pl.multiple_of(tile * part, part), part)].astype(F32)
        unit[pl.ds(pl.multiple_of(n * BLOCK, BLOCK), BLOCK), :] = (mine * scale).astype(BF16)
        return carry

    lax.fori_loop(0, blocks, unit_rows, 0)

    pl.semaphore_wait(barrier, planes - 1 + 4 * owners_in - 1)
    lid_copies = [
        send(lids_own.at[at_plane(d)], z_lids.at[d], zl_send.at[d], zl_recv.at[d], to_plane(d))
        for d in order[1:]
    ]
    row_copies = {}
    for d in order[1:3] + order[:1] + order[3:]:
        wanted = jnp.where(index[0:1, :] == d, index[2:3, :], -1)
        chosen = dot(hot(iota((Z_SLOTS, items), 0) == wanted), unit[...]).astype(BF16)
        if d == 0:
            z_rows[0] = chosen
        else:
            packed[d] = chosen
            row_copies[d] = send(
                packed.at[d], z_rows.at[d], z_send.at[d], z_recv.at[d], to_plane(d)
            )

    for copy in lid_copies:
        copy.wait_recv()
    lids = jnp.concatenate(
        [lids_own[my_plane][0:1]] + [z_lids[d][0:1] for d in range(1, planes)], axis=0
    )
    lids_out[...] = pltpu.roll(lids, lax.rem(owners_in - my_col, owners_in) * SLOTS, 1)
    col_lid_copies = [
        send(lids_out, x_lids.at[k], xl_send.at[k], xl_recv.at[k], to_col(k))
        for k in range(1, owners_in)
    ]
    before = hot(iota((lanes, lanes), 0) < iota((lanes, lanes), 1))
    rank = dot(hot(lids > 0.0), before)
    source = jnp.where(lids > 0.0, rank, -1.0)
    source = jnp.concatenate([source, jnp.zeros((BLOCK - planes, lanes), F32)], axis=0).T

    def forward_rows(d):
        if d:
            row_copies[d].wait_recv()
        take = source[:, d : d + 1].astype(jnp.int32) == iota((lanes, Z_SLOTS), 1)
        staged[d] = dot(hot(take), z_rows[d]).astype(BF16)
        copies = []
        for k in range(owners_in):
            start = pl.multiple_of(at_col(k) * SLOTS, SLOTS)
            src = staged.at[d, pl.ds(start, SLOTS)]
            dst = rows.at[d, pl.ds(k * SLOTS, SLOTS)]
            if k == 0:
                copy = pltpu.make_async_copy(src, dst, x_recv.at[d, 0])
                copy.start()
            else:
                copy = send(src, dst, x_send.at[d, k], x_recv.at[d, k], to_col(k))
            copies.append(copy)
        return copies

    x_copies = {order[0]: forward_rows(order[0])}

    for copy in col_lid_copies:
        copy.wait_recv()
    got = jnp.zeros((planes, lanes), F32)
    marks = lids_out[...]
    group = iota((planes, lanes), 1) // SLOTS
    for k in range(owners_in):
        theirs = lids_out[...] if k == 0 else x_lids[k]
        got += jnp.where(group == k, theirs, 0.0)
        marks = jnp.maximum(marks, theirs)

    def set_of(d):
        which = jnp.zeros(d.shape, jnp.int32)
        for n in range(LATE):
            which = jnp.where(d == order[first_late + n], n + 1, which)
        return which

    member = jnp.concatenate([hot(got == c + 1.0) for c in range(CLU_OWN)], axis=0)
    in_row = dot(member, before)
    in_rows = dot(member, jnp.ones((lanes, lanes), BF16)).astype(BF16)
    a, b = (iota((CLU_OWN * planes, CLU_OWN * planes), n) for n in (0, 1))
    same = (a // planes == b // planes) & (set_of(lax.rem(a, planes)) == set_of(lax.rem(b, planes)))
    rank_all = in_row + dot(hot(same & (b < a)), in_rows)
    a, b = (iota((CLU_OWN * (LATE + 1), CLU_OWN * planes), n) for n in (0, 1))
    same = (lax.rem(a, CLU_OWN) == b // planes) & (a // CLU_OWN == set_of(lax.rem(b, planes)))
    sizes = dot(hot(same), in_rows)
    unfit = (
        (most(marks) >= TOO_MANY)
        | (most(sizes[:CLU_OWN]) > MANY)
        | (most(sizes[CLU_OWN:]) > FEW)
    )
    ranked = jnp.zeros((planes, lanes), F32)
    for c in range(CLU_OWN):
        this = slice(c * planes, (c + 1) * planes)
        ranked += jnp.where(got == c + 1.0, rank_all[this], 0.0)
    late = set_of(iota((planes, lanes), 0))
    cluster = got.astype(jnp.int32) - 1
    ranked = ranked.astype(jnp.int32)
    target = jnp.where(cluster >= 0, cluster * jnp.where(late == 0, MANY, FEW) + ranked, -1)

    def place_rows(n):
        d = order[n]
        copies = x_copies[d]
        copies[0].wait()
        for copy in copies[1:]:
            copy.wait_recv()
        goal = target[d : d + 1]
        if n >= first_late:
            moved = dot(hot(iota((CLU_OWN * FEW, lanes), 0) == goal), rows[d]).astype(BF16)
            start = STARTS[n - first_late + 1]
            for c in range(CLU_OWN):
                sorted_rows[c, start : start + FEW, :] = moved[c * FEW : (c + 1) * FEW]
            return

        def body(c, carry):
            chosen = hot(iota((MANY, lanes), 0) + c * MANY == goal)
            moved = dot(chosen, rows[d]).astype(BF16)
            if n:
                sorted_rows[c, :MANY, :] = sorted_rows[c, :MANY, :] + moved
            else:
                sorted_rows[c, :MANY, :] = moved
            return carry

        lax.fori_loop(0, CLU_OWN, body, 0)

    r, c = (iota((BLOCK, BLOCK), n) for n in (0, 1))
    right, left, across = at_tile(1), at_tile(3), at_tile(2)
    spans = []
    for s, n in enumerate(SCORE_ROWS):
        spans.append((sum(SCORE_ROWS[:s]), n // 2))

    def scores(t, s):
        base = spans[s][0]
        if s == 0:
            for j in range(2):
                block = sorted_rows[2 * t + j, :MANY, :]
                all_pairs = dot(block, block, NT)
                at = base + 2 * j * BLOCK
                partial[t, at : at + BLOCK] = all_pairs[:BLOCK, BLOCK:]
                partial[t, at + BLOCK : at + 2 * BLOCK] = jnp.where(
                    c > r, all_pairs[:BLOCK, :BLOCK], all_pairs[BLOCK:, BLOCK:]
                )
            return
        start, stop = STARTS[s], STARTS[s] + FEW
        full = stop // BLOCK
        ends = []
        for j in range(2):
            new = sorted_rows[2 * t + j, start:stop, :]
            pairs = dot(new, sorted_rows[2 * t + j, : full * BLOCK, :], NT)
            for p in range(full):
                at = base + p * BLOCK + j * FEW
                partial[t, at : at + FEW] = pairs[:, p * BLOCK : (p + 1) * BLOCK]
            if stop % BLOCK:
                ends.append(dot(new, sorted_rows[2 * t + j, start - FEW : stop, :], NT))
        if ends:
            at = base + full * BLOCK
            partial[t, at : at + FEW] = jnp.where(
                c[:FEW] < FEW, pltpu.roll(ends[0], FEW, 1), ends[1]
            )

    y_copies = {}

    def y_send_to(s, n, src, dst, step):
        y_copies[s, n] = send(src, dst, y_send.at[s, n], y_recv.at[s, n], to_tile(step))

    def begin_sum(s):
        base, half = spans[s]
        head, tail, at = pl.ds(base, half), pl.ds(base + half, half), pl.ds(base // 2, half)
        scores(across, s)
        y_send_to(s, 0, partial.at[across, head], relay.at[0, at], 1)
        y_send_to(s, 1, partial.at[across, tail], relay.at[1, at], 3)
        scores(right, s)
        y_send_to(s, 2, partial.at[right, tail], near.at[1, at], 1)
        scores(left, s)
        y_send_to(s, 3, partial.at[left, head], near.at[0, at], 3)
        scores(tile, s)

    def relay_sum(s):
        base, half = spans[s]
        at = pl.ds(base // 2, half)
        y_copies[s, 0].wait_recv()
        forward[0, at] = relay[0, at] + partial[right, pl.ds(base, half)]
        y_send_to(s, 4, forward.at[0, at], far.at[0, at], 1)
        y_copies[s, 1].wait_recv()
        forward[1, at] = relay[1, at] + partial[left, pl.ds(base + half, half)]
        y_send_to(s, 5, forward.at[1, at], far.at[1, at], 3)

    def end_sum(s):
        base, half = spans[s]
        at = pl.ds(base // 2, half)
        for n in range(2, 6):
            y_copies[s, n].wait_recv()
        return jnp.concatenate(
            [partial[tile, pl.ds(base + h * half, half)] + near[h, at] + far[h, at] for h in (0, 1)],
            axis=0,
        )

    size_row = iota((BLOCK, lanes), 0)[: CLU_OWN * (LATE + 1)]
    size = [
        [
            jnp.sum(
                jnp.where(size_row == s * CLU_OWN + 2 * tile + j, sizes, 0.0), axis=0, keepdims=True
            )[:, :BLOCK].astype(jnp.int32)
            for j in range(2)
        ]
        for s in range(LATE + 1)
    ]
    lane = iota((1, BLOCK), 1)
    size_both = [jnp.where(lane < FEW, a, b) for a, b in size]
    by_column = {}
    by_new = {}

    def raise_to(j, p, value):
        by_column[j, p] = jnp.maximum(by_column[j, p], value) if (j, p) in by_column else value

    def best_of(s):
        total = end_sum(s)
        if s == 0:
            above, below = c > r, c < r
            for j in range(2):
                cross = total[2 * j * BLOCK : (2 * j + 1) * BLOCK]
                fold = total[(2 * j + 1) * BLOCK : (2 * j + 2) * BLOCK]
                turned = fold.T
                low, high = r < size[0][j], r + BLOCK < size[0][j]
                raise_to(j, 0, highest(fold, low & above))
                raise_to(j, 0, highest(turned, low & below))
                raise_to(j, 0, highest(cross.T, high))
                raise_to(j, 1, highest(fold, high & below))
                raise_to(j, 1, highest(turned, high & above))
                raise_to(j, 1, highest(cross, low))
            return
        start, stop = STARTS[s], STARTS[s] + FEW
        full = stop // BLOCK
        row_few, col_few = r[:FEW], c[:FEW]
        news = []
        for p in range(full):
            tile_p = total[p * BLOCK : (p + 1) * BLOCK]
            for j in range(2):
                limit = row_few < size[s][j]
                if (p + 1) * BLOCK == stop:
                    limit = limit & (col_few - FEW != row_few)
                raise_to(j, p, highest(tile_p[j * FEW : (j + 1) * FEW], limit))
            if p < 2:
                earlier = r + p * BLOCK < size_both[0]
            else:
                earlier = (r < FEW) & (r < size_both[1])
                if s == 3:
                    earlier = earlier | ((r >= FEW) & (r - FEW < size_both[2]))
            news.append(highest(tile_p.T, earlier))
        if stop % BLOCK:
            limit = (row_few < size_both[s]) & (row_few != lax.rem(col_few, FEW))
            news.append(highest(total[full * BLOCK :], limit))
        by_new[s] = functools.reduce(jnp.maximum, news)

    for n in range(planes):
        if n:
            x_copies[order[n]] = forward_rows(order[n])
            place_rows(n - 1)
            s = n - first_late
            if s == 0:
                begin_sum(0)
            elif s > 0:
                relay_sum(s - 1)
                begin_sum(s)
                if s >= 2:
                    best_of(s - 2)
    place_rows(planes - 1)
    relay_sum(LATE - 1)
    begin_sum(LATE)
    best_of(LATE - 2)
    relay_sum(LATE)
    best_of(LATE - 1)
    best_of(LATE)

    swap = lambda v: pltpu.roll(v, FEW, 1)
    low = lane < FEW
    raise_to(0, 2, jnp.where(low, by_new[1], swap(by_new[2])))
    raise_to(1, 2, jnp.where(low, swap(by_new[1]), by_new[2]))
    raise_to(0, 3, by_new[3])
    raise_to(1, 3, swap(by_new[3]))
    table = jnp.concatenate([by_column[j, p] for j in range(2) for p in range(4)], axis=0)
    table = jnp.concatenate([table, jnp.zeros((BLOCK - 8, BLOCK), F32)], axis=0).T

    where = ranked
    for s in range(1, LATE + 1):
        where = where + jnp.where(late == s, STARTS[s], 0)
    where_row = lax.rem(cluster + 2, 2) * 4 + where // BLOCK
    where_row = jnp.where((cluster >= 0) & (cluster // 2 == tile), where_row, -1)
    where_lane = lax.rem(where, BLOCK)
    picked = []
    for d in range(planes):
        values = jnp.zeros((BLOCK, lanes), F32)
        for n in range(8):
            values = jnp.where(where_row[d : d + 1] == n, table[:, n : n + 1], values)
        mask = iota((BLOCK, lanes), 0) == where_lane[d : d + 1]
        picked.append(jnp.sum(jnp.where(mask, values, 0.0), axis=0, keepdims=True))
    values_out[...] = jnp.where(unfit, TOO_MANY, jnp.concatenate(picked, axis=0))
    col_back = [
        send(
            values_out,
            x_back.at[j, k],
            xb_send.at[j, k],
            xb_recv.at[j, k],
            to_both(owners_in - k, j),
        )
        for k in range(owners_in)
        for j in range(4)
        if k or j
    ]
    home = jnp.where(group == 0, values_out[...], 0.0)
    for copy in col_back:
        copy.wait_recv()
    for k in range(owners_in):
        for j in range(4):
            if k or j:
                home += jnp.where(group == k, x_back[j, k], 0.0)
    values_home[...] = pltpu.roll(home, my_col * SLOTS, 1)
    plane_back = [
        send(values_home, z_back.at[d], zb_send.at[d], zb_recv.at[d], to_plane(planes - d))
        for d in range(1, planes)
    ]
    for copy in plane_back:
        copy.wait_recv()
    marks = values_home[...]
    for d in range(1, planes):
        marks = jnp.maximum(marks, z_back[d])
    flag_ref[0, 0] = jnp.max(marks)
    mine = jnp.concatenate(
        [values_home[0:1]] + [z_back[d][d : d + 1] for d in range(1, planes)], axis=0
    )
    mine = jnp.concatenate([mine, jnp.zeros((BLOCK - planes, lanes), F32)], axis=0).T
    chosen = jnp.where(iota((BLOCK, items), 0) == index[0:1, :], 1.0, 0.0)
    values = dot(mine, chosen, precision=lax.Precision.HIGHEST)
    mask = iota((lanes, items), 0) == index[1:2, :]
    out_ref[...] = jnp.sum(jnp.where(mask, values, 0.0), axis=0, keepdims=True)

    for copy in started:
        copy.wait_send()


def fast(planes, owners_in, embeddings, cluster_ids, part):
    items, width = embeddings.shape
    lanes = owners_in * SLOTS
    total = sum(SCORE_ROWS)
    vmem = pl.BlockSpec(memory_space=pltpu.VMEM)
    dma = lambda *shape: pltpu.SemaphoreType.DMA(shape)
    buffer = pltpu.VMEM
    return pl.pallas_call(
        functools.partial(kernel, planes, owners_in),
        out_shape=(jax.ShapeDtypeStruct((1, items), F32), jax.ShapeDtypeStruct((1, 1), F32)),
        in_specs=[vmem, pl.BlockSpec(memory_space=pl.ANY)],
        out_specs=(vmem, pl.BlockSpec(memory_space=pltpu.SMEM)),
        scratch_shapes=[
            buffer((items // BLOCK, BLOCK, width), BF16),
            buffer((items, part), BF16),
            buffer((8, items), jnp.int32),
            buffer((planes, Z_SLOTS, part), BF16),
            buffer((planes, Z_SLOTS, part), BF16),
            buffer((planes, 8, lanes), F32),
            buffer((planes, 8, lanes), F32),
            buffer((planes, lanes), F32),
            buffer((owners_in, planes, lanes), F32),
            buffer((planes, lanes, part), BF16),
            buffer((planes, lanes, part), BF16),
            buffer((CLU_OWN, CAP, part), BF16),
            buffer((4, total, BLOCK), F32),
            buffer((2, total // 2, BLOCK), F32),
            buffer((2, total // 2, BLOCK), F32),
            buffer((2, total // 2, BLOCK), F32),
            buffer((2, total // 2, BLOCK), F32),
            buffer((planes, lanes), F32),
            buffer((4, owners_in, planes, lanes), F32),
            buffer((planes, lanes), F32),
            buffer((planes, planes, lanes), F32),
            dma(items // BLOCK),
            dma(planes),
            dma(planes),
            dma(planes),
            dma(planes),
            dma(owners_in),
            dma(owners_in),
            dma(planes, owners_in),
            dma(planes, owners_in),
            dma(LATE + 1, 6),
            dma(LATE + 1, 6),
            dma(4, owners_in),
            dma(4, owners_in),
            dma(planes),
            dma(planes),
        ],
        compiler_params=pltpu.CompilerParams(
            collective_id=0, has_side_effects=True, vmem_limit_bytes=60 * 1024 * 1024
        ),
    )(cluster_ids.reshape(1, items), embeddings)


def pair_best(row_block, row_labels, columns, column_labels, column_start):
    scores = lax.dot_general(
        row_block, columns, (((1,), (1,)), ((), ())), preferred_element_type=jnp.float32
    )
    row_ident = jnp.arange(row_block.shape[0], dtype=jnp.int32)
    column_ident = column_start + jnp.arange(columns.shape[0], dtype=jnp.int32)
    in_cluster = (
        (row_labels[:, None] == column_labels[None, :])
        & (row_labels[:, None] >= 0)
        & (row_ident[:, None] != column_ident[None, :])
    )
    return jnp.max(jnp.where(in_cluster, scores, -1.0), axis=1)


def any_layout(embeddings, cluster_ids):
    prod_count = lax.axis_size("prod")
    tile_count = lax.axis_size("tile")
    item_dev = embeddings.shape[0]
    width = embeddings.shape[1]
    group_rows = prod_count * SLOTS
    widened = embeddings.astype(jnp.float32)
    normed = (
        widened * lax.rsqrt(jnp.sum(widened * widened, axis=1, keepdims=True) + 1e-06)
    ).astype(jnp.bfloat16)
    owners = cluster_ids // CLU_OWN
    owner_hot = (owners[:, None] == jnp.arange(prod_count, dtype=jnp.int32)[None, :]).astype(
        jnp.int32
    )
    running = jnp.cumsum(owner_hot, axis=0)
    slot_index = jnp.sum(running * owner_hot, axis=1) - 1
    position = owners * SLOTS + slot_index
    inverse = (
        jnp.full((group_rows,), item_dev, jnp.int32)
        .at[position]
        .set(jnp.arange(item_dev, dtype=jnp.int32))
    )
    padded = jnp.concatenate([normed, jnp.zeros((1, width), jnp.bfloat16)], axis=0)
    labels = jnp.concatenate([cluster_ids, jnp.full((1,), -1, jnp.int32)], axis=0)
    outgoing = padded[inverse].reshape(prod_count, SLOTS, width)
    out_labels = labels[inverse].reshape(prod_count, SLOTS)
    tile_pos = lax.axis_index("tile")
    row_block, row_labels = (
        lax.all_to_all(outgoing, "prod", split_axis=0, concat_axis=0, tiled=True),
        lax.all_to_all(out_labels, "prod", split_axis=0, concat_axis=0, tiled=True),
    )
    row_block = row_block.reshape(group_rows, width)
    row_labels = row_labels.reshape(group_rows)
    piece_rows = group_rows // tile_count
    row_start = tile_pos * piece_rows
    columns = lax.dynamic_slice_in_dim(row_block, row_start, piece_rows, 0)
    column_labels = lax.dynamic_slice_in_dim(row_labels, row_start, piece_rows, 0)
    partial_best = pair_best(row_block, row_labels, columns, column_labels, row_start)
    maxima = lax.pmax(partial_best, "tile")
    returned = lax.all_to_all(
        maxima.reshape(prod_count, -1), "prod", split_axis=0, concat_axis=0, tiled=True
    )
    return returned.reshape(group_rows)[position]


def shards(embeddings, cluster_ids):
    prod_count = lax.axis_size("prod")
    owners_in = 8 if prod_count >= 64 else 4
    planes = prod_count // owners_in
    part = embeddings.shape[1] // lax.axis_size("tile")
    best, mark = fast(planes, owners_in, embeddings, cluster_ids, part)
    fits = mark[0, 0] < TOO_MANY
    return lax.cond(
        fits,
        lambda e, i, b: b,
        lambda e, i, b: any_layout(e, i),
        embeddings,
        cluster_ids,
        best.reshape(-1),
    )


def solution(mesh):
    placed = (P("prod", None), P("prod"))
    return jax.shard_map(shards, mesh=mesh, in_specs=placed, out_specs=P("prod"), check_vma=False)
```

```python
import functools

import jax
import jax.numpy as jnp
from jax import lax
from jax.experimental import pallas as pl
from jax.experimental.pallas import tpu as pltpu
from jax.sharding import PartitionSpec as P

CLU_OWN = 8
SLOTS = 32
Z_SLOTS = 176
NEAR_SLOTS = SLOTS // 2
FAR_SLOTS = 48
BLOCK = 128
LATE = 3
FEW = 64
MANY = 2 * BLOCK
CAP = MANY + LATE * FEW
STARTS = (0, MANY, MANY + FEW, MANY + 2 * FEW)
SCORE_ROWS = (4 * BLOCK, 2 * BLOCK + FEW, 3 * BLOCK, 3 * BLOCK + FEW)
TOO_MANY = 4.0 * CLU_OWN
F32 = jnp.float32
BF16 = jnp.bfloat16
MESH = pl.DeviceIdType.MESH
NN = (((1,), (0,)), ((), ()))
NT = (((1,), (1,)), ((), ()))


def dot(a, b, dims=NN, precision=None):
    return lax.dot_general(a, b, dims, preferred_element_type=F32, precision=precision)


def iota(shape, dim):
    return lax.broadcasted_iota(jnp.int32, shape, dim)


def hot(cond):
    return jnp.where(cond, 1.0, 0.0).astype(BF16)


def nearest_first(n):
    order = [0]
    for d in range(1, n // 2 + 1):
        order += [d] if 2 * d == n else [d, n - d]
    return order


def highest(score, limit):
    return jnp.max(jnp.where(limit, score, -1.0), axis=0, keepdims=True)


def most(a):
    return jnp.max(jnp.max(a, axis=1, keepdims=True), axis=0, keepdims=True)


def kernel(
    planes,
    owners_in,
    ids_ref,
    x_ref,
    out_ref,
    flag_ref,
    x_rows,
    unit,
    index,
    packed,
    z_rows,
    lids_own,
    z_lids,
    lids_out,
    x_lids,
    staged,
    rows,
    far_rows,
    last_rows,
    sorted_rows,
    partial,
    relay,
    near,
    far,
    forward,
    values_out,
    x_back,
    values_home,
    z_back,
    load_sem,
    z_send,
    z_recv,
    zl_send,
    zl_recv,
    xl_send,
    xl_recv,
    x_send,
    x_recv,
    far_send,
    far_recv,
    y_send,
    y_recv,
    xb_send,
    xb_recv,
    zb_send,
    zb_recv,
):
    lanes = owners_in * SLOTS
    owners = planes * owners_in
    items = ids_ref.shape[1]
    blocks, _, width = x_rows.shape
    part = unit.shape[1]
    me = lax.axis_index("prod")
    tile = lax.axis_index("tile")
    my_plane = me // owners_in
    my_col = lax.rem(me, owners_in)
    at_plane = lambda d: lax.rem(my_plane + d, planes)
    at_col = lambda k: lax.rem(my_col + k, owners_in)
    at_tile = lambda k: lax.rem(tile + k, 4)
    to_plane = lambda d: {"prod": at_plane(d) * owners_in + my_col}
    to_col = lambda k: {"prod": my_plane * owners_in + at_col(k)}
    to_tile = lambda k: {"tile": at_tile(k)}
    to_far = lambda k: {"prod": at_plane(far_plane) * owners_in + at_col(k)}
    to_both = lambda k, j: {"prod": my_plane * owners_in + at_col(k), "tile": at_tile(j)}
    order = nearest_first(planes)
    far_plane = order[-1]
    first_late = planes - LATE + 1
    started = []

    def send(src, dst, send_sem, recv_sem, device):
        copy = pltpu.make_async_remote_copy(
            src_ref=src,
            dst_ref=dst,
            send_sem=send_sem,
            recv_sem=recv_sem,
            device_id=device,
            device_id_type=MESH,
        )
        copy.start()
        started.append(copy)
        return copy

    loads = [
        pltpu.make_async_copy(
            x_ref.at[pl.ds(n * BLOCK, BLOCK)], x_rows.at[n], load_sem.at[n]
        )
        for n in range(blocks)
    ]
    for load in loads:
        load.start()

    for k in range(owners_in):
        blank = jnp.zeros((NEAR_SLOTS, part), BF16)
        rows[far_plane, k * SLOTS : k * SLOTS + NEAR_SLOTS, :] = blank
        last_rows[k * SLOTS + NEAR_SLOTS : (k + 1) * SLOTS, :] = blank

    barrier = pltpu.get_barrier_semaphore()
    for d in range(1, planes):
        pl.semaphore_signal(barrier, inc=1, device_id=to_plane(d), device_id_type=MESH)
    for k in range(1, owners_in):
        pl.semaphore_signal(barrier, inc=1, device_id=to_far(k), device_id_type=MESH)
    for k in range(owners_in):
        for j in range(4):
            if k or j:
                pl.semaphore_signal(
                    barrier, inc=1, device_id=to_both(k, j), device_id_type=MESH
                )

    ids = ids_ref[...]
    owner = ids // CLU_OWN
    plane = owner // owners_in
    lid = lax.rem(ids, CLU_OWN)
    owned = jnp.where(iota((owners, items), 0) == owner, 1.0, 0.0)
    before_block = hot(iota((BLOCK, BLOCK), 0) < iota((BLOCK, BLOCK), 1))
    count = jnp.zeros((owners, 1), F32)
    ahead = []
    for n in range(items // BLOCK):
        block = owned[:, n * BLOCK : (n + 1) * BLOCK]
        ahead.append(dot(block.astype(BF16), before_block) + count)
        count += jnp.sum(block, axis=1, keepdims=True)
    ahead = jnp.concatenate(ahead, axis=1)
    a, b = (iota((owners, owners), n) for n in (0, 1))
    lower = hot((a // owners_in == b // owners_in) & (b < a))
    offset = dot(lower, jnp.broadcast_to(count, (owners, BLOCK)).astype(BF16))[:, :1]
    slot = jnp.sum(owned * ahead, axis=0, keepdims=True).astype(jnp.int32)
    position = jnp.sum(owned * (ahead + offset), axis=0, keepdims=True).astype(jnp.int32)
    spill = jnp.broadcast_to(jnp.maximum(count - NEAR_SLOTS, 0.0), (owners, BLOCK)).astype(BF16)
    spill = jnp.sum(owned * dot(lower, spill)[:, :1], axis=0, keepdims=True).astype(jnp.int32)
    column = lax.rem(owner, owners_in)
    place = column * SLOTS + slot
    away = lax.rem(plane - my_plane + planes, planes)
    direct = jnp.where(slot < NEAR_SLOTS, column * NEAR_SLOTS + slot, -1)
    spilled = jnp.where(slot < NEAR_SLOTS, -1, spill + slot - NEAR_SLOTS)
    for n, line in enumerate((away, place, position, direct, spilled)):
        index[n : n + 1, :] = line
    room = (position < Z_SLOTS) & ((away != far_plane) | (spilled < FAR_SLOTS))
    crowded = jnp.max(jnp.where(room, 0.0, TOO_MANY), axis=1, keepdims=True)
    by_plane = jnp.where(iota((planes, items), 0) == plane, lid + 1, 0).astype(F32).astype(BF16)
    by_place = hot(iota((lanes, items), 0) == place)
    lids = dot(by_plane, by_place, NT)
    lids += crowded
    for z in range(planes):
        lids_own[z] = jnp.broadcast_to(lids[z : z + 1], lids_own.shape[1:])

    def unit_rows(n, carry):
        pltpu.make_async_copy(
            x_ref.at[pl.ds(pl.multiple_of(n * BLOCK, BLOCK), BLOCK)], x_rows.at[n], load_sem.at[n]
        ).wait()
        total = jnp.zeros((BLOCK, BLOCK), F32)
        for c in range(width // BLOCK):
            x = x_rows[n, :, c * BLOCK : (c + 1) * BLOCK].astype(F32)
            total += x * x
        scale = lax.rsqrt(jnp.sum(total, axis=1, keepdims=True) + 1e-06)
        mine = x_rows[n, :, pl.ds(pl.multiple_of(tile * part, part), part)].astype(F32)
        unit[pl.ds(pl.multiple_of(n * BLOCK, BLOCK), BLOCK), :] = (mine * scale).astype(BF16)
        return carry

    lax.fori_loop(0, blocks, unit_rows, 0)

    pl.semaphore_wait(barrier, planes - 1 + owners_in - 1 + 4 * owners_in - 1)
    lid_copies = [
        send(lids_own.at[at_plane(d)], z_lids.at[d], zl_send.at[d], zl_recv.at[d], to_plane(d))
        for d in order[1:]
    ]
    row_copies = {}

    def chosen_rows(d, line, count):
        wanted = jnp.where(index[0:1, :] == d, index[line : line + 1, :], -1)
        return dot(hot(iota((count, items), 0) == wanted), unit[...]).astype(BF16)

    def send_rows(d, line, count):
        packed[d, :count, :] = chosen_rows(d, line, count)
        at = pl.ds(0, count)
        row_copies[d] = send(
            packed.at[d, at], z_rows.at[d, at], z_send.at[d], z_recv.at[d], to_plane(d)
        )

    for n, d in enumerate(order[1:-1]):
        if n == planes // 4:
            z_rows[0] = chosen_rows(0, 2, Z_SLOTS)
        if n == len(order) - 4:
            send_rows(far_plane, 4, FAR_SLOTS)
        send_rows(d, 2, Z_SLOTS)
    far_rows[...] = chosen_rows(far_plane, 3, owners_in * NEAR_SLOTS)
    last_copies = []
    for k in range(owners_in):
        start = pl.multiple_of(at_col(k) * NEAR_SLOTS, NEAR_SLOTS)
        last_copies.append(
            send(
                far_rows.at[pl.ds(start, NEAR_SLOTS)],
                last_rows.at[pl.ds(k * SLOTS, NEAR_SLOTS)],
                far_send.at[k],
                far_recv.at[k],
                to_far(k),
            )
        )

    for copy in lid_copies:
        copy.wait_recv()
    lids = jnp.concatenate(
        [lids_own[my_plane][0:1]] + [z_lids[d][0:1] for d in range(1, planes)], axis=0
    )
    lids_out[...] = pltpu.roll(lids, lax.rem(owners_in - my_col, owners_in) * SLOTS, 1)
    col_lid_copies = [
        send(lids_out, x_lids.at[k], xl_send.at[k], xl_recv.at[k], to_col(k))
        for k in range(1, owners_in)
    ]
    before = hot(iota((lanes, lanes), 0) < iota((lanes, lanes), 1))
    near_slot = lax.rem(iota((planes, lanes), 1), SLOTS) < NEAR_SLOTS
    last = near_slot & (iota((planes, lanes), 0) == far_plane)
    taken = (lids > 0.0) & jnp.logical_not(last)
    source = jnp.where(taken, dot(hot(taken), before), -1.0)
    source = jnp.concatenate([source, jnp.zeros((BLOCK - planes, lanes), F32)], axis=0).T

    def forward_rows(d):
        if d:
            row_copies[d].wait_recv()
        count, skip = (FAR_SLOTS, NEAR_SLOTS) if d == far_plane else (Z_SLOTS, 0)
        take = source[:, d : d + 1].astype(jnp.int32) == iota((lanes, count), 1)
        staged[d] = dot(hot(take), z_rows[d, :count, :]).astype(BF16)
        copies = []
        for k in range(owners_in):
            start = pl.multiple_of(at_col(k) * SLOTS + skip, NEAR_SLOTS)
            src = staged.at[d, pl.ds(start, SLOTS - skip)]
            dst = rows.at[d, pl.ds(k * SLOTS + skip, SLOTS - skip)]
            if k == 0:
                copy = pltpu.make_async_copy(src, dst, x_recv.at[d, 0])
                copy.start()
            else:
                copy = send(src, dst, x_send.at[d, k], x_recv.at[d, k], to_col(k))
            copies.append(copy)
        return copies

    steps = order[:-LATE] + [far_plane] + order[-LATE:-1]
    x_copies = {steps[0]: forward_rows(steps[0])}

    for copy in col_lid_copies:
        copy.wait_recv()
    got = jnp.zeros((planes, lanes), F32)
    marks = lids_out[...]
    group = iota((planes, lanes), 1) // SLOTS
    for k in range(owners_in):
        theirs = lids_out[...] if k == 0 else x_lids[k]
        got += jnp.where(group == k, theirs, 0.0)
        marks = jnp.maximum(marks, theirs)

    def set_of(d):
        which = jnp.zeros(d.shape, jnp.int32)
        for n in range(1, LATE):
            which = jnp.where(d == order[n - LATE - 1 + planes], n, which)
        return which

    other = jnp.where(last, 0.0, got)
    member = jnp.concatenate([hot(other == c + 1.0) for c in range(CLU_OWN)], axis=0)
    ending = jnp.where(near_slot, got, 0.0)[far_plane : far_plane + 1]
    ending = hot(ending == iota((CLU_OWN, lanes), 0).astype(F32) + 1.0)
    ending_rank = dot(ending, before)
    ending_size = dot(ending, jnp.ones((lanes, lanes), BF16))
    in_row = dot(member, before)
    in_rows = dot(member, jnp.ones((lanes, lanes), BF16)).astype(BF16)
    a, b = (iota((CLU_OWN * planes, CLU_OWN * planes), n) for n in (0, 1))
    same = (a // planes == b // planes) & (set_of(lax.rem(a, planes)) == set_of(lax.rem(b, planes)))
    rank_all = in_row + dot(hot(same & (b < a)), in_rows)
    a, b = (iota((CLU_OWN * LATE, CLU_OWN * planes), n) for n in (0, 1))
    same = (lax.rem(a, CLU_OWN) == b // planes) & (a // CLU_OWN == set_of(lax.rem(b, planes)))
    sizes = jnp.concatenate([dot(hot(same), in_rows), ending_size], axis=0)
    unfit = (
        (most(marks) >= TOO_MANY)
        | (most(sizes[:CLU_OWN]) > MANY)
        | (most(sizes[CLU_OWN:]) > FEW)
    )
    ranked = jnp.zeros((planes, lanes), F32)
    for c in range(CLU_OWN):
        this = slice(c * planes, (c + 1) * planes)
        rank_here = jnp.where(last, ending_rank[c : c + 1], rank_all[this])
        ranked += jnp.where(got == c + 1.0, rank_here, 0.0)
    late = jnp.where(last, LATE, set_of(iota((planes, lanes), 0)))
    cluster = got.astype(jnp.int32) - 1
    ranked = ranked.astype(jnp.int32)
    target = jnp.where(cluster >= 0, cluster * jnp.where(late == 0, MANY, FEW) + ranked, -1)

    def place_few(n, goal, arrived):
        moved = dot(hot(iota((CLU_OWN * FEW, lanes), 0) == goal), arrived).astype(BF16)
        for c in range(CLU_OWN):
            sorted_rows[c, STARTS[n] : STARTS[n] + FEW, :] = moved[c * FEW : (c + 1) * FEW]

    def place_rows(n):
        d = steps[n]
        copies = x_copies[d]
        copies[0].wait()
        for copy in copies[1:]:
            copy.wait_recv()
        goal = jnp.where(last, -1, target)[d : d + 1]
        if n >= first_late:
            place_few(n - first_late + 1, goal, rows[d])
            return

        def body(c, carry):
            chosen = hot(iota((MANY, lanes), 0) + c * MANY == goal)
            moved = dot(chosen, rows[d]).astype(BF16)
            if n:
                sorted_rows[c, :MANY, :] = sorted_rows[c, :MANY, :] + moved
            else:
                sorted_rows[c, :MANY, :] = moved
            return carry

        lax.fori_loop(0, CLU_OWN, body, 0)

    r, c = (iota((BLOCK, BLOCK), n) for n in (0, 1))
    right, left, across = at_tile(1), at_tile(3), at_tile(2)
    spans = []
    for s, n in enumerate(SCORE_ROWS):
        spans.append((sum(SCORE_ROWS[:s]), n // 2))

    def scores(t, s):
        base = spans[s][0]
        if s == 0:
            for j in range(2):
                block = sorted_rows[2 * t + j, :MANY, :]
                all_pairs = dot(block, block, NT)
                at = base + 2 * j * BLOCK
                partial[t, at : at + BLOCK] = all_pairs[:BLOCK, BLOCK:]
                partial[t, at + BLOCK : at + 2 * BLOCK] = jnp.where(
                    c > r, all_pairs[:BLOCK, :BLOCK], all_pairs[BLOCK:, BLOCK:]
                )
            return
        start, stop = STARTS[s], STARTS[s] + FEW
        full = stop // BLOCK
        ends = []
        for j in range(2):
            new = sorted_rows[2 * t + j, start:stop, :]
            pairs = dot(new, sorted_rows[2 * t + j, : full * BLOCK, :], NT)
            for p in range(full):
                at = base + p * BLOCK + j * FEW
                partial[t, at : at + FEW] = pairs[:, p * BLOCK : (p + 1) * BLOCK]
            if stop % BLOCK:
                ends.append(dot(new, sorted_rows[2 * t + j, start - FEW : stop, :], NT))
        if ends:
            at = base + full * BLOCK
            partial[t, at : at + FEW] = jnp.where(
                c[:FEW] < FEW, pltpu.roll(ends[0], FEW, 1), ends[1]
            )

    y_copies = {}

    def y_send_to(s, n, src, dst, step):
        y_copies[s, n] = send(src, dst, y_send.at[s, n], y_recv.at[s, n], to_tile(step))

    def begin_sum(s):
        base, half = spans[s]
        head, tail, at = pl.ds(base, half), pl.ds(base + half, half), pl.ds(base // 2, half)
        scores(across, s)
        y_send_to(s, 0, partial.at[across, head], relay.at[0, at], 1)
        y_send_to(s, 1, partial.at[across, tail], relay.at[1, at], 3)
        scores(right, s)
        y_send_to(s, 2, partial.at[right, tail], near.at[1, at], 1)
        scores(left, s)
        y_send_to(s, 3, partial.at[left, head], near.at[0, at], 3)
        scores(tile, s)

    def relay_sum(s):
        base, half = spans[s]
        at = pl.ds(base // 2, half)
        y_copies[s, 0].wait_recv()
        forward[0, at] = relay[0, at] + partial[right, pl.ds(base, half)]
        y_send_to(s, 4, forward.at[0, at], far.at[0, at], 1)
        y_copies[s, 1].wait_recv()
        forward[1, at] = relay[1, at] + partial[left, pl.ds(base + half, half)]
        y_send_to(s, 5, forward.at[1, at], far.at[1, at], 3)

    def end_sum(s):
        base, half = spans[s]
        at = pl.ds(base // 2, half)
        for n in range(2, 6):
            y_copies[s, n].wait_recv()
        return jnp.concatenate(
            [partial[tile, pl.ds(base + h * half, half)] + near[h, at] + far[h, at] for h in (0, 1)],
            axis=0,
        )

    size_row = iota((BLOCK, lanes), 0)[: CLU_OWN * (LATE + 1)]
    size = [
        [
            jnp.sum(
                jnp.where(size_row == s * CLU_OWN + 2 * tile + j, sizes, 0.0), axis=0, keepdims=True
            )[:, :BLOCK].astype(jnp.int32)
            for j in range(2)
        ]
        for s in range(LATE + 1)
    ]
    lane = iota((1, BLOCK), 1)
    size_both = [jnp.where(lane < FEW, a, b) for a, b in size]
    by_column = {}
    by_new = {}

    def raise_to(j, p, value):
        by_column[j, p] = jnp.maximum(by_column[j, p], value) if (j, p) in by_column else value

    def best_of(s):
        total = end_sum(s)
        if s == 0:
            above, below = c > r, c < r
            for j in range(2):
                cross = total[2 * j * BLOCK : (2 * j + 1) * BLOCK]
                fold = total[(2 * j + 1) * BLOCK : (2 * j + 2) * BLOCK]
                turned = fold.T
                low, high = r < size[0][j], r + BLOCK < size[0][j]
                raise_to(j, 0, highest(fold, low & above))
                raise_to(j, 0, highest(turned, low & below))
                raise_to(j, 0, highest(cross.T, high))
                raise_to(j, 1, highest(fold, high & below))
                raise_to(j, 1, highest(turned, high & above))
                raise_to(j, 1, highest(cross, low))
            return
        start, stop = STARTS[s], STARTS[s] + FEW
        full = stop // BLOCK
        row_few, col_few = r[:FEW], c[:FEW]
        news = []
        for p in range(full):
            tile_p = total[p * BLOCK : (p + 1) * BLOCK]
            for j in range(2):
                limit = row_few < size[s][j]
                if (p + 1) * BLOCK == stop:
                    limit = limit & (col_few - FEW != row_few)
                raise_to(j, p, highest(tile_p[j * FEW : (j + 1) * FEW], limit))
            if p < 2:
                earlier = r + p * BLOCK < size_both[0]
            else:
                earlier = (r < FEW) & (r < size_both[1])
                if s == 3:
                    earlier = earlier | ((r >= FEW) & (r - FEW < size_both[2]))
            news.append(highest(tile_p.T, earlier))
        if stop % BLOCK:
            limit = (row_few < size_both[s]) & (row_few != lax.rem(col_few, FEW))
            news.append(highest(total[full * BLOCK :], limit))
        by_new[s] = functools.reduce(jnp.maximum, news)

    def after(n):
        s = n - first_late + 1
        if s == 0:
            begin_sum(0)
        elif s > 0:
            relay_sum(s - 1)
            begin_sum(s)
            if s >= 2:
                best_of(s - 2)

    for n in range(1, planes):
        x_copies[steps[n]] = forward_rows(steps[n])
        place_rows(n - 1)
        after(n - 1)
    place_rows(planes - 1)
    after(planes - 1)
    for copy in last_copies:
        copy.wait_recv()
    place_few(LATE, jnp.where(last, target, -1)[far_plane : far_plane + 1], last_rows[...])
    after(planes)
    relay_sum(LATE)
    best_of(LATE - 1)
    best_of(LATE)

    swap = lambda v: pltpu.roll(v, FEW, 1)
    low = lane < FEW
    raise_to(0, 2, jnp.where(low, by_new[1], swap(by_new[2])))
    raise_to(1, 2, jnp.where(low, swap(by_new[1]), by_new[2]))
    raise_to(0, 3, by_new[3])
    raise_to(1, 3, swap(by_new[3]))
    table = jnp.concatenate([by_column[j, p] for j in range(2) for p in range(4)], axis=0)
    table = jnp.concatenate([table, jnp.zeros((BLOCK - 8, BLOCK), F32)], axis=0).T

    where = ranked
    for s in range(1, LATE + 1):
        where = where + jnp.where(late == s, STARTS[s], 0)
    where_row = lax.rem(cluster + 2, 2) * 4 + where // BLOCK
    where_row = jnp.where((cluster >= 0) & (cluster // 2 == tile), where_row, -1)
    where_lane = lax.rem(where, BLOCK)
    picked = []
    for d in range(planes):
        values = jnp.zeros((BLOCK, lanes), F32)
        for n in range(8):
            values = jnp.where(where_row[d : d + 1] == n, table[:, n : n + 1], values)
        mask = iota((BLOCK, lanes), 0) == where_lane[d : d + 1]
        picked.append(jnp.sum(jnp.where(mask, values, 0.0), axis=0, keepdims=True))
    values = jnp.where(unfit, TOO_MANY, jnp.concatenate(picked, axis=0))

    def turn(v):
        shifted = [v] + [pltpu.roll(v, n * SLOTS, 1) for n in range(1, planes)]
        mine = iota(v.shape, 0) == group
        lines = []
        for b in range(planes):
            line = jnp.zeros(v.shape, F32)
            for a in range(planes):
                line = jnp.where(mine & (group == a), shifted[(a - b) % planes], line)
            lines.append(jnp.sum(line, axis=0, keepdims=True))
        return lines

    for k, line in enumerate(turn(values)):
        values_out[k] = line
    col_back = [
        send(
            values_out.at[k],
            x_back.at[j, k],
            xb_send.at[j, k],
            xb_recv.at[j, k],
            to_both(owners_in - k, j),
        )
        for k in range(owners_in)
        for j in range(4)
        if k or j
    ]
    for copy in col_back:
        copy.wait_recv()
    home = []
    for k in range(owners_in):
        parts = [x_back[j, k] if k or j else values_out[0] for j in range(4)]
        home.append(functools.reduce(jnp.add, parts))
    home = jnp.concatenate(turn(jnp.concatenate(home, axis=0)), axis=0)
    home = pltpu.roll(home, my_col * SLOTS, 1)
    for d in range(planes):
        values_home[d] = home[d : d + 1]
    plane_back = [
        send(
            values_home.at[d], z_back.at[d], zb_send.at[d], zb_recv.at[d], to_plane(planes - d)
        )
        for d in range(1, planes)
    ]
    for copy in plane_back:
        copy.wait_recv()
    mine = jnp.concatenate([values_home[0]] + [z_back[d] for d in range(1, planes)], axis=0)
    flag_ref[0, 0] = jnp.max(mine)
    mine = jnp.concatenate([mine, jnp.zeros((BLOCK - planes, lanes), F32)], axis=0).T
    values = jnp.zeros((lanes, items), F32)
    for d in range(planes):
        values = jnp.where(index[0:1, :] == d, mine[:, d : d + 1], values)
    mask = iota((lanes, items), 0) == index[1:2, :]
    out_ref[...] = jnp.sum(jnp.where(mask, values, 0.0), axis=0, keepdims=True)

    for copy in started:
        copy.wait_send()


def fast(planes, owners_in, embeddings, cluster_ids, part):
    items, width = embeddings.shape
    lanes = owners_in * SLOTS
    total = sum(SCORE_ROWS)
    vmem = pl.BlockSpec(memory_space=pltpu.VMEM)
    dma = lambda *shape: pltpu.SemaphoreType.DMA(shape)
    buffer = pltpu.VMEM
    return pl.pallas_call(
        functools.partial(kernel, planes, owners_in),
        out_shape=(jax.ShapeDtypeStruct((1, items), F32), jax.ShapeDtypeStruct((1, 1), F32)),
        in_specs=[vmem, pl.BlockSpec(memory_space=pl.ANY)],
        out_specs=(vmem, pl.BlockSpec(memory_space=pltpu.SMEM)),
        scratch_shapes=[
            buffer((items // BLOCK, BLOCK, width), BF16),
            buffer((items, part), BF16),
            buffer((8, items), jnp.int32),
            buffer((planes, Z_SLOTS, part), BF16),
            buffer((planes, Z_SLOTS, part), BF16),
            buffer((planes, 8, lanes), F32),
            buffer((planes, 8, lanes), F32),
            buffer((planes, lanes), F32),
            buffer((owners_in, planes, lanes), F32),
            buffer((planes, lanes, part), BF16),
            buffer((planes, lanes, part), BF16),
            buffer((owners_in * NEAR_SLOTS, part), BF16),
            buffer((lanes, part), BF16),
            buffer((CLU_OWN, CAP, part), BF16),
            buffer((4, total, BLOCK), F32),
            buffer((2, total // 2, BLOCK), F32),
            buffer((2, total // 2, BLOCK), F32),
            buffer((2, total // 2, BLOCK), F32),
            buffer((2, total // 2, BLOCK), F32),
            buffer((owners_in, 1, lanes), F32),
            buffer((4, owners_in, 1, lanes), F32),
            buffer((planes, 1, lanes), F32),
            buffer((planes, 1, lanes), F32),
            dma(items // BLOCK),
            dma(planes),
            dma(planes),
            dma(planes),
            dma(planes),
            dma(owners_in),
            dma(owners_in),
            dma(planes, owners_in),
            dma(planes, owners_in),
            dma(owners_in),
            dma(owners_in),
            dma(LATE + 1, 6),
            dma(LATE + 1, 6),
            dma(4, owners_in),
            dma(4, owners_in),
            dma(planes),
            dma(planes),
        ],
        compiler_params=pltpu.CompilerParams(
            collective_id=0, has_side_effects=True, vmem_limit_bytes=60 * 1024 * 1024
        ),
    )(cluster_ids.reshape(1, items), embeddings)


def pair_best(row_block, row_labels, columns, column_labels, column_start):
    scores = lax.dot_general(
        row_block, columns, (((1,), (1,)), ((), ())), preferred_element_type=jnp.float32
    )
    row_ident = jnp.arange(row_block.shape[0], dtype=jnp.int32)
    column_ident = column_start + jnp.arange(columns.shape[0], dtype=jnp.int32)
    in_cluster = (
        (row_labels[:, None] == column_labels[None, :])
        & (row_labels[:, None] >= 0)
        & (row_ident[:, None] != column_ident[None, :])
    )
    return jnp.max(jnp.where(in_cluster, scores, -1.0), axis=1)


def any_layout(embeddings, cluster_ids):
    prod_count = lax.axis_size("prod")
    tile_count = lax.axis_size("tile")
    item_dev = embeddings.shape[0]
    width = embeddings.shape[1]
    group_rows = prod_count * SLOTS
    widened = embeddings.astype(jnp.float32)
    normed = (
        widened * lax.rsqrt(jnp.sum(widened * widened, axis=1, keepdims=True) + 1e-06)
    ).astype(jnp.bfloat16)
    owners = cluster_ids // CLU_OWN
    owner_hot = (owners[:, None] == jnp.arange(prod_count, dtype=jnp.int32)[None, :]).astype(
        jnp.int32
    )
    running = jnp.cumsum(owner_hot, axis=0)
    slot_index = jnp.sum(running * owner_hot, axis=1) - 1
    position = owners * SLOTS + slot_index
    inverse = (
        jnp.full((group_rows,), item_dev, jnp.int32)
        .at[position]
        .set(jnp.arange(item_dev, dtype=jnp.int32))
    )
    padded = jnp.concatenate([normed, jnp.zeros((1, width), jnp.bfloat16)], axis=0)
    labels = jnp.concatenate([cluster_ids, jnp.full((1,), -1, jnp.int32)], axis=0)
    outgoing = padded[inverse].reshape(prod_count, SLOTS, width)
    out_labels = labels[inverse].reshape(prod_count, SLOTS)
    tile_pos = lax.axis_index("tile")
    row_block, row_labels = (
        lax.all_to_all(outgoing, "prod", split_axis=0, concat_axis=0, tiled=True),
        lax.all_to_all(out_labels, "prod", split_axis=0, concat_axis=0, tiled=True),
    )
    row_block = row_block.reshape(group_rows, width)
    row_labels = row_labels.reshape(group_rows)
    piece_rows = group_rows // tile_count
    row_start = tile_pos * piece_rows
    columns = lax.dynamic_slice_in_dim(row_block, row_start, piece_rows, 0)
    column_labels = lax.dynamic_slice_in_dim(row_labels, row_start, piece_rows, 0)
    partial_best = pair_best(row_block, row_labels, columns, column_labels, row_start)
    maxima = lax.pmax(partial_best, "tile")
    returned = lax.all_to_all(
        maxima.reshape(prod_count, -1), "prod", split_axis=0, concat_axis=0, tiled=True
    )
    return returned.reshape(group_rows)[position]


def shards(embeddings, cluster_ids):
    prod_count = lax.axis_size("prod")
    owners_in = 8 if prod_count >= 64 else 4
    planes = prod_count // owners_in
    part = embeddings.shape[1] // lax.axis_size("tile")
    best, mark = fast(planes, owners_in, embeddings, cluster_ids, part)
    fits = mark[0, 0] < TOO_MANY
    return lax.cond(
        fits,
        lambda e, i, b: b,
        lambda e, i, b: any_layout(e, i),
        embeddings,
        cluster_ids,
        best.reshape(-1),
    )


def solution(mesh):
    placed = (P("prod", None), P("prod"))
    return jax.shard_map(shards, mesh=mesh, in_specs=placed, out_specs=P("prod"), check_vma=False)
```

```python
import functools

import jax
import jax.numpy as jnp
from jax import lax
from jax.experimental import pallas as pl
from jax.experimental.pallas import tpu as pltpu
from jax.sharding import PartitionSpec as P

CLU_OWN = 8
SLOTS = 32
Z_SLOTS = 176
NEAR_SLOTS = SLOTS // 2
FAR_SLOTS = 48
BLOCK = 128
LATE = 3
FEW = 64
LAST = 48
MANY = 2 * BLOCK
CAP = MANY + LATE * FEW
STARTS = (0, MANY, MANY + FEW, MANY + 2 * FEW)
NEW = (0, FEW, FEW, LAST)
SCORE_ROWS = (4 * BLOCK, 5 * FEW, 6 * FEW, 7 * LAST)
TOO_MANY = 4.0 * CLU_OWN
F32 = jnp.float32
BF16 = jnp.bfloat16
MESH = pl.DeviceIdType.MESH
NN = (((1,), (0,)), ((), ()))
NT = (((1,), (1,)), ((), ()))


def dot(a, b, dims=NN, precision=None):
    return lax.dot_general(a, b, dims, preferred_element_type=F32, precision=precision)


def iota(shape, dim):
    return lax.broadcasted_iota(jnp.int32, shape, dim)


def hot(cond):
    return jnp.where(cond, 1.0, 0.0).astype(BF16)


def nearest_first(n):
    order = [0]
    for d in range(1, n // 2 + 1):
        order += [d] if 2 * d == n else [d, n - d]
    return order


def highest(score, limit):
    return jnp.max(jnp.where(limit, score, -1.0), axis=0, keepdims=True)


def most(a):
    return jnp.max(jnp.max(a, axis=1, keepdims=True), axis=0, keepdims=True)


def kernel(
    planes,
    owners_in,
    ids_ref,
    x_ref,
    out_ref,
    flag_ref,
    x_rows,
    unit,
    index,
    packed,
    z_rows,
    lids_own,
    z_lids,
    lids_out,
    x_lids,
    staged,
    rows,
    far_rows,
    last_rows,
    sorted_rows,
    partial,
    relay,
    near,
    far,
    forward,
    values_out,
    x_back,
    values_home,
    z_back,
    load_sem,
    z_send,
    z_recv,
    zl_send,
    zl_recv,
    xl_send,
    xl_recv,
    x_send,
    x_recv,
    far_send,
    far_recv,
    y_send,
    y_recv,
    xb_send,
    xb_recv,
    zb_send,
    zb_recv,
):
    lanes = owners_in * SLOTS
    owners = planes * owners_in
    items = ids_ref.shape[1]
    blocks, _, width = x_rows.shape
    part = unit.shape[1]
    me = lax.axis_index("prod")
    tile = lax.axis_index("tile")
    my_plane = me // owners_in
    my_col = lax.rem(me, owners_in)
    at_plane = lambda d: lax.rem(my_plane + d, planes)
    at_col = lambda k: lax.rem(my_col + k, owners_in)
    at_tile = lambda k: lax.rem(tile + k, 4)
    to_plane = lambda d: {"prod": at_plane(d) * owners_in + my_col}
    to_col = lambda k: {"prod": my_plane * owners_in + at_col(k)}
    to_tile = lambda k: {"tile": at_tile(k)}
    to_far = lambda k: {"prod": at_plane(far_plane) * owners_in + at_col(k)}
    to_both = lambda k, j: {"prod": my_plane * owners_in + at_col(k), "tile": at_tile(j)}
    order = nearest_first(planes)
    far_plane = order[-1]
    first_late = planes - LATE + 1
    started = []

    def send(src, dst, send_sem, recv_sem, device):
        copy = pltpu.make_async_remote_copy(
            src_ref=src,
            dst_ref=dst,
            send_sem=send_sem,
            recv_sem=recv_sem,
            device_id=device,
            device_id_type=MESH,
        )
        copy.start()
        started.append(copy)
        return copy

    loads = [
        pltpu.make_async_copy(
            x_ref.at[pl.ds(n * BLOCK, BLOCK)], x_rows.at[n], load_sem.at[n]
        )
        for n in range(blocks)
    ]
    for load in loads:
        load.start()

    for k in range(owners_in):
        blank = jnp.zeros((NEAR_SLOTS, part), BF16)
        rows[far_plane, k * SLOTS : k * SLOTS + NEAR_SLOTS, :] = blank
        last_rows[k * SLOTS + NEAR_SLOTS : (k + 1) * SLOTS, :] = blank

    barrier = pltpu.get_barrier_semaphore()
    for d in range(1, planes):
        pl.semaphore_signal(barrier, inc=1, device_id=to_plane(d), device_id_type=MESH)
    for k in range(1, owners_in):
        pl.semaphore_signal(barrier, inc=1, device_id=to_col(k), device_id_type=MESH)
    for k in range(1, 4):
        pl.semaphore_signal(barrier, inc=1, device_id=to_tile(k), device_id_type=MESH)

    ids = ids_ref[...]
    owner = ids // CLU_OWN
    plane = owner // owners_in
    lid = lax.rem(ids, CLU_OWN)
    owned = jnp.where(iota((owners, items), 0) == owner, 1.0, 0.0)
    before_block = hot(iota((BLOCK, BLOCK), 0) < iota((BLOCK, BLOCK), 1))
    count = jnp.zeros((owners, 1), F32)
    ahead = []
    for n in range(items // BLOCK):
        block = owned[:, n * BLOCK : (n + 1) * BLOCK]
        ahead.append(dot(block.astype(BF16), before_block) + count)
        count += jnp.sum(block, axis=1, keepdims=True)
    ahead = jnp.concatenate(ahead, axis=1)
    a, b = (iota((owners, owners), n) for n in (0, 1))
    lower = hot((a // owners_in == b // owners_in) & (b < a))
    offset = dot(lower, jnp.broadcast_to(count, (owners, BLOCK)).astype(BF16))[:, :1]
    slot = jnp.sum(owned * ahead, axis=0, keepdims=True).astype(jnp.int32)
    position = jnp.sum(owned * (ahead + offset), axis=0, keepdims=True).astype(jnp.int32)
    spill = jnp.broadcast_to(jnp.maximum(count - NEAR_SLOTS, 0.0), (owners, BLOCK)).astype(BF16)
    spill = jnp.sum(owned * dot(lower, spill)[:, :1], axis=0, keepdims=True).astype(jnp.int32)
    column = lax.rem(owner, owners_in)
    place = column * SLOTS + slot
    away = lax.rem(plane - my_plane + planes, planes)
    direct = jnp.where(slot < NEAR_SLOTS, column * NEAR_SLOTS + slot, -1)
    spilled = jnp.where(slot < NEAR_SLOTS, -1, spill + slot - NEAR_SLOTS)
    for n, line in enumerate((away, place, position, direct, spilled)):
        index[n : n + 1, :] = line
    room = (position < Z_SLOTS) & ((away != far_plane) | (spilled < FAR_SLOTS))
    crowded = jnp.max(jnp.where(room, 0.0, TOO_MANY), axis=1, keepdims=True)
    by_plane = jnp.where(iota((planes, items), 0) == plane, lid + 1, 0).astype(F32).astype(BF16)
    by_place = hot(iota((lanes, items), 0) == place)
    lids = dot(by_plane, by_place, NT)
    lids += crowded
    for z in range(planes):
        lids_own[z] = jnp.broadcast_to(lids[z : z + 1], lids_own.shape[1:])

    def unit_rows(n, carry):
        pltpu.make_async_copy(
            x_ref.at[pl.ds(pl.multiple_of(n * BLOCK, BLOCK), BLOCK)], x_rows.at[n], load_sem.at[n]
        ).wait()
        total = jnp.zeros((BLOCK, BLOCK), F32)
        for c in range(width // BLOCK):
            x = x_rows[n, :, c * BLOCK : (c + 1) * BLOCK].astype(F32)
            total += x * x
        scale = lax.rsqrt(jnp.sum(total, axis=1, keepdims=True) + 1e-06)
        mine = x_rows[n, :, pl.ds(pl.multiple_of(tile * part, part), part)].astype(F32)
        unit[pl.ds(pl.multiple_of(n * BLOCK, BLOCK), BLOCK), :] = (mine * scale).astype(BF16)
        return carry

    lax.fori_loop(0, blocks, unit_rows, 0)

    pl.semaphore_wait(barrier, planes - 1 + owners_in - 1 + 3)
    lid_copies = [
        send(lids_own.at[at_plane(d)], z_lids.at[d], zl_send.at[d], zl_recv.at[d], to_plane(d))
        for d in order[1:]
    ]
    row_copies = {}

    def chosen_rows(d, line, count):
        wanted = jnp.where(index[0:1, :] == d, index[line : line + 1, :], -1)
        return dot(hot(iota((count, items), 0) == wanted), unit[...]).astype(BF16)

    def pack_rows(d, line, count):
        packed[d, :count, :] = chosen_rows(d, line, count)

    def send_rows(d, count):
        at = pl.ds(0, count)
        row_copies[d] = send(
            packed.at[d, at], z_rows.at[d, at], z_send.at[d], z_recv.at[d], to_plane(d)
        )

    held = order[-LATE:-1]
    for n, d in enumerate(order[1:-LATE]):
        pack_rows(d, 2, Z_SLOTS)
        send_rows(d, Z_SLOTS)
        if n == 1:
            z_rows[0] = chosen_rows(0, 2, Z_SLOTS)
    if planes < 8:
        z_rows[0] = chosen_rows(0, 2, Z_SLOTS)
    pack_rows(far_plane, 4, FAR_SLOTS)
    send_rows(far_plane, FAR_SLOTS)
    for d in held:
        pack_rows(d, 2, Z_SLOTS)
    far_rows[...] = chosen_rows(far_plane, 3, owners_in * NEAR_SLOTS)

    def send_held():
        for d in held:
            send_rows(d, Z_SLOTS)

    last_copies = []

    def send_last():
        for k in range(owners_in):
            start = pl.multiple_of(at_col(k) * NEAR_SLOTS, NEAR_SLOTS)
            last_copies.append(
                send(
                    far_rows.at[pl.ds(start, NEAR_SLOTS)],
                    last_rows.at[pl.ds(k * SLOTS, NEAR_SLOTS)],
                    far_send.at[k],
                    far_recv.at[k],
                    to_far(k),
                )
            )

    for copy in lid_copies:
        copy.wait_recv()
    lids = jnp.concatenate(
        [lids_own[my_plane][0:1]] + [z_lids[d][0:1] for d in range(1, planes)], axis=0
    )
    lids_out[...] = pltpu.roll(lids, lax.rem(owners_in - my_col, owners_in) * SLOTS, 1)
    col_lid_copies = [
        send(lids_out, x_lids.at[k], xl_send.at[k], xl_recv.at[k], to_col(k))
        for k in range(1, owners_in)
    ]
    before = hot(iota((lanes, lanes), 0) < iota((lanes, lanes), 1))
    near_slot = lax.rem(iota((planes, lanes), 1), SLOTS) < NEAR_SLOTS
    last = near_slot & (iota((planes, lanes), 0) == far_plane)
    taken = (lids > 0.0) & jnp.logical_not(last)
    source = jnp.where(taken, dot(hot(taken), before), -1.0)
    source = jnp.concatenate([source, jnp.zeros((BLOCK - planes, lanes), F32)], axis=0).T

    def forward_rows(d):
        if d:
            row_copies[d].wait_recv()
        count, skip = (FAR_SLOTS, NEAR_SLOTS) if d == far_plane else (Z_SLOTS, 0)
        take = source[:, d : d + 1].astype(jnp.int32) == iota((lanes, count), 1)
        staged[d] = dot(hot(take), z_rows[d, :count, :]).astype(BF16)
        copies = []
        for k in range(owners_in):
            start = pl.multiple_of(at_col(k) * SLOTS + skip, NEAR_SLOTS)
            src = staged.at[d, pl.ds(start, SLOTS - skip)]
            dst = rows.at[d, pl.ds(k * SLOTS + skip, SLOTS - skip)]
            if k == 0:
                copy = pltpu.make_async_copy(src, dst, x_recv.at[d, 0])
                copy.start()
            else:
                copy = send(src, dst, x_send.at[d, k], x_recv.at[d, k], to_col(k))
            copies.append(copy)
        return copies

    steps = order[:-LATE] + [far_plane] + order[-LATE:-1]
    x_copies = {steps[0]: forward_rows(steps[0])}

    for copy in col_lid_copies:
        copy.wait_recv()
    got = jnp.zeros((planes, lanes), F32)
    marks = lids_out[...]
    group = iota((planes, lanes), 1) // SLOTS
    for k in range(owners_in):
        theirs = lids_out[...] if k == 0 else x_lids[k]
        got += jnp.where(group == k, theirs, 0.0)
        marks = jnp.maximum(marks, theirs)

    def set_of(d):
        which = jnp.zeros(d.shape, jnp.int32)
        for n in range(1, LATE):
            which = jnp.where(d == order[n - LATE - 1 + planes], n, which)
        return which

    other = jnp.where(last, 0.0, got)
    member = jnp.concatenate([hot(other == c + 1.0) for c in range(CLU_OWN)], axis=0)
    ending = jnp.where(near_slot, got, 0.0)[far_plane : far_plane + 1]
    ending = hot(ending == iota((CLU_OWN, lanes), 0).astype(F32) + 1.0)
    ending_rank = dot(ending, before)
    ending_size = dot(ending, jnp.ones((lanes, lanes), BF16))
    in_row = dot(member, before)
    in_rows = dot(member, jnp.ones((lanes, lanes), BF16)).astype(BF16)
    a, b = (iota((CLU_OWN * planes, CLU_OWN * planes), n) for n in (0, 1))
    same = (a // planes == b // planes) & (set_of(lax.rem(a, planes)) == set_of(lax.rem(b, planes)))
    rank_all = in_row + dot(hot(same & (b < a)), in_rows)
    a, b = (iota((CLU_OWN * LATE, CLU_OWN * planes), n) for n in (0, 1))
    same = (lax.rem(a, CLU_OWN) == b // planes) & (a // CLU_OWN == set_of(lax.rem(b, planes)))
    sizes = jnp.concatenate([dot(hot(same), in_rows), ending_size], axis=0)
    unfit = (
        (most(marks) >= TOO_MANY)
        | (most(sizes[:CLU_OWN]) > MANY)
        | (most(sizes[CLU_OWN:]) > FEW)
        | (most(sizes[CLU_OWN * LATE :]) > LAST)
    )
    ranked = jnp.zeros((planes, lanes), F32)
    for c in range(CLU_OWN):
        this = slice(c * planes, (c + 1) * planes)
        rank_here = jnp.where(last, ending_rank[c : c + 1], rank_all[this])
        ranked += jnp.where(got == c + 1.0, rank_here, 0.0)
    late = jnp.where(last, LATE, set_of(iota((planes, lanes), 0)))
    cluster = got.astype(jnp.int32) - 1
    ranked = ranked.astype(jnp.int32)
    target = jnp.where(cluster >= 0, cluster * jnp.where(late == 0, MANY, FEW) + ranked, -1)

    def place_few(n, goal, arrived):
        moved = dot(hot(iota((CLU_OWN * FEW, lanes), 0) == goal), arrived).astype(BF16)
        for c in range(CLU_OWN):
            sorted_rows[c, STARTS[n] : STARTS[n] + FEW, :] = moved[c * FEW : (c + 1) * FEW]

    def place_rows(n):
        d = steps[n]
        copies = x_copies[d]
        copies[0].wait()
        for copy in copies[1:]:
            copy.wait_recv()
        goal = jnp.where(last, -1, target)[d : d + 1]
        if n >= first_late:
            place_few(n - first_late + 1, goal, rows[d])
            return

        def body(c, carry):
            chosen = hot(iota((MANY, lanes), 0) + c * MANY == goal)
            moved = dot(chosen, rows[d]).astype(BF16)
            if n:
                sorted_rows[c, :MANY, :] = sorted_rows[c, :MANY, :] + moved
            else:
                sorted_rows[c, :MANY, :] = moved
            return carry

        lax.fori_loop(0, CLU_OWN, body, 0)

    r, c = (iota((BLOCK, BLOCK), n) for n in (0, 1))
    right, left, across = at_tile(1), at_tile(3), at_tile(2)
    spans = []
    for s, n in enumerate(SCORE_ROWS):
        spans.append((sum(SCORE_ROWS[:s]), n // 2))

    def scores(t, s):
        base = spans[s][0]
        if s == 0:
            for j in range(2):
                block = sorted_rows[2 * t + j, :MANY, :]
                all_pairs = dot(block, block, NT)
                at = base + 2 * j * BLOCK
                partial[t, at : at + BLOCK] = all_pairs[:BLOCK, BLOCK:]
                partial[t, at + BLOCK : at + 2 * BLOCK] = jnp.where(
                    c > r, all_pairs[:BLOCK, :BLOCK], all_pairs[BLOCK:, BLOCK:]
                )
            return
        start, stop, fresh = STARTS[s], STARTS[s] + FEW, NEW[s]
        full = stop // BLOCK
        ends = []
        for j in range(2):
            new = sorted_rows[2 * t + j, start : start + fresh, :]
            pairs = dot(new, sorted_rows[2 * t + j, : full * BLOCK, :], NT)
            for p in range(full):
                at = base + (2 * p + j) * fresh
                partial[t, at : at + fresh] = pairs[:, p * BLOCK : (p + 1) * BLOCK]
            if stop % BLOCK:
                ends.append(dot(new, sorted_rows[2 * t + j, start - FEW : stop, :], NT))
        if ends:
            at = base + 2 * full * fresh
            partial[t, at : at + fresh] = jnp.where(
                c[:fresh] < FEW, pltpu.roll(ends[0], FEW, 1), ends[1]
            )

    y_copies = {}

    def y_send_to(s, n, src, dst, step):
        y_copies[s, n] = send(src, dst, y_send.at[s, n], y_recv.at[s, n], to_tile(step))

    def begin_sum(s):
        base, half = spans[s]
        head, tail, at = pl.ds(base, half), pl.ds(base + half, half), pl.ds(base // 2, half)
        scores(across, s)
        y_send_to(s, 0, partial.at[across, head], relay.at[0, at], 1)
        y_send_to(s, 1, partial.at[across, tail], relay.at[1, at], 3)
        scores(right, s)
        y_send_to(s, 2, partial.at[right, tail], near.at[1, at], 1)
        scores(left, s)
        y_send_to(s, 3, partial.at[left, head], near.at[0, at], 3)
        scores(tile, s)

    def relay_sum(s):
        base, half = spans[s]
        at = pl.ds(base // 2, half)
        y_copies[s, 0].wait_recv()
        forward[0, at] = relay[0, at] + partial[right, pl.ds(base, half)]
        y_send_to(s, 4, forward.at[0, at], far.at[0, at], 1)
        y_copies[s, 1].wait_recv()
        forward[1, at] = relay[1, at] + partial[left, pl.ds(base + half, half)]
        y_send_to(s, 5, forward.at[1, at], far.at[1, at], 3)

    def end_sum(s):
        base, half = spans[s]
        at = pl.ds(base // 2, half)
        for n in range(2, 6):
            y_copies[s, n].wait_recv()
        return jnp.concatenate(
            [partial[tile, pl.ds(base + h * half, half)] + near[h, at] + far[h, at] for h in (0, 1)],
            axis=0,
        )

    size_row = iota((BLOCK, lanes), 0)[: CLU_OWN * (LATE + 1)]
    size = [
        [
            jnp.sum(
                jnp.where(size_row == s * CLU_OWN + 2 * tile + j, sizes, 0.0), axis=0, keepdims=True
            )[:, :BLOCK].astype(jnp.int32)
            for j in range(2)
        ]
        for s in range(LATE + 1)
    ]
    lane = iota((1, BLOCK), 1)
    size_both = [jnp.where(lane < FEW, a, b) for a, b in size]
    by_column = {}
    by_new = {}

    def raise_to(j, p, value):
        by_column[j, p] = jnp.maximum(by_column[j, p], value) if (j, p) in by_column else value

    def best_of(s):
        total = end_sum(s)
        if s == 0:
            above, below = c > r, c < r
            for j in range(2):
                cross = total[2 * j * BLOCK : (2 * j + 1) * BLOCK]
                fold = total[(2 * j + 1) * BLOCK : (2 * j + 2) * BLOCK]
                turned = fold.T
                low, high = r < size[0][j], r + BLOCK < size[0][j]
                raise_to(j, 0, highest(fold, low & above))
                raise_to(j, 0, highest(turned, low & below))
                raise_to(j, 0, highest(cross.T, high))
                raise_to(j, 1, highest(fold, high & below))
                raise_to(j, 1, highest(turned, high & above))
                raise_to(j, 1, highest(cross, low))
            return
        stop, fresh = STARTS[s] + FEW, NEW[s]
        full = stop // BLOCK
        row_few, col_few = r[:fresh], c[:fresh]
        news = []
        for p in range(full):
            halves = [total[(2 * p + j) * fresh : (2 * p + j + 1) * fresh] for j in range(2)]
            for j in range(2):
                limit = row_few < size[s][j]
                if (p + 1) * BLOCK == stop:
                    limit = limit & (col_few - FEW != row_few)
                raise_to(j, p, highest(halves[j], limit))
            if p < 2:
                earlier = r + p * BLOCK < size_both[0]
            else:
                earlier = (r < FEW) & (r < size_both[1])
                if s == 3:
                    earlier = earlier | ((r >= FEW) & (r - FEW < size_both[2]))
            if fresh < FEW:
                blank = jnp.zeros((FEW - fresh, BLOCK), F32)
                halves = [halves[0], blank, halves[1], blank]
            news.append(highest(jnp.concatenate(halves, axis=0).T, earlier))
        if stop % BLOCK:
            limit = (row_few < size_both[s]) & (row_few != lax.rem(col_few, FEW))
            news.append(highest(total[2 * full * fresh :], limit))
        by_new[s] = functools.reduce(jnp.maximum, news)

    for n in range(1, planes):
        x_copies[steps[n]] = forward_rows(steps[n])
        if n == planes // 4:
            send_held()
        if n == planes - 2:
            send_last()
        place_rows(n - 1)
        if n == first_late:
            begin_sum(0)
        elif n > first_late:
            begin_sum(n - first_late)
            relay_sum(n - first_late - 1)
    place_rows(planes - 1)
    begin_sum(LATE - 1)
    relay_sum(LATE - 2)
    best_of(0)
    for copy in last_copies:
        copy.wait_recv()
    place_few(LATE, jnp.where(last, target, -1)[far_plane : far_plane + 1], last_rows[...])
    begin_sum(LATE)
    relay_sum(LATE - 1)
    best_of(LATE - 2)
    relay_sum(LATE)
    best_of(LATE - 1)
    best_of(LATE)

    swap = lambda v: pltpu.roll(v, FEW, 1)
    low = lane < FEW
    raise_to(0, 2, jnp.where(low, by_new[1], swap(by_new[2])))
    raise_to(1, 2, jnp.where(low, swap(by_new[1]), by_new[2]))
    raise_to(0, 3, by_new[3])
    raise_to(1, 3, swap(by_new[3]))
    table = jnp.concatenate([by_column[j, p] for j in range(2) for p in range(4)], axis=0)
    table = jnp.concatenate([table, jnp.zeros((BLOCK - 8, BLOCK), F32)], axis=0).T

    where = ranked
    for s in range(1, LATE + 1):
        where = where + jnp.where(late == s, STARTS[s], 0)
    where_row = lax.rem(cluster + 2, 2) * 4 + where // BLOCK
    where_row = jnp.where((cluster >= 0) & (cluster // 2 == tile), where_row, -1)
    where_lane = lax.rem(where, BLOCK)
    picked = []
    for d in range(planes):
        values = jnp.zeros((BLOCK, lanes), F32)
        for n in range(8):
            values = jnp.where(where_row[d : d + 1] == n, table[:, n : n + 1], values)
        mask = iota((BLOCK, lanes), 0) == where_lane[d : d + 1]
        picked.append(jnp.sum(jnp.where(mask, values, 0.0), axis=0, keepdims=True))
    values = jnp.where(unfit, TOO_MANY, jnp.concatenate(picked, axis=0))

    def turn(v):
        shifted = [v] + [pltpu.roll(v, n * SLOTS, 1) for n in range(1, planes)]
        mine = iota(v.shape, 0) == group
        lines = []
        for b in range(planes):
            line = jnp.zeros(v.shape, F32)
            for a in range(planes):
                line = jnp.where(mine & (group == a), shifted[(a - b) % planes], line)
            lines.append(jnp.sum(line, axis=0, keepdims=True))
        return lines

    for k, line in enumerate(turn(values)):
        values_out[k] = line
    col_back = [
        send(
            values_out.at[k],
            x_back.at[j, k],
            xb_send.at[j, k],
            xb_recv.at[j, k],
            to_both(owners_in - k, j),
        )
        for k in range(owners_in)
        for j in range(4)
        if k or j
    ]
    for copy in col_back:
        copy.wait_recv()
    home = []
    for k in range(owners_in):
        parts = [x_back[j, k] if k or j else values_out[0] for j in range(4)]
        home.append(functools.reduce(jnp.add, parts))
    home = jnp.concatenate(turn(jnp.concatenate(home, axis=0)), axis=0)
    home = pltpu.roll(home, my_col * SLOTS, 1)
    for d in range(planes):
        values_home[d] = home[d : d + 1]
    plane_back = [
        send(
            values_home.at[d], z_back.at[d], zb_send.at[d], zb_recv.at[d], to_plane(planes - d)
        )
        for d in range(1, planes)
    ]
    for copy in plane_back:
        copy.wait_recv()
    mine = jnp.concatenate([values_home[0]] + [z_back[d] for d in range(1, planes)], axis=0)
    flag_ref[0, 0] = jnp.max(mine)
    mine = jnp.concatenate([mine, jnp.zeros((BLOCK - planes, lanes), F32)], axis=0).T
    values = jnp.zeros((lanes, items), F32)
    for d in range(planes):
        values = jnp.where(index[0:1, :] == d, mine[:, d : d + 1], values)
    mask = iota((lanes, items), 0) == index[1:2, :]
    out_ref[...] = jnp.sum(jnp.where(mask, values, 0.0), axis=0, keepdims=True)

    for copy in started:
        copy.wait_send()


def fast(planes, owners_in, embeddings, cluster_ids, part):
    items, width = embeddings.shape
    lanes = owners_in * SLOTS
    total = sum(SCORE_ROWS)
    vmem = pl.BlockSpec(memory_space=pltpu.VMEM)
    dma = lambda *shape: pltpu.SemaphoreType.DMA(shape)
    buffer = pltpu.VMEM
    return pl.pallas_call(
        functools.partial(kernel, planes, owners_in),
        out_shape=(jax.ShapeDtypeStruct((1, items), F32), jax.ShapeDtypeStruct((1, 1), F32)),
        in_specs=[vmem, pl.BlockSpec(memory_space=pl.ANY)],
        out_specs=(vmem, pl.BlockSpec(memory_space=pltpu.SMEM)),
        scratch_shapes=[
            buffer((items // BLOCK, BLOCK, width), BF16),
            buffer((items, part), BF16),
            buffer((8, items), jnp.int32),
            buffer((planes, Z_SLOTS, part), BF16),
            buffer((planes, Z_SLOTS, part), BF16),
            buffer((planes, 8, lanes), F32),
            buffer((planes, 8, lanes), F32),
            buffer((planes, lanes), F32),
            buffer((owners_in, planes, lanes), F32),
            buffer((planes, lanes, part), BF16),
            buffer((planes, lanes, part), BF16),
            buffer((owners_in * NEAR_SLOTS, part), BF16),
            buffer((lanes, part), BF16),
            buffer((CLU_OWN, CAP, part), BF16),
            buffer((4, total, BLOCK), F32),
            buffer((2, total // 2, BLOCK), F32),
            buffer((2, total // 2, BLOCK), F32),
            buffer((2, total // 2, BLOCK), F32),
            buffer((2, total // 2, BLOCK), F32),
            buffer((owners_in, 1, lanes), F32),
            buffer((4, owners_in, 1, lanes), F32),
            buffer((planes, 1, lanes), F32),
            buffer((planes, 1, lanes), F32),
            dma(items // BLOCK),
            dma(planes),
            dma(planes),
            dma(planes),
            dma(planes),
            dma(owners_in),
            dma(owners_in),
            dma(planes, owners_in),
            dma(planes, owners_in),
            dma(owners_in),
            dma(owners_in),
            dma(LATE + 1, 6),
            dma(LATE + 1, 6),
            dma(4, owners_in),
            dma(4, owners_in),
            dma(planes),
            dma(planes),
        ],
        compiler_params=pltpu.CompilerParams(
            collective_id=0, has_side_effects=True, vmem_limit_bytes=60 * 1024 * 1024
        ),
    )(cluster_ids.reshape(1, items), embeddings)


def pair_best(row_block, row_labels, columns, column_labels, column_start):
    scores = lax.dot_general(
        row_block, columns, (((1,), (1,)), ((), ())), preferred_element_type=jnp.float32
    )
    row_ident = jnp.arange(row_block.shape[0], dtype=jnp.int32)
    column_ident = column_start + jnp.arange(columns.shape[0], dtype=jnp.int32)
    in_cluster = (
        (row_labels[:, None] == column_labels[None, :])
        & (row_labels[:, None] >= 0)
        & (row_ident[:, None] != column_ident[None, :])
    )
    return jnp.max(jnp.where(in_cluster, scores, -1.0), axis=1)


def any_layout(embeddings, cluster_ids):
    prod_count = lax.axis_size("prod")
    tile_count = lax.axis_size("tile")
    item_dev = embeddings.shape[0]
    width = embeddings.shape[1]
    group_rows = prod_count * SLOTS
    widened = embeddings.astype(jnp.float32)
    normed = (
        widened * lax.rsqrt(jnp.sum(widened * widened, axis=1, keepdims=True) + 1e-06)
    ).astype(jnp.bfloat16)
    owners = cluster_ids // CLU_OWN
    owner_hot = (owners[:, None] == jnp.arange(prod_count, dtype=jnp.int32)[None, :]).astype(
        jnp.int32
    )
    running = jnp.cumsum(owner_hot, axis=0)
    slot_index = jnp.sum(running * owner_hot, axis=1) - 1
    position = owners * SLOTS + slot_index
    inverse = (
        jnp.full((group_rows,), item_dev, jnp.int32)
        .at[position]
        .set(jnp.arange(item_dev, dtype=jnp.int32))
    )
    padded = jnp.concatenate([normed, jnp.zeros((1, width), jnp.bfloat16)], axis=0)
    labels = jnp.concatenate([cluster_ids, jnp.full((1,), -1, jnp.int32)], axis=0)
    outgoing = padded[inverse].reshape(prod_count, SLOTS, width)
    out_labels = labels[inverse].reshape(prod_count, SLOTS)
    tile_pos = lax.axis_index("tile")
    row_block, row_labels = (
        lax.all_to_all(outgoing, "prod", split_axis=0, concat_axis=0, tiled=True),
        lax.all_to_all(out_labels, "prod", split_axis=0, concat_axis=0, tiled=True),
    )
    row_block = row_block.reshape(group_rows, width)
    row_labels = row_labels.reshape(group_rows)
    piece_rows = group_rows // tile_count
    row_start = tile_pos * piece_rows
    columns = lax.dynamic_slice_in_dim(row_block, row_start, piece_rows, 0)
    column_labels = lax.dynamic_slice_in_dim(row_labels, row_start, piece_rows, 0)
    partial_best = pair_best(row_block, row_labels, columns, column_labels, row_start)
    maxima = lax.pmax(partial_best, "tile")
    returned = lax.all_to_all(
        maxima.reshape(prod_count, -1), "prod", split_axis=0, concat_axis=0, tiled=True
    )
    return returned.reshape(group_rows)[position]


def shards(embeddings, cluster_ids):
    prod_count = lax.axis_size("prod")
    owners_in = 8 if prod_count >= 64 else 4
    planes = prod_count // owners_in
    part = embeddings.shape[1] // lax.axis_size("tile")
    best, mark = fast(planes, owners_in, embeddings, cluster_ids, part)
    fits = mark[0, 0] < TOO_MANY
    return lax.cond(
        fits,
        lambda e, i, b: b,
        lambda e, i, b: any_layout(e, i),
        embeddings,
        cluster_ids,
        best.reshape(-1),
    )


def solution(mesh):
    placed = (P("prod", None), P("prod"))
    return jax.shard_map(shards, mesh=mesh, in_specs=placed, out_specs=P("prod"), check_vma=False)
```

```python
import functools

import jax
import jax.numpy as jnp
from jax import lax
from jax.experimental import pallas as pl
from jax.experimental.pallas import tpu as pltpu
from jax.sharding import PartitionSpec as P

CLU_OWN = 8
SLOTS = 32
Z_SLOTS = 176
NEAR_SLOTS = SLOTS // 2
FAR_SLOTS = 48
BLOCK = 128
LATE = 3
FEW = 64
LAST = 48
MANY = 2 * BLOCK
CAP = MANY + LATE * FEW
STARTS = (0, MANY, MANY + FEW, MANY + 2 * FEW)
NEW = (0, FEW, FEW, LAST)
SCORE_ROWS = (4 * BLOCK, 5 * FEW, 6 * FEW, 7 * LAST)
TOO_MANY = 4.0 * CLU_OWN
F32 = jnp.float32
BF16 = jnp.bfloat16
MESH = pl.DeviceIdType.MESH
NN = (((1,), (0,)), ((), ()))
NT = (((1,), (1,)), ((), ()))


def dot(a, b, dims=NN, precision=None):
    return lax.dot_general(a, b, dims, preferred_element_type=F32, precision=precision)


def iota(shape, dim):
    return lax.broadcasted_iota(jnp.int32, shape, dim)


def hot(cond):
    return jnp.where(cond, 1.0, 0.0).astype(BF16)


def nearest_first(n):
    order = [0]
    for d in range(1, n // 2 + 1):
        order += [d] if 2 * d == n else [d, n - d]
    return order


def highest(score, limit):
    return jnp.max(jnp.where(limit, score, -1.0), axis=0, keepdims=True)


def most(a):
    return jnp.max(jnp.max(a, axis=1, keepdims=True), axis=0, keepdims=True)


def kernel(
    planes,
    owners_in,
    ids_ref,
    x_ref,
    out_ref,
    flag_ref,
    x_rows,
    unit,
    index,
    packed,
    z_rows,
    lids_own,
    z_lids,
    lids_out,
    x_lids,
    staged,
    rows,
    far_rows,
    last_rows,
    sorted_rows,
    partial,
    relay,
    near,
    far,
    forward,
    values_out,
    x_back,
    values_home,
    z_back,
    load_sem,
    z_send,
    z_recv,
    zl_send,
    zl_recv,
    xl_send,
    xl_recv,
    x_send,
    x_recv,
    far_send,
    far_recv,
    y_send,
    y_recv,
    xb_send,
    xb_recv,
    zb_send,
    zb_recv,
):
    lanes = owners_in * SLOTS
    owners = planes * owners_in
    items = ids_ref.shape[1]
    blocks, _, width = x_rows.shape
    part = unit.shape[1]
    me = lax.axis_index("prod")
    tile = lax.axis_index("tile")
    my_plane = me // owners_in
    my_col = lax.rem(me, owners_in)
    at_plane = lambda d: lax.rem(my_plane + d, planes)
    at_col = lambda k: lax.rem(my_col + k, owners_in)
    at_tile = lambda k: lax.rem(tile + k, 4)
    to_plane = lambda d: {"prod": at_plane(d) * owners_in + my_col}
    to_col = lambda k: {"prod": my_plane * owners_in + at_col(k)}
    to_tile = lambda k: {"tile": at_tile(k)}
    to_far = lambda k: {"prod": at_plane(far_plane) * owners_in + at_col(k)}
    to_both = lambda k, j: {"prod": my_plane * owners_in + at_col(k), "tile": at_tile(j)}
    order = nearest_first(planes)
    far_plane = order[-1]
    first_late = planes - LATE + 1
    started = []

    def drain(ref, sem):
        pltpu.make_async_copy(ref, ref, sem).wait()

    def send(src, dst, send_sem, recv_sem, device, alone=False):
        copy = pltpu.make_async_remote_copy(
            src_ref=src,
            dst_ref=dst,
            send_sem=send_sem,
            recv_sem=recv_sem,
            device_id=device,
            device_id_type=MESH,
        )
        copy.start()
        if alone:
            started.append(copy)
        return copy

    barrier = pltpu.get_barrier_semaphore()
    for d in range(1, planes):
        pl.semaphore_signal(barrier, inc=1, device_id=to_plane(d), device_id_type=MESH)
    for k in range(1, owners_in):
        pl.semaphore_signal(barrier, inc=1, device_id=to_col(k), device_id_type=MESH)
    for k in range(1, 4):
        pl.semaphore_signal(barrier, inc=1, device_id=to_tile(k), device_id_type=MESH)

    loads = [
        pltpu.make_async_copy(
            x_ref.at[pl.ds(n * BLOCK, BLOCK)], x_rows.at[n], load_sem.at[n]
        )
        for n in range(blocks)
    ]
    for load in loads:
        load.start()

    for k in range(owners_in):
        blank = jnp.zeros((NEAR_SLOTS, part), BF16)
        rows[far_plane, k * SLOTS : k * SLOTS + NEAR_SLOTS, :] = blank
        last_rows[k * SLOTS + NEAR_SLOTS : (k + 1) * SLOTS, :] = blank

    ids = ids_ref[...]
    owner = ids // CLU_OWN
    plane = owner // owners_in
    lid = lax.rem(ids, CLU_OWN)
    owned = jnp.where(iota((owners, items), 0) == owner, 1.0, 0.0)
    before_block = hot(iota((BLOCK, BLOCK), 0) < iota((BLOCK, BLOCK), 1))
    count = jnp.zeros((owners, 1), F32)
    ahead = []
    for n in range(items // BLOCK):
        block = owned[:, n * BLOCK : (n + 1) * BLOCK]
        ahead.append(dot(block.astype(BF16), before_block) + count)
        count += jnp.sum(block, axis=1, keepdims=True)
    ahead = jnp.concatenate(ahead, axis=1)
    a, b = (iota((owners, owners), n) for n in (0, 1))
    lower = hot((a // owners_in == b // owners_in) & (b < a))
    offset = dot(lower, jnp.broadcast_to(count, (owners, BLOCK)).astype(BF16))[:, :1]
    slot = jnp.sum(owned * ahead, axis=0, keepdims=True).astype(jnp.int32)
    position = jnp.sum(owned * (ahead + offset), axis=0, keepdims=True).astype(jnp.int32)
    spill = jnp.broadcast_to(jnp.maximum(count - NEAR_SLOTS, 0.0), (owners, BLOCK)).astype(BF16)
    spill = jnp.sum(owned * dot(lower, spill)[:, :1], axis=0, keepdims=True).astype(jnp.int32)
    column = lax.rem(owner, owners_in)
    place = column * SLOTS + slot
    away = lax.rem(plane - my_plane + planes, planes)
    direct = jnp.where(slot < NEAR_SLOTS, column * NEAR_SLOTS + slot, -1)
    spilled = jnp.where(slot < NEAR_SLOTS, -1, spill + slot - NEAR_SLOTS)
    for n, line in enumerate((away, place, position, direct, spilled)):
        index[n : n + 1, :] = line
    room = (position < Z_SLOTS) & ((away != far_plane) | (spilled < FAR_SLOTS))
    crowded = jnp.max(jnp.where(room, 0.0, TOO_MANY), axis=1, keepdims=True)
    by_plane = jnp.where(iota((planes, items), 0) == plane, lid + 1, 0).astype(F32).astype(BF16)
    by_place = hot(iota((lanes, items), 0) == place)
    lids = dot(by_plane, by_place, NT)
    lids += crowded
    for z in range(planes):
        lids_own[z] = jnp.broadcast_to(lids[z : z + 1], lids_own.shape[1:])

    def unit_rows(n, carry):
        pltpu.make_async_copy(
            x_ref.at[pl.ds(pl.multiple_of(n * BLOCK, BLOCK), BLOCK)], x_rows.at[n], load_sem.at[n]
        ).wait()
        total = jnp.zeros((BLOCK, BLOCK), F32)
        for c in range(width // BLOCK):
            x = x_rows[n, :, c * BLOCK : (c + 1) * BLOCK].astype(F32)
            total += x * x
        scale = lax.rsqrt(jnp.sum(total, axis=1, keepdims=True) + 1e-06)
        mine = x_rows[n, :, pl.ds(pl.multiple_of(tile * part, part), part)].astype(F32)
        unit[pl.ds(pl.multiple_of(n * BLOCK, BLOCK), BLOCK), :] = (mine * scale).astype(BF16)
        return carry

    lax.fori_loop(0, blocks, unit_rows, 0)

    pl.semaphore_wait(barrier, planes - 1 + owners_in - 1 + 3)
    for d in order[1:]:
        send(lids_own.at[at_plane(d)], z_lids.at[d], zl_send, zl_recv, to_plane(d))
    row_copies = {}

    def chosen_rows(d, line, count):
        wanted = jnp.where(index[0:1, :] == d, index[line : line + 1, :], -1)
        return dot(hot(iota((count, items), 0) == wanted), unit[...]).astype(BF16)

    def pack_rows(d, line, count):
        packed[d, :count, :] = chosen_rows(d, line, count)

    def send_rows(d, count):
        at = pl.ds(0, count)
        row_copies[d] = send(
            packed.at[d, at], z_rows.at[d, at], z_send.at[d], z_recv.at[d], to_plane(d), True
        )

    held = order[-LATE:-1]
    for n, d in enumerate(order[1:-LATE]):
        pack_rows(d, 2, Z_SLOTS)
        send_rows(d, Z_SLOTS)
        if n == 1:
            z_rows[0] = chosen_rows(0, 2, Z_SLOTS)
    if planes < 8:
        z_rows[0] = chosen_rows(0, 2, Z_SLOTS)
    pack_rows(far_plane, 4, FAR_SLOTS)
    send_rows(far_plane, FAR_SLOTS)
    for d in held:
        pack_rows(d, 2, Z_SLOTS)
    far_rows[...] = chosen_rows(far_plane, 3, owners_in * NEAR_SLOTS)

    def send_held():
        for d in held:
            send_rows(d, Z_SLOTS)

    def send_last():
        for k in range(owners_in):
            start = pl.multiple_of(at_col(k) * NEAR_SLOTS, NEAR_SLOTS)
            send(
                far_rows.at[pl.ds(start, NEAR_SLOTS)],
                last_rows.at[pl.ds(k * SLOTS, NEAR_SLOTS)],
                far_send,
                far_recv,
                to_far(k),
            )

    drain(z_lids.at[pl.ds(1, planes - 1)], zl_recv)
    lids = jnp.concatenate(
        [lids_own[my_plane][0:1]] + [z_lids[d][0:1] for d in range(1, planes)], axis=0
    )
    lids_out[...] = pltpu.roll(lids, lax.rem(owners_in - my_col, owners_in) * SLOTS, 1)
    for k in range(1, owners_in):
        send(lids_out, x_lids.at[k], xl_send, xl_recv, to_col(k))
    before = hot(iota((lanes, lanes), 0) < iota((lanes, lanes), 1))
    near_slot = lax.rem(iota((planes, lanes), 1), SLOTS) < NEAR_SLOTS
    last = near_slot & (iota((planes, lanes), 0) == far_plane)
    taken = (lids > 0.0) & jnp.logical_not(last)
    source = jnp.where(taken, dot(hot(taken), before), -1.0)
    source = jnp.concatenate([source, jnp.zeros((BLOCK - planes, lanes), F32)], axis=0).T

    def others(d):
        return pl.ds(0, (owners_in - 1) * (NEAR_SLOTS if d == far_plane else SLOTS))

    def forward_rows(d):
        if d:
            row_copies[d].wait_recv()
        count, skip = (FAR_SLOTS, NEAR_SLOTS) if d == far_plane else (Z_SLOTS, 0)
        take = source[:, d : d + 1].astype(jnp.int32) == iota((lanes, count), 1)
        staged[d] = dot(hot(take), z_rows[d, :count, :]).astype(BF16)
        for k in range(owners_in):
            start = pl.multiple_of(at_col(k) * SLOTS + skip, NEAR_SLOTS)
            src = staged.at[d, pl.ds(start, SLOTS - skip)]
            dst = rows.at[d, pl.ds(k * SLOTS + skip, SLOTS - skip)]
            if k:
                send(src, dst, x_send.at[d], x_recv.at[d], to_col(k))
            else:
                rows[d, skip:SLOTS, :] = staged[d, pl.ds(start, SLOTS - skip), :]

    steps = order[:-LATE] + [far_plane] + order[-LATE:-1]
    forward_rows(steps[0])

    drain(x_lids.at[pl.ds(1, owners_in - 1)], xl_recv)
    got = jnp.zeros((planes, lanes), F32)
    marks = lids_out[...]
    group = iota((planes, lanes), 1) // SLOTS
    for k in range(owners_in):
        theirs = lids_out[...] if k == 0 else x_lids[k]
        got += jnp.where(group == k, theirs, 0.0)
        marks = jnp.maximum(marks, theirs)

    def set_of(d):
        which = jnp.zeros(d.shape, jnp.int32)
        for n in range(1, LATE):
            which = jnp.where(d == order[n - LATE - 1 + planes], n, which)
        return which

    other = jnp.where(last, 0.0, got)
    member = jnp.concatenate([hot(other == c + 1.0) for c in range(CLU_OWN)], axis=0)
    ending = jnp.where(near_slot, got, 0.0)[far_plane : far_plane + 1]
    ending = hot(ending == iota((CLU_OWN, lanes), 0).astype(F32) + 1.0)
    ending_rank = dot(ending, before)
    ending_size = dot(ending, jnp.ones((lanes, lanes), BF16))
    in_row = dot(member, before)
    in_rows = dot(member, jnp.ones((lanes, lanes), BF16)).astype(BF16)
    a, b = (iota((CLU_OWN * planes, CLU_OWN * planes), n) for n in (0, 1))
    same = (a // planes == b // planes) & (set_of(lax.rem(a, planes)) == set_of(lax.rem(b, planes)))
    rank_all = in_row + dot(hot(same & (b < a)), in_rows)
    a, b = (iota((CLU_OWN * LATE, CLU_OWN * planes), n) for n in (0, 1))
    same = (lax.rem(a, CLU_OWN) == b // planes) & (a // CLU_OWN == set_of(lax.rem(b, planes)))
    sizes = jnp.concatenate([dot(hot(same), in_rows), ending_size], axis=0)
    unfit = (
        (most(marks) >= TOO_MANY)
        | (most(sizes[:CLU_OWN]) > MANY)
        | (most(sizes[CLU_OWN:]) > FEW)
        | (most(sizes[CLU_OWN * LATE :]) > LAST)
    )
    ranked = jnp.zeros((planes, lanes), F32)
    for c in range(CLU_OWN):
        this = slice(c * planes, (c + 1) * planes)
        rank_here = jnp.where(last, ending_rank[c : c + 1], rank_all[this])
        ranked += jnp.where(got == c + 1.0, rank_here, 0.0)
    late = jnp.where(last, LATE, set_of(iota((planes, lanes), 0)))
    cluster = got.astype(jnp.int32) - 1
    ranked = ranked.astype(jnp.int32)
    target = jnp.where(cluster >= 0, cluster * jnp.where(late == 0, MANY, FEW) + ranked, -1)

    def place_few(n, goal, arrived):
        moved = dot(hot(iota((CLU_OWN * FEW, lanes), 0) == goal), arrived).astype(BF16)
        for c in range(CLU_OWN):
            sorted_rows[c, STARTS[n] : STARTS[n] + FEW, :] = moved[c * FEW : (c + 1) * FEW]

    def place_rows(n):
        d = steps[n]
        drain(rows.at[d, others(d)], x_recv.at[d])
        goal = jnp.where(last, -1, target)[d : d + 1]
        if n >= first_late:
            place_few(n - first_late + 1, goal, rows[d])
            return

        def body(c, carry):
            chosen = hot(iota((MANY, lanes), 0) + c * MANY == goal)
            moved = dot(chosen, rows[d]).astype(BF16)
            if n:
                sorted_rows[c, :MANY, :] = sorted_rows[c, :MANY, :] + moved
            else:
                sorted_rows[c, :MANY, :] = moved
            return carry

        lax.fori_loop(0, CLU_OWN, body, 0)

    r, c = (iota((BLOCK, BLOCK), n) for n in (0, 1))
    right, left, across = at_tile(1), at_tile(3), at_tile(2)
    spans = []
    for s, n in enumerate(SCORE_ROWS):
        spans.append((sum(SCORE_ROWS[:s]), n // 2))

    def scores(t, s):
        base = spans[s][0]
        if s == 0:
            for j in range(2):
                block = sorted_rows[2 * t + j, :MANY, :]
                all_pairs = dot(block, block, NT)
                at = base + 2 * j * BLOCK
                partial[t, at : at + BLOCK] = all_pairs[:BLOCK, BLOCK:]
                partial[t, at + BLOCK : at + 2 * BLOCK] = jnp.where(
                    c > r, all_pairs[:BLOCK, :BLOCK], all_pairs[BLOCK:, BLOCK:]
                )
            return
        start, stop, fresh = STARTS[s], STARTS[s] + FEW, NEW[s]
        full = stop // BLOCK
        ends = []
        for j in range(2):
            new = sorted_rows[2 * t + j, start : start + fresh, :]
            pairs = dot(new, sorted_rows[2 * t + j, : full * BLOCK, :], NT)
            for p in range(full):
                at = base + (2 * p + j) * fresh
                partial[t, at : at + fresh] = pairs[:, p * BLOCK : (p + 1) * BLOCK]
            if stop % BLOCK:
                ends.append(dot(new, sorted_rows[2 * t + j, start - FEW : stop, :], NT))
        if ends:
            at = base + 2 * full * fresh
            partial[t, at : at + fresh] = jnp.where(
                c[:fresh] < FEW, pltpu.roll(ends[0], FEW, 1), ends[1]
            )

    y_copies = {}

    def y_send_to(s, n, src, dst, step):
        y_copies[s, n] = send(src, dst, y_send, y_recv.at[s, n], to_tile(step))

    def begin_sum(s):
        base, half = spans[s]
        head, tail, at = pl.ds(base, half), pl.ds(base + half, half), pl.ds(base // 2, half)
        scores(across, s)
        y_send_to(s, 0, partial.at[across, head], relay.at[0, at], 1)
        y_send_to(s, 1, partial.at[across, tail], relay.at[1, at], 3)
        scores(right, s)
        y_send_to(s, 2, partial.at[right, tail], near.at[1, at], 1)
        scores(left, s)
        y_send_to(s, 3, partial.at[left, head], near.at[0, at], 3)
        scores(tile, s)

    def relay_sum(s):
        base, half = spans[s]
        at = pl.ds(base // 2, half)
        y_copies[s, 0].wait_recv()
        forward[0, at] = relay[0, at] + partial[right, pl.ds(base, half)]
        y_send_to(s, 4, forward.at[0, at], far.at[0, at], 1)
        y_copies[s, 1].wait_recv()
        forward[1, at] = relay[1, at] + partial[left, pl.ds(base + half, half)]
        y_send_to(s, 5, forward.at[1, at], far.at[1, at], 3)

    def end_sum(s):
        base, half = spans[s]
        at = pl.ds(base // 2, half)
        for n in range(2, 6):
            y_copies[s, n].wait_recv()
        return jnp.concatenate(
            [partial[tile, pl.ds(base + h * half, half)] + near[h, at] + far[h, at] for h in (0, 1)],
            axis=0,
        )

    size_row = iota((BLOCK, lanes), 0)[: CLU_OWN * (LATE + 1)]
    size = [
        [
            jnp.sum(
                jnp.where(size_row == s * CLU_OWN + 2 * tile + j, sizes, 0.0), axis=0, keepdims=True
            )[:, :BLOCK].astype(jnp.int32)
            for j in range(2)
        ]
        for s in range(LATE + 1)
    ]
    lane = iota((1, BLOCK), 1)
    size_both = [jnp.where(lane < FEW, a, b) for a, b in size]
    by_column = {}
    by_new = {}

    def raise_to(j, p, value):
        by_column[j, p] = jnp.maximum(by_column[j, p], value) if (j, p) in by_column else value

    def best_of(s):
        total = end_sum(s)
        if s == 0:
            above, below = c > r, c < r
            for j in range(2):
                cross = total[2 * j * BLOCK : (2 * j + 1) * BLOCK]
                fold = total[(2 * j + 1) * BLOCK : (2 * j + 2) * BLOCK]
                turned = fold.T
                low, high = r < size[0][j], r + BLOCK < size[0][j]
                raise_to(j, 0, highest(fold, low & above))
                raise_to(j, 0, highest(turned, low & below))
                raise_to(j, 0, highest(cross.T, high))
                raise_to(j, 1, highest(fold, high & below))
                raise_to(j, 1, highest(turned, high & above))
                raise_to(j, 1, highest(cross, low))
            return
        stop, fresh = STARTS[s] + FEW, NEW[s]
        full = stop // BLOCK
        row_few, col_few = r[:fresh], c[:fresh]
        news = []
        for p in range(full):
            halves = [total[(2 * p + j) * fresh : (2 * p + j + 1) * fresh] for j in range(2)]
            for j in range(2):
                limit = row_few < size[s][j]
                if (p + 1) * BLOCK == stop:
                    limit = limit & (col_few - FEW != row_few)
                raise_to(j, p, highest(halves[j], limit))
            if p < 2:
                earlier = r + p * BLOCK < size_both[0]
            else:
                earlier = (r < FEW) & (r < size_both[1])
                if s == 3:
                    earlier = earlier | ((r >= FEW) & (r - FEW < size_both[2]))
            if fresh < FEW:
                blank = jnp.zeros((FEW - fresh, BLOCK), F32)
                halves = [halves[0], blank, halves[1], blank]
            news.append(highest(jnp.concatenate(halves, axis=0).T, earlier))
        if stop % BLOCK:
            limit = (row_few < size_both[s]) & (row_few != lax.rem(col_few, FEW))
            news.append(highest(total[2 * full * fresh :], limit))
        by_new[s] = functools.reduce(jnp.maximum, news)

    for n in range(1, planes):
        forward_rows(steps[n])
        if n == planes // 4:
            send_held()
        if n == planes - 2:
            send_last()
        place_rows(n - 1)
        if n == first_late:
            begin_sum(0)
        elif n > first_late:
            begin_sum(n - first_late)
            relay_sum(n - first_late - 1)
    place_rows(planes - 1)
    begin_sum(LATE - 1)
    relay_sum(LATE - 2)
    best_of(0)
    drain(last_rows.at[pl.ds(0, owners_in * NEAR_SLOTS)], far_recv)
    place_few(LATE, jnp.where(last, target, -1)[far_plane : far_plane + 1], last_rows[...])
    begin_sum(LATE)
    relay_sum(LATE - 1)
    best_of(LATE - 2)
    relay_sum(LATE)
    best_of(LATE - 1)
    best_of(LATE)

    swap = lambda v: pltpu.roll(v, FEW, 1)
    low = lane < FEW
    raise_to(0, 2, jnp.where(low, by_new[1], swap(by_new[2])))
    raise_to(1, 2, jnp.where(low, swap(by_new[1]), by_new[2]))
    raise_to(0, 3, by_new[3])
    raise_to(1, 3, swap(by_new[3]))
    table = jnp.concatenate([by_column[j, p] for j in range(2) for p in range(4)], axis=0)
    table = jnp.concatenate([table, jnp.zeros((BLOCK - 8, BLOCK), F32)], axis=0).T

    where = ranked
    for s in range(1, LATE + 1):
        where = where + jnp.where(late == s, STARTS[s], 0)
    where_row = lax.rem(cluster + 2, 2) * 4 + where // BLOCK
    where_row = jnp.where((cluster >= 0) & (cluster // 2 == tile), where_row, -1)
    where_lane = lax.rem(where, BLOCK)
    picked = []
    for d in range(planes):
        values = jnp.zeros((BLOCK, lanes), F32)
        for n in range(8):
            values = jnp.where(where_row[d : d + 1] == n, table[:, n : n + 1], values)
        mask = iota((BLOCK, lanes), 0) == where_lane[d : d + 1]
        picked.append(jnp.sum(jnp.where(mask, values, 0.0), axis=0, keepdims=True))
    values = jnp.where(unfit, TOO_MANY, jnp.concatenate(picked, axis=0))

    def turn(v):
        shifted = [v] + [pltpu.roll(v, n * SLOTS, 1) for n in range(1, planes)]
        mine = iota(v.shape, 0) == group
        lines = []
        for b in range(planes):
            line = jnp.zeros(v.shape, F32)
            for a in range(planes):
                line = jnp.where(mine & (group == a), shifted[(a - b) % planes], line)
            lines.append(jnp.sum(line, axis=0, keepdims=True))
        return lines

    for k, line in enumerate(turn(values)):
        values_out[k] = line
    for k in range(owners_in):
        for j in range(4):
            if k or j:
                dst = x_back.at[j * owners_in + k]
                send(values_out.at[k], dst, xb_send, xb_recv, to_both(owners_in - k, j))
    drain(x_back.at[pl.ds(1, 4 * owners_in - 1)], xb_recv)
    home = []
    for k in range(owners_in):
        parts = [x_back[j * owners_in + k] if k or j else values_out[0] for j in range(4)]
        home.append(functools.reduce(jnp.add, parts))
    home = jnp.concatenate(turn(jnp.concatenate(home, axis=0)), axis=0)
    home = pltpu.roll(home, my_col * SLOTS, 1)
    for d in range(planes):
        values_home[d] = home[d : d + 1]
    for d in range(1, planes):
        send(values_home.at[d], z_back.at[d], zb_send, zb_recv, to_plane(planes - d))
    drain(z_back.at[pl.ds(1, planes - 1)], zb_recv)
    mine = jnp.concatenate([values_home[0]] + [z_back[d] for d in range(1, planes)], axis=0)
    flag_ref[0, 0] = jnp.max(mine)
    mine = jnp.concatenate([mine, jnp.zeros((BLOCK - planes, lanes), F32)], axis=0).T
    values = jnp.zeros((lanes, items), F32)
    for d in range(planes):
        values = jnp.where(index[0:1, :] == d, mine[:, d : d + 1], values)
    mask = iota((lanes, items), 0) == index[1:2, :]
    out_ref[...] = jnp.sum(jnp.where(mask, values, 0.0), axis=0, keepdims=True)

    for copy in started:
        copy.wait_send()
    for d in order:
        drain(staged.at[d, others(d)], x_send.at[d])
    drain(far_rows, far_send)
    drain(partial.at[pl.ds(0, 3)], y_send)
    drain(z_lids.at[pl.ds(1, planes - 1)], zl_send)
    drain(x_lids.at[pl.ds(1, owners_in - 1)], xl_send)
    drain(x_back.at[pl.ds(1, 4 * owners_in - 1)], xb_send)
    drain(z_back.at[pl.ds(1, planes - 1)], zb_send)


def fast(planes, owners_in, embeddings, cluster_ids, part):
    items, width = embeddings.shape
    lanes = owners_in * SLOTS
    total = sum(SCORE_ROWS)
    vmem = pl.BlockSpec(memory_space=pltpu.VMEM)
    one = pltpu.SemaphoreType.DMA
    dma = lambda *shape: one(shape)
    buffer = pltpu.VMEM
    return pl.pallas_call(
        functools.partial(kernel, planes, owners_in),
        out_shape=(jax.ShapeDtypeStruct((1, items), F32), jax.ShapeDtypeStruct((1, 1), F32)),
        in_specs=[vmem, pl.BlockSpec(memory_space=pl.ANY)],
        out_specs=(vmem, pl.BlockSpec(memory_space=pltpu.SMEM)),
        scratch_shapes=[
            buffer((items // BLOCK, BLOCK, width), BF16),
            buffer((items, part), BF16),
            buffer((8, items), jnp.int32),
            buffer((planes, Z_SLOTS, part), BF16),
            buffer((planes, Z_SLOTS, part), BF16),
            buffer((planes, 8, lanes), F32),
            buffer((planes, 8, lanes), F32),
            buffer((planes, lanes), F32),
            buffer((owners_in, planes, lanes), F32),
            buffer((planes, lanes, part), BF16),
            buffer((planes, lanes, part), BF16),
            buffer((owners_in * NEAR_SLOTS, part), BF16),
            buffer((lanes, part), BF16),
            buffer((CLU_OWN, CAP, part), BF16),
            buffer((4, total, BLOCK), F32),
            buffer((2, total // 2, BLOCK), F32),
            buffer((2, total // 2, BLOCK), F32),
            buffer((2, total // 2, BLOCK), F32),
            buffer((2, total // 2, BLOCK), F32),
            buffer((owners_in, 1, lanes), F32),
            buffer((4 * owners_in, 1, lanes), F32),
            buffer((planes, 1, lanes), F32),
            buffer((planes, 1, lanes), F32),
            dma(items // BLOCK),
            dma(planes),
            dma(planes),
            one,
            one,
            one,
            one,
            dma(planes),
            dma(planes),
            one,
            one,
            one,
            dma(LATE + 1, 6),
            one,
            one,
            one,
            one,
        ],
        compiler_params=pltpu.CompilerParams(
            collective_id=0, has_side_effects=True, vmem_limit_bytes=60 * 1024 * 1024
        ),
    )(cluster_ids.reshape(1, items), embeddings)


def pair_best(row_block, row_labels, columns, column_labels, column_start):
    scores = lax.dot_general(
        row_block, columns, (((1,), (1,)), ((), ())), preferred_element_type=jnp.float32
    )
    row_ident = jnp.arange(row_block.shape[0], dtype=jnp.int32)
    column_ident = column_start + jnp.arange(columns.shape[0], dtype=jnp.int32)
    in_cluster = (
        (row_labels[:, None] == column_labels[None, :])
        & (row_labels[:, None] >= 0)
        & (row_ident[:, None] != column_ident[None, :])
    )
    return jnp.max(jnp.where(in_cluster, scores, -1.0), axis=1)


def any_layout(embeddings, cluster_ids):
    prod_count = lax.axis_size("prod")
    tile_count = lax.axis_size("tile")
    item_dev = embeddings.shape[0]
    width = embeddings.shape[1]
    group_rows = prod_count * SLOTS
    widened = embeddings.astype(jnp.float32)
    normed = (
        widened * lax.rsqrt(jnp.sum(widened * widened, axis=1, keepdims=True) + 1e-06)
    ).astype(jnp.bfloat16)
    owners = cluster_ids // CLU_OWN
    owner_hot = (owners[:, None] == jnp.arange(prod_count, dtype=jnp.int32)[None, :]).astype(
        jnp.int32
    )
    running = jnp.cumsum(owner_hot, axis=0)
    slot_index = jnp.sum(running * owner_hot, axis=1) - 1
    position = owners * SLOTS + slot_index
    inverse = (
        jnp.full((group_rows,), item_dev, jnp.int32)
        .at[position]
        .set(jnp.arange(item_dev, dtype=jnp.int32))
    )
    padded = jnp.concatenate([normed, jnp.zeros((1, width), jnp.bfloat16)], axis=0)
    labels = jnp.concatenate([cluster_ids, jnp.full((1,), -1, jnp.int32)], axis=0)
    outgoing = padded[inverse].reshape(prod_count, SLOTS, width)
    out_labels = labels[inverse].reshape(prod_count, SLOTS)
    tile_pos = lax.axis_index("tile")
    row_block, row_labels = (
        lax.all_to_all(outgoing, "prod", split_axis=0, concat_axis=0, tiled=True),
        lax.all_to_all(out_labels, "prod", split_axis=0, concat_axis=0, tiled=True),
    )
    row_block = row_block.reshape(group_rows, width)
    row_labels = row_labels.reshape(group_rows)
    piece_rows = group_rows // tile_count
    row_start = tile_pos * piece_rows
    columns = lax.dynamic_slice_in_dim(row_block, row_start, piece_rows, 0)
    column_labels = lax.dynamic_slice_in_dim(row_labels, row_start, piece_rows, 0)
    partial_best = pair_best(row_block, row_labels, columns, column_labels, row_start)
    maxima = lax.pmax(partial_best, "tile")
    returned = lax.all_to_all(
        maxima.reshape(prod_count, -1), "prod", split_axis=0, concat_axis=0, tiled=True
    )
    return returned.reshape(group_rows)[position]


def shards(embeddings, cluster_ids):
    prod_count = lax.axis_size("prod")
    owners_in = 8 if prod_count >= 64 else 4
    planes = prod_count // owners_in
    part = embeddings.shape[1] // lax.axis_size("tile")
    best, mark = fast(planes, owners_in, embeddings, cluster_ids, part)
    fits = mark[0, 0] < TOO_MANY
    return lax.cond(
        fits,
        lambda e, i, b: b,
        lambda e, i, b: any_layout(e, i),
        embeddings,
        cluster_ids,
        best.reshape(-1),
    )


def solution(mesh):
    placed = (P("prod", None), P("prod"))
    return jax.shard_map(shards, mesh=mesh, in_specs=placed, out_specs=P("prod"), check_vma=False)
```

```python
import functools

import jax
import jax.numpy as jnp
from jax import lax
from jax.experimental import pallas as pl
from jax.experimental.pallas import tpu as pltpu
from jax.sharding import PartitionSpec as P

CLU_OWN = 8
SLOTS = 32
Z_SLOTS = 176
NEAR_SLOTS = SLOTS // 2
FAR_SLOTS = 48
BLOCK = 128
LATE = 3
FEW = 64
LAST = 48
MANY = 2 * BLOCK
CAP = MANY + LATE * FEW
STARTS = (0, MANY, MANY + FEW, MANY + 2 * FEW)
NEW = (0, FEW, FEW, LAST)
SCORE_ROWS = (4 * BLOCK, 5 * FEW, 6 * FEW, 7 * LAST)
TOO_MANY = 4.0 * CLU_OWN
F32 = jnp.float32
BF16 = jnp.bfloat16
MESH = pl.DeviceIdType.MESH
NN = (((1,), (0,)), ((), ()))
NT = (((1,), (1,)), ((), ()))


def dot(a, b, dims=NN, precision=None):
    return lax.dot_general(a, b, dims, preferred_element_type=F32, precision=precision)


def iota(shape, dim):
    return lax.broadcasted_iota(jnp.int32, shape, dim)


def hot(cond):
    return jnp.where(cond, 1.0, 0.0).astype(BF16)


def nearest_first(n):
    order = [0]
    for d in range(1, n // 2 + 1):
        order += [d] if 2 * d == n else [d, n - d]
    return order


def highest(score, limit):
    return jnp.max(jnp.where(limit, score, -1.0), axis=0, keepdims=True)


def most(a):
    return jnp.max(jnp.max(a, axis=1, keepdims=True), axis=0, keepdims=True)


def kernel(
    planes,
    owners_in,
    ids_ref,
    x_ref,
    out_ref,
    flag_ref,
    x_rows,
    unit,
    index,
    packed,
    z_rows,
    lids_own,
    z_lids,
    lids_out,
    x_lids,
    staged,
    rows,
    far_rows,
    last_rows,
    sorted_rows,
    partial,
    relay,
    near,
    far,
    forward,
    values_out,
    x_back,
    values_home,
    z_back,
    load_sem,
    z_send,
    z_recv,
    zl_send,
    zl_recv,
    xl_send,
    xl_recv,
    x_send,
    x_recv,
    far_send,
    far_recv,
    y_send,
    y_recv,
    xb_send,
    xb_recv,
    zb_send,
    zb_recv,
):
    lanes = owners_in * SLOTS
    owners = planes * owners_in
    items = ids_ref.shape[1]
    blocks, _, width = x_rows.shape
    part = unit.shape[1]
    me = lax.axis_index("prod")
    tile = lax.axis_index("tile")
    my_plane = me // owners_in
    my_col = lax.rem(me, owners_in)
    at_plane = lambda d: lax.rem(my_plane + d, planes)
    at_col = lambda k: lax.rem(my_col + k, owners_in)
    at_tile = lambda k: lax.rem(tile + k, 4)
    to_plane = lambda d: {"prod": at_plane(d) * owners_in + my_col}
    to_col = lambda k: {"prod": my_plane * owners_in + at_col(k)}
    to_tile = lambda k: {"tile": at_tile(k)}
    to_far = lambda k: {"prod": at_plane(far_plane) * owners_in + at_col(k)}
    to_both = lambda k, j: {"prod": my_plane * owners_in + at_col(k), "tile": at_tile(j)}
    order = nearest_first(planes)
    far_plane = order[-1]
    first_late = planes - LATE + 1
    started = []

    def drain(ref, sem):
        pltpu.make_async_copy(ref, ref, sem).wait()

    def send(src, dst, send_sem, recv_sem, device, alone=False):
        copy = pltpu.make_async_remote_copy(
            src_ref=src,
            dst_ref=dst,
            send_sem=send_sem,
            recv_sem=recv_sem,
            device_id=device,
            device_id_type=MESH,
        )
        copy.start()
        if alone:
            started.append(copy)
        return copy

    barrier = pltpu.get_barrier_semaphore()
    for d in range(1, planes):
        pl.semaphore_signal(barrier, inc=1, device_id=to_plane(d), device_id_type=MESH)
    for k in range(1, owners_in):
        pl.semaphore_signal(barrier, inc=1, device_id=to_col(k), device_id_type=MESH)
    for k in range(1, 4):
        pl.semaphore_signal(barrier, inc=1, device_id=to_tile(k), device_id_type=MESH)

    loads = [
        pltpu.make_async_copy(
            x_ref.at[pl.ds(n * BLOCK, BLOCK)], x_rows.at[n], load_sem.at[n]
        )
        for n in range(blocks)
    ]
    for load in loads:
        load.start()

    for k in range(owners_in):
        blank = jnp.zeros((NEAR_SLOTS, part), BF16)
        rows[far_plane, k * SLOTS : k * SLOTS + NEAR_SLOTS, :] = blank
        last_rows[k * SLOTS + NEAR_SLOTS : (k + 1) * SLOTS, :] = blank

    ids = ids_ref[...]
    owner = ids // CLU_OWN
    plane = owner // owners_in
    lid = lax.rem(ids, CLU_OWN)
    owned = jnp.where(iota((owners, items), 0) == owner, 1.0, 0.0)
    before_block = hot(iota((BLOCK, BLOCK), 0) < iota((BLOCK, BLOCK), 1))
    count = jnp.zeros((owners, 1), F32)
    ahead = []
    for n in range(items // BLOCK):
        block = owned[:, n * BLOCK : (n + 1) * BLOCK]
        ahead.append(dot(block.astype(BF16), before_block) + count)
        count += jnp.sum(block, axis=1, keepdims=True)
    ahead = jnp.concatenate(ahead, axis=1)
    a, b = (iota((owners, owners), n) for n in (0, 1))
    lower = hot((a // owners_in == b // owners_in) & (b < a))
    offset = dot(lower, jnp.broadcast_to(count, (owners, BLOCK)).astype(BF16))[:, :1]
    slot = jnp.sum(owned * ahead, axis=0, keepdims=True).astype(jnp.int32)
    position = jnp.sum(owned * (ahead + offset), axis=0, keepdims=True).astype(jnp.int32)
    spill = jnp.broadcast_to(jnp.maximum(count - NEAR_SLOTS, 0.0), (owners, BLOCK)).astype(BF16)
    spill = jnp.sum(owned * dot(lower, spill)[:, :1], axis=0, keepdims=True).astype(jnp.int32)
    column = lax.rem(owner, owners_in)
    place = column * SLOTS + slot
    away = lax.rem(plane - my_plane + planes, planes)
    direct = jnp.where(slot < NEAR_SLOTS, column * NEAR_SLOTS + slot, -1)
    spilled = jnp.where(slot < NEAR_SLOTS, -1, spill + slot - NEAR_SLOTS)
    for n, line in enumerate((away, place, position, direct, spilled)):
        index[n : n + 1, :] = line
    room = (position < Z_SLOTS) & ((away != far_plane) | (spilled < FAR_SLOTS))
    crowded = jnp.max(jnp.where(room, 0.0, TOO_MANY), axis=1, keepdims=True)
    by_plane = jnp.where(iota((planes, items), 0) == plane, lid + 1, 0).astype(F32).astype(BF16)
    by_place = hot(iota((lanes, items), 0) == place)
    lids = dot(by_plane, by_place, NT)
    lids += crowded
    for z in range(planes):
        lids_own[z] = jnp.broadcast_to(lids[z : z + 1], lids_own.shape[1:])

    def unit_rows(n, carry):
        pltpu.make_async_copy(
            x_ref.at[pl.ds(pl.multiple_of(n * BLOCK, BLOCK), BLOCK)], x_rows.at[n], load_sem.at[n]
        ).wait()
        total = jnp.zeros((BLOCK, BLOCK), F32)
        for c in range(width // BLOCK):
            x = x_rows[n, :, c * BLOCK : (c + 1) * BLOCK].astype(F32)
            total += x * x
        scale = lax.rsqrt(jnp.sum(total, axis=1, keepdims=True) + 1e-06)
        mine = x_rows[n, :, pl.ds(pl.multiple_of(tile * part, part), part)].astype(F32)
        unit[pl.ds(pl.multiple_of(n * BLOCK, BLOCK), BLOCK), :] = (mine * scale).astype(BF16)
        return carry

    lax.fori_loop(0, blocks, unit_rows, 0)

    pl.semaphore_wait(barrier, planes - 1 + owners_in - 1 + 3)
    for d in order[1:]:
        send(lids_own.at[at_plane(d)], z_lids.at[d], zl_send, zl_recv, to_plane(d))
    row_copies = {}

    def chosen_rows(d, line, count):
        wanted = jnp.where(index[0:1, :] == d, index[line : line + 1, :], -1)
        return dot(hot(iota((count, items), 0) == wanted), unit[...]).astype(BF16)

    def pack_rows(d, line, count):
        packed[d, :count, :] = chosen_rows(d, line, count)

    def send_rows(d, count):
        at = pl.ds(0, count)
        row_copies[d] = send(
            packed.at[d, at], z_rows.at[d, at], z_send.at[d], z_recv.at[d], to_plane(d), True
        )

    held = order[-LATE:-1]
    for n, d in enumerate(order[1:-LATE]):
        pack_rows(d, 2, Z_SLOTS)
        send_rows(d, Z_SLOTS)
        if n == 1:
            z_rows[0] = chosen_rows(0, 2, Z_SLOTS)
    if planes < 8:
        z_rows[0] = chosen_rows(0, 2, Z_SLOTS)
    pack_rows(far_plane, 4, FAR_SLOTS)
    send_rows(far_plane, FAR_SLOTS)
    for d in held:
        pack_rows(d, 2, Z_SLOTS)
    far_rows[...] = chosen_rows(far_plane, 3, owners_in * NEAR_SLOTS)

    def send_held():
        for d in held:
            send_rows(d, Z_SLOTS)

    def send_last():
        for k in range(owners_in):
            start = pl.multiple_of(at_col(k) * NEAR_SLOTS, NEAR_SLOTS)
            send(
                far_rows.at[pl.ds(start, NEAR_SLOTS)],
                last_rows.at[pl.ds(k * SLOTS, NEAR_SLOTS)],
                far_send,
                far_recv,
                to_far(k),
            )

    drain(z_lids.at[pl.ds(1, planes - 1)], zl_recv)
    lids = jnp.concatenate(
        [lids_own[my_plane][0:1]] + [z_lids[d][0:1] for d in range(1, planes)], axis=0
    )
    lids_out[...] = pltpu.roll(lids, lax.rem(owners_in - my_col, owners_in) * SLOTS, 1)
    for k in range(1, owners_in):
        send(lids_out, x_lids.at[k], xl_send, xl_recv, to_col(k))
    before = hot(iota((lanes, lanes), 0) < iota((lanes, lanes), 1))
    near_slot = lax.rem(iota((planes, lanes), 1), SLOTS) < NEAR_SLOTS
    last = near_slot & (iota((planes, lanes), 0) == far_plane)
    taken = (lids > 0.0) & jnp.logical_not(last)
    source = jnp.where(taken, dot(hot(taken), before), -1.0)
    source = jnp.concatenate([source, jnp.zeros((BLOCK - planes, lanes), F32)], axis=0).T

    def others(d):
        return pl.ds(0, (owners_in - 1) * (NEAR_SLOTS if d == far_plane else SLOTS))

    def forward_rows(d):
        if d:
            row_copies[d].wait_recv()
        count, skip = (FAR_SLOTS, NEAR_SLOTS) if d == far_plane else (Z_SLOTS, 0)
        take = source[:, d : d + 1].astype(jnp.int32) == iota((lanes, count), 1)
        staged[d] = dot(hot(take), z_rows[d, :count, :]).astype(BF16)
        for k in range(owners_in):
            start = pl.multiple_of(at_col(k) * SLOTS + skip, NEAR_SLOTS)
            src = staged.at[d, pl.ds(start, SLOTS - skip)]
            dst = rows.at[d, pl.ds(k * SLOTS + skip, SLOTS - skip)]
            if k:
                send(src, dst, x_send.at[d], x_recv.at[d], to_col(k))
            else:
                rows[d, skip:SLOTS, :] = staged[d, pl.ds(start, SLOTS - skip), :]

    steps = order[:-LATE] + [far_plane] + order[-LATE:-1]
    forward_rows(steps[0])

    drain(x_lids.at[pl.ds(1, owners_in - 1)], xl_recv)
    got = jnp.zeros((planes, lanes), F32)
    marks = lids_out[...]
    group = iota((planes, lanes), 1) // SLOTS
    for k in range(owners_in):
        theirs = lids_out[...] if k == 0 else x_lids[k]
        got += jnp.where(group == k, theirs, 0.0)
        marks = jnp.maximum(marks, theirs)

    def set_of(d):
        which = jnp.zeros(d.shape, jnp.int32)
        for n in range(1, LATE):
            which = jnp.where(d == order[n - LATE - 1 + planes], n, which)
        return which

    other = jnp.where(last, 0.0, got)
    member = jnp.concatenate([hot(other == c + 1.0) for c in range(CLU_OWN)], axis=0)
    ending = jnp.where(near_slot, got, 0.0)[far_plane : far_plane + 1]
    ending = hot(ending == iota((CLU_OWN, lanes), 0).astype(F32) + 1.0)
    ending_rank = dot(ending, before)
    ending_size = dot(ending, jnp.ones((lanes, lanes), BF16))
    in_row = dot(member, before)
    in_rows = dot(member, jnp.ones((lanes, lanes), BF16)).astype(BF16)
    a, b = (iota((CLU_OWN * planes, CLU_OWN * planes), n) for n in (0, 1))
    same = (a // planes == b // planes) & (set_of(lax.rem(a, planes)) == set_of(lax.rem(b, planes)))
    rank_all = in_row + dot(hot(same & (b < a)), in_rows)
    a, b = (iota((CLU_OWN * LATE, CLU_OWN * planes), n) for n in (0, 1))
    same = (lax.rem(a, CLU_OWN) == b // planes) & (a // CLU_OWN == set_of(lax.rem(b, planes)))
    sizes = jnp.concatenate([dot(hot(same), in_rows), ending_size], axis=0)
    unfit = (
        (most(marks) >= TOO_MANY)
        | (most(sizes[:CLU_OWN]) > MANY)
        | (most(sizes[CLU_OWN:]) > FEW)
        | (most(sizes[CLU_OWN * LATE :]) > LAST)
    )
    ranked = jnp.zeros((planes, lanes), F32)
    for c in range(CLU_OWN):
        this = slice(c * planes, (c + 1) * planes)
        rank_here = jnp.where(last, ending_rank[c : c + 1], rank_all[this])
        ranked += jnp.where(got == c + 1.0, rank_here, 0.0)
    late = jnp.where(last, LATE, set_of(iota((planes, lanes), 0)))
    cluster = got.astype(jnp.int32) - 1
    ranked = ranked.astype(jnp.int32)
    target = jnp.where(cluster >= 0, cluster * jnp.where(late == 0, MANY, FEW) + ranked, -1)

    def place_few(n, goal, arrived):
        moved = dot(hot(iota((CLU_OWN * FEW, lanes), 0) == goal), arrived).astype(BF16)
        for c in range(CLU_OWN):
            sorted_rows[c, STARTS[n] : STARTS[n] + FEW, :] = moved[c * FEW : (c + 1) * FEW]

    def place_rows(n):
        d = steps[n]
        drain(rows.at[d, others(d)], x_recv.at[d])
        goal = jnp.where(last, -1, target)[d : d + 1]
        if n >= first_late:
            place_few(n - first_late + 1, goal, rows[d])
            return

        def body(c, carry):
            chosen = hot(iota((MANY, lanes), 0) + c * MANY == goal)
            moved = dot(chosen, rows[d]).astype(BF16)
            if n:
                sorted_rows[c, :MANY, :] = sorted_rows[c, :MANY, :] + moved
            else:
                sorted_rows[c, :MANY, :] = moved
            return carry

        lax.fori_loop(0, CLU_OWN, body, 0)

    r, c = (iota((BLOCK, BLOCK), n) for n in (0, 1))
    right, left, across = at_tile(1), at_tile(3), at_tile(2)
    spans = []
    for s, n in enumerate(SCORE_ROWS):
        spans.append((sum(SCORE_ROWS[:s]), n // 2))

    def scores(t, s):
        base = spans[s][0]
        if s == 0:
            for j in range(2):
                block = sorted_rows[2 * t + j, :MANY, :]
                all_pairs = dot(block, block, NT)
                at = base + 2 * j * BLOCK
                partial[t, at : at + BLOCK] = all_pairs[:BLOCK, BLOCK:]
                partial[t, at + BLOCK : at + 2 * BLOCK] = jnp.where(
                    c > r, all_pairs[:BLOCK, :BLOCK], all_pairs[BLOCK:, BLOCK:]
                )
            return
        start, stop, fresh = STARTS[s], STARTS[s] + FEW, NEW[s]
        full = stop // BLOCK
        ends = []
        for j in range(2):
            new = sorted_rows[2 * t + j, start : start + fresh, :]
            pairs = dot(new, sorted_rows[2 * t + j, : full * BLOCK, :], NT)
            for p in range(full):
                at = base + (2 * p + j) * fresh
                partial[t, at : at + fresh] = pairs[:, p * BLOCK : (p + 1) * BLOCK]
            if stop % BLOCK:
                ends.append(dot(new, sorted_rows[2 * t + j, start - FEW : stop, :], NT))
        if ends:
            at = base + 2 * full * fresh
            partial[t, at : at + fresh] = jnp.where(
                c[:fresh] < FEW, pltpu.roll(ends[0], FEW, 1), ends[1]
            )

    y_copies = {}

    def y_send_to(s, n, src, dst, step):
        y_copies[s, n] = send(src, dst, y_send, y_recv.at[s, n], to_tile(step))

    def begin_sum(s):
        base, half = spans[s]
        head, tail, at = pl.ds(base, half), pl.ds(base + half, half), pl.ds(base // 2, half)
        scores(across, s)
        y_send_to(s, 0, partial.at[across, head], relay.at[0, at], 1)
        y_send_to(s, 1, partial.at[across, tail], relay.at[1, at], 3)
        scores(right, s)
        y_send_to(s, 2, partial.at[right, tail], near.at[1, at], 1)
        scores(left, s)
        y_send_to(s, 3, partial.at[left, head], near.at[0, at], 3)
        scores(tile, s)

    def relay_sum(s):
        base, half = spans[s]
        at = pl.ds(base // 2, half)
        y_copies[s, 0].wait_recv()
        forward[0, at] = relay[0, at] + partial[right, pl.ds(base, half)]
        y_send_to(s, 4, forward.at[0, at], far.at[0, at], 1)
        y_copies[s, 1].wait_recv()
        forward[1, at] = relay[1, at] + partial[left, pl.ds(base + half, half)]
        y_send_to(s, 5, forward.at[1, at], far.at[1, at], 3)

    def end_sum(s):
        base, half = spans[s]
        at = pl.ds(base // 2, half)
        for n in range(2, 6):
            y_copies[s, n].wait_recv()
        return jnp.concatenate(
            [partial[tile, pl.ds(base + h * half, half)] + near[h, at] + far[h, at] for h in (0, 1)],
            axis=0,
        )

    size_row = iota((BLOCK, lanes), 0)[: CLU_OWN * (LATE + 1)]
    size = [
        [
            jnp.sum(
                jnp.where(size_row == s * CLU_OWN + 2 * tile + j, sizes, 0.0), axis=0, keepdims=True
            )[:, :BLOCK].astype(jnp.int32)
            for j in range(2)
        ]
        for s in range(LATE + 1)
    ]
    lane = iota((1, BLOCK), 1)
    size_both = [jnp.where(lane < FEW, a, b) for a, b in size]
    by_column = {}
    by_new = {}

    def raise_to(j, p, value):
        by_column[j, p] = jnp.maximum(by_column[j, p], value) if (j, p) in by_column else value

    def best_of(s):
        total = end_sum(s)
        if s == 0:
            above, below = c > r, c < r
            for j in range(2):
                cross = total[2 * j * BLOCK : (2 * j + 1) * BLOCK]
                fold = total[(2 * j + 1) * BLOCK : (2 * j + 2) * BLOCK]
                turned = fold.T
                low, high = r < size[0][j], r + BLOCK < size[0][j]
                raise_to(j, 0, highest(fold, low & above))
                raise_to(j, 0, highest(turned, low & below))
                raise_to(j, 0, highest(cross.T, high))
                raise_to(j, 1, highest(fold, high & below))
                raise_to(j, 1, highest(turned, high & above))
                raise_to(j, 1, highest(cross, low))
            return
        stop, fresh = STARTS[s] + FEW, NEW[s]
        full = stop // BLOCK
        row_few, col_few = r[:fresh], c[:fresh]
        news = []
        for p in range(full):
            halves = [total[(2 * p + j) * fresh : (2 * p + j + 1) * fresh] for j in range(2)]
            for j in range(2):
                limit = row_few < size[s][j]
                if (p + 1) * BLOCK == stop:
                    limit = limit & (col_few - FEW != row_few)
                raise_to(j, p, highest(halves[j], limit))
            if p < 2:
                earlier = r + p * BLOCK < size_both[0]
            else:
                earlier = (r < FEW) & (r < size_both[1])
                if s == 3:
                    earlier = earlier | ((r >= FEW) & (r - FEW < size_both[2]))
            if fresh < FEW:
                blank = jnp.zeros((FEW - fresh, BLOCK), F32)
                halves = [halves[0], blank, halves[1], blank]
            news.append(highest(jnp.concatenate(halves, axis=0).T, earlier))
        if stop % BLOCK:
            limit = (row_few < size_both[s]) & (row_few != lax.rem(col_few, FEW))
            news.append(highest(total[2 * full * fresh :], limit))
        by_new[s] = functools.reduce(jnp.maximum, news)

    for n in range(1, planes):
        if n == first_late:
            place_rows(n - 1)
            begin_sum(0)
        forward_rows(steps[n])
        if n == planes // 4:
            send_held()
        if n == planes - 2:
            send_last()
        if n == first_late:
            relay_sum(0)
        else:
            place_rows(n - 1)
        if n > first_late:
            begin_sum(n - first_late)
            if n > first_late + 1:
                relay_sum(n - first_late - 1)
    place_rows(planes - 1)
    begin_sum(LATE - 1)
    relay_sum(LATE - 2)
    best_of(0)
    drain(last_rows.at[pl.ds(0, owners_in * NEAR_SLOTS)], far_recv)
    place_few(LATE, jnp.where(last, target, -1)[far_plane : far_plane + 1], last_rows[...])
    begin_sum(LATE)
    relay_sum(LATE - 1)
    best_of(LATE - 2)
    relay_sum(LATE)
    best_of(LATE - 1)
    best_of(LATE)

    swap = lambda v: pltpu.roll(v, FEW, 1)
    low = lane < FEW
    raise_to(0, 2, jnp.where(low, by_new[1], swap(by_new[2])))
    raise_to(1, 2, jnp.where(low, swap(by_new[1]), by_new[2]))
    raise_to(0, 3, by_new[3])
    raise_to(1, 3, swap(by_new[3]))
    table = jnp.concatenate([by_column[j, p] for j in range(2) for p in range(4)], axis=0)
    table = jnp.concatenate([table, jnp.zeros((BLOCK - 8, BLOCK), F32)], axis=0).T

    where = ranked
    for s in range(1, LATE + 1):
        where = where + jnp.where(late == s, STARTS[s], 0)
    where_row = lax.rem(cluster + 2, 2) * 4 + where // BLOCK
    where_row = jnp.where((cluster >= 0) & (cluster // 2 == tile), where_row, -1)
    where_lane = lax.rem(where, BLOCK)
    picked = []
    for d in range(planes):
        values = jnp.zeros((BLOCK, lanes), F32)
        for n in range(8):
            values = jnp.where(where_row[d : d + 1] == n, table[:, n : n + 1], values)
        mask = iota((BLOCK, lanes), 0) == where_lane[d : d + 1]
        picked.append(jnp.sum(jnp.where(mask, values, 0.0), axis=0, keepdims=True))
    values = jnp.where(unfit, TOO_MANY, jnp.concatenate(picked, axis=0))

    def turn(v):
        shifted = [v] + [pltpu.roll(v, n * SLOTS, 1) for n in range(1, planes)]
        mine = iota(v.shape, 0) == group
        lines = []
        for b in range(planes):
            line = jnp.zeros(v.shape, F32)
            for a in range(planes):
                line = jnp.where(mine & (group == a), shifted[(a - b) % planes], line)
            lines.append(jnp.sum(line, axis=0, keepdims=True))
        return lines

    for k, line in enumerate(turn(values)):
        values_out[k] = line
    for k in reversed(nearest_first(owners_in)):
        for j in (2, 1, 3, 0):
            if k or j:
                dst = x_back.at[j * owners_in + k]
                send(values_out.at[k], dst, xb_send, xb_recv, to_both(owners_in - k, j))
    drain(x_back.at[pl.ds(1, 4 * owners_in - 1)], xb_recv)
    home = []
    for k in range(owners_in):
        parts = [x_back[j * owners_in + k] if k or j else values_out[0] for j in range(4)]
        home.append(functools.reduce(jnp.add, parts))
    home = jnp.concatenate(turn(jnp.concatenate(home, axis=0)), axis=0)
    home = pltpu.roll(home, my_col * SLOTS, 1)
    for d in range(planes):
        values_home[d] = home[d : d + 1]
    for d in reversed(order[1:]):
        send(values_home.at[d], z_back.at[d], zb_send, zb_recv, to_plane(planes - d))
    drain(z_back.at[pl.ds(1, planes - 1)], zb_recv)
    mine = jnp.concatenate([values_home[0]] + [z_back[d] for d in range(1, planes)], axis=0)
    flag_ref[0, 0] = jnp.max(mine)
    mine = jnp.concatenate([mine, jnp.zeros((BLOCK - planes, lanes), F32)], axis=0).T
    values = jnp.zeros((lanes, items), F32)
    for d in range(planes):
        values = jnp.where(index[0:1, :] == d, mine[:, d : d + 1], values)
    mask = iota((lanes, items), 0) == index[1:2, :]
    out_ref[...] = jnp.sum(jnp.where(mask, values, 0.0), axis=0, keepdims=True)

    for copy in started:
        copy.wait_send()
    for d in order:
        drain(staged.at[d, others(d)], x_send.at[d])
    drain(far_rows, far_send)
    drain(partial.at[pl.ds(0, 3)], y_send)
    drain(z_lids.at[pl.ds(1, planes - 1)], zl_send)
    drain(x_lids.at[pl.ds(1, owners_in - 1)], xl_send)
    drain(x_back.at[pl.ds(1, 4 * owners_in - 1)], xb_send)
    drain(z_back.at[pl.ds(1, planes - 1)], zb_send)


def fast(planes, owners_in, embeddings, cluster_ids, part):
    items, width = embeddings.shape
    lanes = owners_in * SLOTS
    total = sum(SCORE_ROWS)
    vmem = pl.BlockSpec(memory_space=pltpu.VMEM)
    one = pltpu.SemaphoreType.DMA
    dma = lambda *shape: one(shape)
    buffer = pltpu.VMEM
    return pl.pallas_call(
        functools.partial(kernel, planes, owners_in),
        out_shape=(jax.ShapeDtypeStruct((1, items), F32), jax.ShapeDtypeStruct((1, 1), F32)),
        in_specs=[vmem, pl.BlockSpec(memory_space=pl.ANY)],
        out_specs=(vmem, pl.BlockSpec(memory_space=pltpu.SMEM)),
        scratch_shapes=[
            buffer((items // BLOCK, BLOCK, width), BF16),
            buffer((items, part), BF16),
            buffer((8, items), jnp.int32),
            buffer((planes, Z_SLOTS, part), BF16),
            buffer((planes, Z_SLOTS, part), BF16),
            buffer((planes, 8, lanes), F32),
            buffer((planes, 8, lanes), F32),
            buffer((planes, lanes), F32),
            buffer((owners_in, planes, lanes), F32),
            buffer((planes, lanes, part), BF16),
            buffer((planes, lanes, part), BF16),
            buffer((owners_in * NEAR_SLOTS, part), BF16),
            buffer((lanes, part), BF16),
            buffer((CLU_OWN, CAP, part), BF16),
            buffer((4, total, BLOCK), F32),
            buffer((2, total // 2, BLOCK), F32),
            buffer((2, total // 2, BLOCK), F32),
            buffer((2, total // 2, BLOCK), F32),
            buffer((2, total // 2, BLOCK), F32),
            buffer((owners_in, 1, lanes), F32),
            buffer((4 * owners_in, 1, lanes), F32),
            buffer((planes, 1, lanes), F32),
            buffer((planes, 1, lanes), F32),
            dma(items // BLOCK),
            dma(planes),
            dma(planes),
            one,
            one,
            one,
            one,
            dma(planes),
            dma(planes),
            one,
            one,
            one,
            dma(LATE + 1, 6),
            one,
            one,
            one,
            one,
        ],
        compiler_params=pltpu.CompilerParams(
            collective_id=0, has_side_effects=True, vmem_limit_bytes=60 * 1024 * 1024
        ),
    )(cluster_ids.reshape(1, items), embeddings)


def pair_best(row_block, row_labels, columns, column_labels, column_start):
    scores = lax.dot_general(
        row_block, columns, (((1,), (1,)), ((), ())), preferred_element_type=jnp.float32
    )
    row_ident = jnp.arange(row_block.shape[0], dtype=jnp.int32)
    column_ident = column_start + jnp.arange(columns.shape[0], dtype=jnp.int32)
    in_cluster = (
        (row_labels[:, None] == column_labels[None, :])
        & (row_labels[:, None] >= 0)
        & (row_ident[:, None] != column_ident[None, :])
    )
    return jnp.max(jnp.where(in_cluster, scores, -1.0), axis=1)


def any_layout(embeddings, cluster_ids):
    prod_count = lax.axis_size("prod")
    tile_count = lax.axis_size("tile")
    item_dev = embeddings.shape[0]
    width = embeddings.shape[1]
    group_rows = prod_count * SLOTS
    widened = embeddings.astype(jnp.float32)
    normed = (
        widened * lax.rsqrt(jnp.sum(widened * widened, axis=1, keepdims=True) + 1e-06)
    ).astype(jnp.bfloat16)
    owners = cluster_ids // CLU_OWN
    owner_hot = (owners[:, None] == jnp.arange(prod_count, dtype=jnp.int32)[None, :]).astype(
        jnp.int32
    )
    running = jnp.cumsum(owner_hot, axis=0)
    slot_index = jnp.sum(running * owner_hot, axis=1) - 1
    position = owners * SLOTS + slot_index
    inverse = (
        jnp.full((group_rows,), item_dev, jnp.int32)
        .at[position]
        .set(jnp.arange(item_dev, dtype=jnp.int32))
    )
    padded = jnp.concatenate([normed, jnp.zeros((1, width), jnp.bfloat16)], axis=0)
    labels = jnp.concatenate([cluster_ids, jnp.full((1,), -1, jnp.int32)], axis=0)
    outgoing = padded[inverse].reshape(prod_count, SLOTS, width)
    out_labels = labels[inverse].reshape(prod_count, SLOTS)
    tile_pos = lax.axis_index("tile")
    row_block, row_labels = (
        lax.all_to_all(outgoing, "prod", split_axis=0, concat_axis=0, tiled=True),
        lax.all_to_all(out_labels, "prod", split_axis=0, concat_axis=0, tiled=True),
    )
    row_block = row_block.reshape(group_rows, width)
    row_labels = row_labels.reshape(group_rows)
    piece_rows = group_rows // tile_count
    row_start = tile_pos * piece_rows
    columns = lax.dynamic_slice_in_dim(row_block, row_start, piece_rows, 0)
    column_labels = lax.dynamic_slice_in_dim(row_labels, row_start, piece_rows, 0)
    partial_best = pair_best(row_block, row_labels, columns, column_labels, row_start)
    maxima = lax.pmax(partial_best, "tile")
    returned = lax.all_to_all(
        maxima.reshape(prod_count, -1), "prod", split_axis=0, concat_axis=0, tiled=True
    )
    return returned.reshape(group_rows)[position]


def shards(embeddings, cluster_ids):
    prod_count = lax.axis_size("prod")
    owners_in = 8 if prod_count >= 64 else 4
    planes = prod_count // owners_in
    part = embeddings.shape[1] // lax.axis_size("tile")
    best, mark = fast(planes, owners_in, embeddings, cluster_ids, part)
    fits = mark[0, 0] < TOO_MANY
    return lax.cond(
        fits,
        lambda e, i, b: b,
        lambda e, i, b: any_layout(e, i),
        embeddings,
        cluster_ids,
        best.reshape(-1),
    )


def solution(mesh):
    placed = (P("prod", None), P("prod"))
    return jax.shard_map(shards, mesh=mesh, in_specs=placed, out_specs=P("prod"), check_vma=False)
```
